256 devices in a mesh: rows: 32 (over z, y), snode: 8 (over x, core).
Axes of the slice: x: 4, y: 4, z: 8, core: 2. Of those that a mesh axis runs over, the one named last changes fastest.
Arguments:
- a_tiles: bfloat16 [6144, 256, 256], P(('rows', 'snode')), may hold values from -0.21875 to 0.21875
- tile_row: int32 [6144], P(('rows', 'snode')), may hold values from 0 to 7
- tile_col: int32 [6144], P(('rows', 'snode')), may hold values from 0 to 127, as said below
- right_side: float32 [2048, 32, 256], P(('rows', 'snode')), may hold values from -6 to 6
- estimate: float32 [4, 32, 32, 256], P(None, 'snode'), may hold values from -6 to 6
- diag_inverse: bfloat16 [4, 32, 256, 256], P(None, 'snode'), may hold values from -1.5 to 3
- coupling: bfloat16 [3, 32, 3, 256, 256], P(None, 'snode'), may hold values from -0.15625 to 0.15625
- coupling_source: int32 [3, 32, 3], P(None, 'snode'), may hold values from 0 to 95, as said below
Outputs:
- new_estimate: float32 [4, 32, 32, 256], P(None, 'snode')
- residual: float32 [2048, 32, 256], P(('rows', 'snode'))
The draws below stay inside these ranges and needn't reach their ends.
Inputs may be any that keep to these rules, and one draw needn't show every extreme that they name: `tile_col`: on each device (each aligned block of 24 entries), at most 6 entries name column tiles c with (c % 32) // 4 equal to one value, and on every device some value is named exactly 6 times. `coupling_source`: at level index m, entry 0 of the 32 supernodes is a permutation of the supernodes of level m (indices m * 32 to (m + 1) * 32 - 1); the other entries are below (m + 1) * 32.
All inputs are finite; a program needn't handle non-finite values.
Results may differ from the reference program's by a relative error of at most 0.012.
Values may be sent and summed in bfloat16 or wider, within the bound.
No kernel may reach another device: no remote copies, remote signals or barrier semaphores. Data moves between devices by JAX's collectives and lax.ppermute only.
A program may use at most 64 MiB of HBM per device.

```python
import jax
import jax.numpy as jnp
from jax import lax

T_SIZE = 256
K = 32
TILES_DEV = 24
RT_DEV = 8
SN_DEV = 4
LEV = 4
NCH = 3
SL = 32
NSN = 128
NTILES = 6144
ROWTILES = 2048
CAP = 6
N_ROWS = 32
N_SNODE = 8


def draw_tile_col(key, part):
    key = jax.random.fold_in(key, 11)
    subkeys = jax.random.split(key, 5)
    device_total = N_ROWS * N_SNODE
    slot_total = N_SNODE * CAP
    full_owner = jax.random.randint(subkeys[0], (device_total, 1), 0, N_SNODE)
    slot_ids = jnp.arange(slot_total, dtype=jnp.int32)[None, :]
    scores = jax.random.randint(subkeys[1], (device_total, slot_total), 0, 1 << 16) * slot_total + slot_ids
    scores = jnp.where(slot_ids // CAP == full_owner, slot_ids - slot_total, scores)
    chosen = jnp.argsort(scores, axis=1)[:, :TILES_DEV]
    mixing = jax.random.randint(subkeys[2], (device_total, TILES_DEV), 0, 1 << 16) * TILES_DEV + jnp.arange(TILES_DEV, dtype=jnp.int32)[None, :]
    order_perm = jnp.argsort(mixing, axis=1)
    chosen = jnp.take_along_axis(chosen, order_perm, axis=1)
    owner_pick = chosen // CAP
    level_pick = jax.random.randint(subkeys[3], (device_total, TILES_DEV), 0, LEV)
    inner_pick = jax.random.randint(subkeys[4], (device_total, TILES_DEV), 0, SN_DEV)
    return (level_pick * SL + owner_pick * SN_DEV + inner_pick).reshape(NTILES).astype(jnp.int32)


def draw_coupling_source(key, part):
    key = jax.random.fold_in(key, 23)
    first_key, second_key = jax.random.split(key, 2)
    perm_keys = jax.random.split(first_key, LEV - 1)
    firsts = jax.vmap(lambda subkey: jax.random.permutation(subkey, SL))(perm_keys).astype(jnp.int32)
    level_base = (jnp.arange(LEV - 1, dtype=jnp.int32) * SL)[:, None]
    firsts = (firsts + level_base)[:, :, None]
    upper_bound = ((jnp.arange(LEV - 1, dtype=jnp.int32) + 1) * SL)[:, None, None]
    others = jax.random.randint(second_key, (LEV - 1, SL, NCH - 1), 0, upper_bound)
    return jnp.concatenate([firsts, others.astype(jnp.int32)], axis=2).astype(jnp.int32)


def draw_diag_inverse(key, part):
    key = jax.random.fold_in(key, 37)
    first_key, second_key = jax.random.split(key, 2)
    full_shape = (LEV, SL, T_SIZE, T_SIZE)
    identity = jnp.eye(T_SIZE, dtype=jnp.float32)
    spread = jnp.clip(jax.random.normal(first_key, full_shape, jnp.float32), -4.0, 4.0) * (0.6 / T_SIZE ** 0.5)
    row_scale = jnp.exp(jax.random.uniform(second_key, (LEV, SL, T_SIZE, 1), jnp.float32, -0.35, 0.35))
    return ((spread + identity) * row_scale).astype(jnp.bfloat16)


def place_ends(values, rng, low, high):
    longest = values.shape.index(max(values.shape))
    spots = []
    for shift in (0, 1):
        where = [jax.random.randint(jax.random.fold_in(rng, axis), (), 0, length) for axis, length in enumerate(values.shape)]
        where[longest] = (where[longest] + shift) % values.shape[longest]
        spots.append(tuple(where))
    return values.at[spots[0]].set(low).at[spots[1]].set(high)


def steps_of(key, dims, cuts, least, high):
    gain = 1.0
    for dim, blocks in cuts:
        draws = jax.random.uniform(jax.random.fold_in(jax.random.fold_in(key, 6), dim), (blocks,), jnp.float32, least / len(cuts), high / len(cuts))
        gain = gain * jnp.repeat(jnp.exp(draws), dims[dim] // blocks).reshape((-1,) + (1,) * (len(dims) - 1 - dim))
    return gain


def gaussian(own_key, shape, deviation, most, cuts=(), kind=jnp.bfloat16):
    drawn = jax.random.normal(own_key, shape, jnp.float32) * deviation
    if len(cuts) > 0:
        drawn = steps_of(own_key, shape, cuts, -0.22, 0.18) * drawn
    return jnp.clip(drawn, min=-most, max=most).astype(kind)


def setup_inputs(seed: int = 0) -> dict:
    arg_keys = jax.random.split(jax.random.key(seed), 9)
    return {
        "a_tiles": gaussian(arg_keys[0], (NTILES, T_SIZE, T_SIZE), (T_SIZE * max(1, TILES_DEV // RT_DEV)) ** -0.5, 0.21875, ((0, 256),)),
        "tile_row": place_ends(jax.random.randint(arg_keys[1], (NTILES,), 0, RT_DEV), jax.random.fold_in(arg_keys[1], 1), 0, RT_DEV - 1).astype(jnp.int32),
        "tile_col": draw_tile_col(jax.random.fold_in(arg_keys[8], 71), 0),
        "right_side": gaussian(arg_keys[3], (ROWTILES, K, T_SIZE), 1.0, 6.0, ((0, 256),), jnp.float32),
        "estimate": gaussian(arg_keys[4], (LEV, SL, K, T_SIZE), 1.0, 6.0, ((1, 8),), jnp.float32),
        "diag_inverse": draw_diag_inverse(jax.random.fold_in(arg_keys[8], 71), 0),
        "coupling": gaussian(arg_keys[6], (LEV - 1, SL, NCH, T_SIZE, T_SIZE), (2 * T_SIZE * NCH) ** -0.5, 0.15625, ((1, 8),)),
        "coupling_source": draw_coupling_source(jax.random.fold_in(arg_keys[8], 71), 0),
    }


def reference(a_tiles, tile_row, tile_col, right_side, estimate, diag_inverse, coupling, coupling_source):
    devices_all = N_ROWS * N_SNODE
    estimate_low = estimate.astype(jnp.bfloat16).reshape(NSN, K, T_SIZE)
    tile_blocks = a_tiles.reshape(devices_all, TILES_DEV, T_SIZE, T_SIZE)
    row_lists = tile_row.reshape(devices_all, TILES_DEV)
    col_lists = tile_col.reshape(devices_all, TILES_DEV)
    side_blocks = right_side.reshape(devices_all, RT_DEV, K, T_SIZE)

    def one_device(gradient, inputs):
        tile_block, rows_here, cols_here, side_block = inputs
        tile_wide = tile_block.astype(jnp.float32)
        product = jnp.einsum("nkc,nrc->nkr", estimate_low[cols_here].astype(jnp.float32), tile_wide, precision=lax.Precision.HIGHEST)
        applied = jnp.zeros((RT_DEV, K, T_SIZE), jnp.float32).at[rows_here].add(product)
        residual = side_block - applied
        residual_low = residual.astype(jnp.bfloat16)
        pushed = jnp.einsum("nkr,nrc->nkc", residual_low[rows_here].astype(jnp.float32), tile_wide, precision=lax.Precision.HIGHEST)
        return gradient.at[cols_here].add(pushed), residual

    gradient, residual = lax.scan(one_device, jnp.zeros((NSN, K, T_SIZE), jnp.float32), (tile_blocks, row_lists, col_lists, side_blocks))
    gradient = gradient.reshape(LEV, SL, K, T_SIZE)
    known_low = jnp.zeros((NSN, K, T_SIZE), jnp.bfloat16)
    solved = []
    for level in range(LEV):
        accumulated = gradient[level]
        if level > 0:
            sources = coupling_source[level - 1]
            accumulated = accumulated - jnp.einsum("snkc,sncj->skj", known_low[sources].astype(jnp.float32), coupling[level - 1].astype(jnp.float32), precision=lax.Precision.HIGHEST)
        rounded = lax.optimization_barrier(accumulated.astype(jnp.bfloat16)).astype(jnp.float32)
        value = jnp.einsum("skt,stj->skj", rounded, diag_inverse[level].astype(jnp.float32), precision=lax.Precision.HIGHEST)
        solved.append(value)
        known_low = known_low.at[level * SL:(level + 1) * SL].set(value.astype(jnp.bfloat16))
    pending = jnp.zeros((NSN, K, T_SIZE), jnp.float32)
    updates = [None] * LEV
    for level in reversed(range(LEV)):
        remaining = solved[level] - pending[level * SL:(level + 1) * SL]
        rounded = lax.optimization_barrier(remaining.astype(jnp.bfloat16)).astype(jnp.float32)
        change = jnp.einsum("skj,stj->skt", rounded, diag_inverse[level].astype(jnp.float32), precision=lax.Precision.HIGHEST)
        updates[level] = change
        if level > 0:
            change_low = lax.optimization_barrier(change.astype(jnp.bfloat16)).astype(jnp.float32)
            pushed = jnp.einsum("skj,sncj->snkc", change_low, coupling[level - 1].astype(jnp.float32), precision=lax.Precision.HIGHEST)
            pending = pending.at[coupling_source[level - 1].reshape(-1)].add(pushed.reshape(-1, K, T_SIZE))
    new_estimate = estimate + jnp.stack(updates)
    return new_estimate, residual.reshape(ROWTILES, K, T_SIZE)
```

```python
import functools

import jax
import jax.numpy as jnp
from jax import lax
from jax.experimental import pallas as pl
from jax.experimental.pallas import tpu as pltpu
from jax.sharding import PartitionSpec as P

CAP = 6
X, CORE, Y, Z = 4, 2, 4, 8
OWNERS = X * CORE
F32 = jnp.float32
BF16 = jnp.bfloat16
NT = (((1,), (1,)), ((), ()))
NN = (((1,), (0,)), ((), ()))
SMEM = pl.BlockSpec(memory_space=pltpu.SMEM)
VMEM = pl.BlockSpec(memory_space=pltpu.VMEM)
ANY = pl.BlockSpec(memory_space=pl.ANY)
PARAMS = pltpu.CompilerParams(vmem_limit_bytes=16 * 1024 * 1024)


def dot(x, y, dims):
    return lax.dot_general(x, y, dims, preferred_element_type=F32)


def ring_away(owner, here):
    step = (lax.shift_right_logical(owner, 1) + X - lax.shift_right_logical(here, 1)) & (X - 1)
    return step * CORE + ((owner ^ here) & 1)


def plan_kernel(sn, here_ref, col_ref, row_ref, plan_ref, note_ref, count_ref, note):
    note[...] = jnp.zeros_like(note)
    for o in range(OWNERS):
        count_ref[o] = 0
    for t in range(col_ref.shape[0]):
        c = col_ref[t]
        level, owner, inner = c // (sn * OWNERS), (c // sn) % OWNERS, c % sn
        rank = count_ref[owner]
        count_ref[owner] = rank + 1
        plan_ref[0, t] = ring_away(owner, here_ref[0])
        plan_ref[1, t] = level * sn + inner
        plan_ref[2, t] = row_ref[t]
        plan_ref[3, t] = owner
        plan_ref[4, t] = rank
        mark = (level * sn + inner + 1).astype(F32)
        note[owner, pl.ds(rank, 1), :] = jnp.full((1, note.shape[2]), mark, F32)
    note_ref[...] = note[...].astype(BF16)


def tile_kernel(n_blocks, plan_ref, note_ref, side_ref, a_ref, *refs):
    blocks = refs[:n_blocks]
    res_ref, send_ref, x_all, low_ref, sems = refs[n_blocks:]
    tiles = a_ref.shape[0]
    mine = x_all.shape[0] // OWNERS
    half = x_all.shape[1] // 2
    per = send_ref.shape[0] // OWNERS
    copies = []
    for i, block in enumerate(blocks):
        target = x_all.at[pl.ds(i * mine, mine)]
        copies.append(pltpu.make_async_copy(block, target, sems.at[i]))
    for copy in copies:
        copy.start()
    send_ref[...] = jnp.zeros_like(send_ref)
    for o in range(OWNERS):
        send_ref[o * per + per - 1] = note_ref[o]
    res_ref[...] = side_ref[...]
    for copy in copies:
        copy.wait()
    for t in range(tiles):
        q = plan_ref[2, t]
        res_ref[q] -= dot(x_all[plan_ref[0, t] * mine + plan_ref[1, t]], a_ref[t], NT)
    low_ref[...] = res_ref[...].astype(BF16)
    for t in range(tiles):
        spot = plan_ref[3, t] * per + 2 * plan_ref[4, t]
        term = dot(low_ref[plan_ref[2, t]], a_ref[t], NN).astype(BF16)
        send_ref[spot] = term[:half]
        send_ref[spot + 1] = term[half:]


def in_hbm(x):
    return pltpu.with_memory_space_constraint(x, pltpu.HBM)


def in_vmem(x):
    return pltpu.with_memory_space_constraint(x, pltpu.VMEM)


def near_kernel(n, parts, *refs):
    sems = refs[-1]
    outs = refs[-1 - n : -1]
    copies = []
    for i in range(n):
        size = refs[i].shape[0] // parts[i]
        for k in range(parts[i]):
            piece = pl.ds(k * size, size)
            copies.append(pltpu.make_async_copy(refs[i].at[piece], outs[i].at[piece], sems.at[len(copies)]))
    for copy in copies:
        copy.start()
    for copy in copies:
        copy.wait()


def bring_near(after, *operands):
    n = len(operands)
    parts = tuple(4 if x.shape[0] % 4 == 0 else x.shape[0] for x in operands)
    operands = [in_hbm(x) for x in operands]
    if after is not None:
        operands.append(in_hbm(after))
    out_shape = [pltpu.VMEM(x.shape, x.dtype) if after is not None else jax.ShapeDtypeStruct(x.shape, x.dtype) for x in operands]
    return pl.pallas_call(
        functools.partial(near_kernel, n, parts),
        out_shape=tuple(out_shape[:n]),
        in_specs=[ANY] * len(operands),
        out_specs=(VMEM,) * n,
        scratch_shapes=[pltpu.SemaphoreType.DMA((sum(parts),))],
        compiler_params=PARAMS,
        name="bring_near",
    )(*operands)


def forward_rows(level, sn, g, look_ref, known_refs, c_ref, d_ref):
    if level > 0:
        known = jnp.concatenate([ref[...].reshape(-1, ref.shape[2]) for ref in known_refs], axis=0).astype(BF16)
        found = dot(look_ref[...], known, NN)
    rows = []
    for j in range(sn):
        acc = g[level * sn + j : level * sn + j + 1, :]
        if level > 0:
            n = c_ref.shape[2]
            for i in range(n):
                row = found[j * n + i : j * n + i + 1, :].astype(BF16)
                acc = acc - dot(row, c_ref[0, j, i], NN)
        rows.append(dot(acc.astype(BF16), d_ref[0, j], NN))
    return rows


def backward_rows(level, sn, remaining, c_ref, d_ref, change_ref, stage):
    for j in range(sn):
        change = dot(remaining[j].astype(BF16), d_ref[0, j], NT)
        change_ref[j : j + 1, :] = change
        if level > 0:
            n = c_ref.shape[2]
            low = change.astype(BF16)
            for i in range(n):
                stage[j * n + i : j * n + i + 1, :] = dot(low, c_ref[0, j, i], NT)


def spread(scatter_ref, stage):
    terms = stage[...]
    high = terms.astype(BF16)
    low = (terms - high.astype(F32)).astype(BF16)
    return dot(scatter_ref[...], high, NN) + dot(scatter_ref[...], low, NN)


def store_pend(pend, out_ref, rest_refs):
    n, rows, width = out_ref.shape
    base = pend.shape[0] - n * rows
    out_ref[...] = pend[base:, :].reshape(n, rows, width)
    for ref in rest_refs:
        ref[...] = pend[:base, :]


def spread_rows(rows, own_ref, out_ref):
    out_ref[...] = jnp.zeros_like(out_ref)
    for j, row in enumerate(rows):
        own_ref[j : j + 1, :] = row
        for o in range(out_ref.shape[0]):
            out_ref[o, j : j + 1, :] = row


def first_kernel(sn, parts_ref, d_ref, g_ref, own_ref, out_ref):
    total = parts_ref[0].astype(F32)
    for i in range(1, parts_ref.shape[0]):
        total = total + parts_ref[i].astype(F32)
    g_ref[...] = total
    spread_rows(forward_rows(0, sn, total, None, [], None, d_ref), own_ref, out_ref)


def forward_kernel(level, sn, g_ref, look_ref, *refs):
    known_refs, (c_ref, d_ref, own_ref, out_ref) = refs[:level], refs[level:]
    rows = forward_rows(level, sn, g_ref[...], look_ref, known_refs, c_ref, d_ref)
    spread_rows(rows, own_ref, out_ref)


def turn_kernel(level, sn, g_ref, look_ref, scatter_ref, *refs):
    known_refs, refs = refs[:level], refs[level:]
    c_ref, d_ref, change_ref, out_ref, rest_ref, stage = refs
    rows = forward_rows(level, sn, g_ref[...], look_ref, known_refs, c_ref, d_ref)
    stage[...] = jnp.zeros_like(stage)
    backward_rows(level, sn, rows, c_ref, d_ref, change_ref, stage)
    store_pend(spread(scatter_ref, stage), out_ref, [rest_ref])


def remaining_rows(sn, solved_ref, recv_ref):
    got = recv_ref[0]
    for i in range(1, recv_ref.shape[0]):
        got = got + recv_ref[i]
    return [solved_ref[j : j + 1, :] - got[j : j + 1, :] for j in range(sn)]


def backward_kernel(level, sn, solved_ref, recv_ref, pend_ref, scatter_ref, c_ref, d_ref, *refs):
    change_ref, out_ref, rest_refs, stage = refs[0], refs[1], refs[2:-1], refs[-1]
    stage[...] = jnp.zeros_like(stage)
    backward_rows(level, sn, remaining_rows(sn, solved_ref, recv_ref), c_ref, d_ref, change_ref, stage)
    store_pend(pend_ref[...] + spread(scatter_ref, stage), out_ref, rest_refs)


def last_kernel(sn, solved_ref, recv_ref, c3_ref, c2_ref, c1_ref, d_ref, out_ref, change):
    backward_rows(0, sn, remaining_rows(sn, solved_ref, recv_ref), None, d_ref, change, None)
    mine = jnp.concatenate([change[...], c1_ref[...], c2_ref[...], c3_ref[...]], axis=0).astype(BF16)
    for i in range(out_ref.shape[0]):
        out_ref[i] = mine


def shift(size, step):
    return [(i, (i + step) % size) for i in range(size)]


def local(a_tiles, tile_row, tile_col, right_side, estimate, diag_inverse, coupling, coupling_source):
    tiles, T = a_tiles.shape[0], a_tiles.shape[1]
    row_tiles, K = right_side.shape[0], right_side.shape[1]
    levels, sn = estimate.shape[0], estimate.shape[1]
    snode = ("x", "core")
    width = sn * OWNERS
    mine = levels * sn
    me = lax.axis_index("x") * CORE + lax.axis_index("core")
    here = me.reshape(1)

    e = estimate.astype(BF16).reshape(mine, K, T)
    other = functools.partial(lax.ppermute, axis_name="core", perm=shift(CORE, 1))

    ahead = lax.ppermute(e, "x", shift(X, X - 1))
    behind = lax.ppermute(e, "x", shift(X, 1))
    swapped = other(e)
    plan, note = pl.pallas_call(
        functools.partial(plan_kernel, sn),
        out_shape=(
            jax.ShapeDtypeStruct((5, tiles), jnp.int32),
            jax.ShapeDtypeStruct((OWNERS, 16, T), BF16),
        ),
        in_specs=[SMEM, SMEM, SMEM],
        out_specs=(SMEM, VMEM),
        scratch_shapes=[pltpu.SMEM((OWNERS,), jnp.int32), pltpu.VMEM((OWNERS, 16, T), F32)],
        compiler_params=PARAMS,
        name="plan",
    )(here, in_hbm(tile_col), in_hbm(tile_row))
    a_near, side = bring_near(None, a_tiles, right_side)
    ahead, behind, note, a_near = lax.optimization_barrier((ahead, behind, note, a_near))
    core = lax.axis_index("core")
    onward = []
    for x in range(X):
        onward.append((x * CORE, (x + 1) % X * CORE))
        onward.append((x * CORE + 1, (x - 1) % X * CORE + 1))
    far = lax.ppermute(jnp.where(core == 0, behind, ahead), snode, onward)
    blocks = [e, swapped, ahead, other(ahead), far, other(far), behind, other(behind)]

    slot_rows = CAP * K + 16
    residual, send = pl.pallas_call(
        functools.partial(tile_kernel, len(blocks)),
        out_shape=(
            jax.ShapeDtypeStruct((row_tiles, K, T), F32),
            jax.ShapeDtypeStruct((OWNERS * slot_rows // 16, 16, T), BF16),
        ),
        in_specs=[SMEM, VMEM, VMEM, VMEM] + [ANY] * len(blocks),
        out_specs=(VMEM, VMEM),
        scratch_shapes=[
            pltpu.VMEM((OWNERS * mine, K, T), BF16),
            pltpu.VMEM((row_tiles, K, T), BF16),
            pltpu.SemaphoreType.DMA((len(blocks),)),
        ],
        compiler_params=PARAMS,
        name="tile_products",
    )(plan, note, side, a_near, *blocks)

    send, coupling_source = lax.optimization_barrier((send, coupling_source))
    source = coupling_source.reshape(levels - 1, -1)
    block_rows = 8
    spot_at = source // sn * block_rows + source % sn
    n_terms = source.shape[1]
    pad_terms = -n_terms % 16
    spot_at = jnp.pad(spot_at, ((0, 0), (0, pad_terms)), constant_values=-1)
    look, scatter = [], []
    for level in range(1, levels):
        spots = jnp.arange(level * OWNERS * block_rows)
        look.append((spot_at[level - 1][:, None] == spots[None, :]).astype(BF16))
        scatter.append((spots[:, None] == spot_at[level - 1][None, :]).astype(BF16))
    stage = pltpu.VMEM((n_terms + pad_terms, T), F32)

    recv = lax.all_to_all(send, snode, 0, 0, tiled=True)
    (c_near,) = bring_near(residual, coupling)
    recv, c_near, look, scatter = lax.optimization_barrier((recv, c_near, look, scatter))
    recv = recv.reshape(OWNERS, slot_rows, T)

    spot = recv[:, CAP * K : CAP * K + CAP, 0].astype(jnp.int32) - 1
    spot = jnp.pad(jnp.repeat(spot, K, axis=1), ((0, 0), (0, 16)), constant_values=-1).reshape(-1)
    pick_row = jnp.arange(K * mine)
    pick_col = jnp.arange(OWNERS * slot_rows) % slot_rows
    y = lax.axis_index("y")
    row_k = (pick_row // mine) % Z * Y + (pick_row // (mine * Z) + y) % Y
    pick = (row_k[:, None] == pick_col[None, :] % K) & (pick_row[:, None] % mine == spot[None, :])
    part = jnp.dot(pick.astype(BF16), recv.reshape(OWNERS * slot_rows, T), preferred_element_type=F32)
    part = part.astype(BF16).reshape(Y, Z * mine, T)
    total = part[0].astype(F32)
    for s in range(1, Y):
        total = total + lax.ppermute(part[s], "y", shift(Y, s)).astype(F32)
    parts = lax.all_to_all(total.astype(BF16).reshape(Z, mine, T), "z", 0, 0, tiled=True)

    def d_spec(level):
        return pl.BlockSpec((1, sn, T, T), lambda i: (level, 0, 0, 0))

    def c_spec(level):
        return pl.BlockSpec((1, sn, coupling.shape[2], T, T), lambda i: (level - 1, 0, 0, 0, 0))

    row4 = jax.ShapeDtypeStruct((sn, T), F32)
    by_owner = jax.ShapeDtypeStruct((OWNERS, block_rows, T), F32)

    def rest_of(level):
        return (jax.ShapeDtypeStruct(((level - 1) * OWNERS * block_rows, T), F32),) if level > 1 else ()

    g, value, out = pl.pallas_call(
        functools.partial(first_kernel, sn),
        grid=(1,),
        out_shape=(jax.ShapeDtypeStruct((mine, T), F32), row4, by_owner),
        in_specs=[VMEM, d_spec(0)],
        out_specs=(VMEM, VMEM, VMEM),
        compiler_params=PARAMS,
        name="forward_0",
    )(parts, diag_inverse)
    known, solved = [], [value]
    for level in range(1, levels):
        known.append(lax.all_to_all(out, snode, 0, 0, tiled=True))
        if level < levels - 1:
            value, out = pl.pallas_call(
                functools.partial(forward_kernel, level, sn),
                grid=(1,),
                out_shape=(row4, by_owner),
                in_specs=[VMEM] * (2 + level) + [c_spec(level), d_spec(level)],
                out_specs=(VMEM, VMEM),
                compiler_params=PARAMS,
                name=f"forward_{level}",
            )(g, look[level - 1], *known, in_vmem(c_near), diag_inverse)
            solved.append(value)
        else:
            out_shape = (row4, by_owner) + rest_of(level)
            change, out, *rest = pl.pallas_call(
                functools.partial(turn_kernel, level, sn),
                grid=(1,),
                out_shape=out_shape,
                in_specs=[VMEM] * (3 + level) + [c_spec(level), d_spec(level)],
                out_specs=(VMEM,) * len(out_shape),
                scratch_shapes=[stage],
                compiler_params=PARAMS,
                name="turn",
            )(g, look[level - 1], scatter[level - 1], *known, in_vmem(c_near), diag_inverse)
    changes = [change]
    for level in reversed(range(levels - 1)):
        arrived = lax.all_to_all(out, snode, 0, 0, tiled=True)
        if level > 0:
            out_shape = (row4, by_owner) + rest_of(level)
            change, out, *rest = pl.pallas_call(
                functools.partial(backward_kernel, level, sn),
                grid=(1,),
                out_shape=out_shape,
                in_specs=[VMEM] * 4 + [c_spec(level), d_spec(level)],
                out_specs=(VMEM,) * len(out_shape),
                scratch_shapes=[stage],
                compiler_params=PARAMS,
                name=f"backward_{level}",
            )(solved[level], arrived, rest[0], scatter[level - 1], in_vmem(c_near), diag_inverse)
            changes.append(change)
        else:
            change = pl.pallas_call(
                functools.partial(last_kernel, sn),
                grid=(1,),
                out_shape=jax.ShapeDtypeStruct((Z, mine, T), BF16),
                in_specs=[VMEM] * 5 + [d_spec(0)],
                out_specs=VMEM,
                scratch_shapes=[pltpu.VMEM((sn, T), F32)],
                compiler_params=PARAMS,
                name="backward_0",
            )(solved[0], arrived, *changes, diag_inverse)
    column = lax.all_to_all(change, "z", 0, 0, tiled=True)
    pieces = [column] + [lax.ppermute(column, "y", shift(Y, -s % Y)) for s in range(1, Y)]
    pieces = jnp.concatenate(pieces, axis=0).reshape(Y * Z * mine, T)
    to = jnp.arange(mine * K)
    source = jnp.arange(Y * Z * mine)
    column_k = (source // mine) % Z * Y + (source // (mine * Z) + y) % Y
    source = (source % mine) * K + column_k
    sort = (to[:, None] == source[None, :]).astype(BF16)
    change = jnp.dot(sort, pieces, preferred_element_type=F32)
    new_estimate = estimate + change.reshape(estimate.shape)
    return new_estimate, residual


def solution(mesh):
    grid = jax.sharding.Mesh(mesh.devices.reshape(Z, Y, X, CORE), ("z", "y", "x", "core"))
    every, snode = ("z", "y", "x", "core"), ("x", "core")
    in_specs = (
        P(every, None, None),
        P(every),
        P(every),
        P(every, None, None),
        P(None, snode, None, None),
        P(None, snode, None, None),
        P(None, snode, None, None, None),
        P(None, snode, None),
    )
    out_specs = (P(None, snode, None, None), P(every, None, None))
    return jax.shard_map(local, mesh=grid, in_specs=in_specs, out_specs=out_specs, check_vma=False)
```

```python
import functools

import jax
import jax.numpy as jnp
from jax import lax
from jax.experimental import pallas as pl
from jax.experimental.pallas import tpu as pltpu
from jax.sharding import PartitionSpec as P

CAP = 6
X, CORE, Y, Z = 4, 2, 4, 8
OWNERS = X * CORE
F32 = jnp.float32
BF16 = jnp.bfloat16
NT = (((1,), (1,)), ((), ()))
NN = (((1,), (0,)), ((), ()))
SMEM = pl.BlockSpec(memory_space=pltpu.SMEM)
VMEM = pl.BlockSpec(memory_space=pltpu.VMEM)
ANY = pl.BlockSpec(memory_space=pl.ANY)
PARAMS = pltpu.CompilerParams(vmem_limit_bytes=16 * 1024 * 1024)


def dot(x, y, dims):
    return lax.dot_general(x, y, dims, preferred_element_type=F32)


def ring_away(owner, here):
    step = (lax.shift_right_logical(owner, 1) + X - lax.shift_right_logical(here, 1)) & (X - 1)
    return step * CORE + ((owner ^ here) & 1)


def plan_kernel(sn, here_ref, col_ref, row_ref, plan_ref, note_ref, count_ref, note):
    note[...] = jnp.zeros_like(note)
    for o in range(OWNERS):
        count_ref[o] = 0
    for t in range(col_ref.shape[0]):
        c = col_ref[t]
        level, owner, inner = c // (sn * OWNERS), (c // sn) % OWNERS, c % sn
        rank = count_ref[owner]
        count_ref[owner] = rank + 1
        plan_ref[0, t] = ring_away(owner, here_ref[0])
        plan_ref[1, t] = level * sn + inner
        plan_ref[2, t] = row_ref[t]
        plan_ref[3, t] = owner
        plan_ref[4, t] = rank
        mark = (level * sn + inner + 1).astype(F32)
        note[owner, pl.ds(rank, 1), :] = jnp.full((1, note.shape[2]), mark, F32)
    note_ref[...] = note[...].astype(BF16)


def tile_kernel(n_blocks, core_ref, plan_ref, note_ref, side_ref, a_ref, *refs):
    blocks = refs[:n_blocks]
    core = core_ref[0]
    res_ref, send_ref, x_all, low_ref, sems, note_sems = refs[n_blocks:]
    tiles = a_ref.shape[0]
    mine = x_all.shape[0] // OWNERS
    half = x_all.shape[1] // 2
    per = send_ref.shape[0] // OWNERS
    copies = [pltpu.make_async_copy(side_ref, res_ref, sems.at[len(blocks)])]
    own, rest = (2 * X - 2 - 4 * core) * mine, (2 + 4 * core) * mine
    spots = [0, mine, 4 * mine, 9 * mine // 2, 5 * mine, 11 * mine // 2]
    spots += [own, own + mine // 2, own + mine, rest, rest + mine, rest + 3 * mine // 2]
    for i, block in enumerate(blocks):
        target = x_all.at[pl.ds(spots[i], block.shape[0])]
        copies.append(pltpu.make_async_copy(block, target, sems.at[i]))
    for copy in copies:
        copy.start()
    send_ref[...] = jnp.zeros_like(send_ref)
    for o in range(OWNERS):
        copies.append(pltpu.make_async_copy(note_ref.at[o], send_ref.at[(o + 1) * per - 1], note_sems.at[o]))
        copies[-1].start()
    for copy in copies:
        copy.wait()
    for t in range(tiles):
        q = plan_ref[2, t]
        res_ref[q] -= dot(x_all[plan_ref[0, t] * mine + plan_ref[1, t]], a_ref[t], NT)
    low_ref[...] = res_ref[...].astype(BF16)
    for t in range(tiles):
        spot = plan_ref[3, t] * per + 2 * plan_ref[4, t]
        term = dot(low_ref[plan_ref[2, t]], a_ref[t], NN).astype(BF16)
        send_ref[spot] = term[:half]
        send_ref[spot + 1] = term[half:]


def in_hbm(x):
    return pltpu.with_memory_space_constraint(x, pltpu.HBM)


def in_vmem(x):
    return pltpu.with_memory_space_constraint(x, pltpu.VMEM)


def near_kernel(n, parts, *refs):
    sems = refs[-1]
    outs = refs[-1 - n : -1]
    copies = []
    for i in range(n):
        size = refs[i].shape[0] // parts[i]
        for k in range(parts[i]):
            piece = pl.ds(k * size, size)
            copies.append(pltpu.make_async_copy(refs[i].at[piece], outs[i].at[piece], sems.at[len(copies)]))
    for copy in copies:
        copy.start()
    for copy in copies:
        copy.wait()


def bring_near(after, *operands):
    n = len(operands)
    parts = tuple(4 if x.shape[0] % 4 == 0 else x.shape[0] for x in operands)
    operands = [in_hbm(x) for x in operands]
    if after is not None:
        operands.append(in_hbm(after))
    out_shape = [jax.ShapeDtypeStruct(x.shape, x.dtype) for x in operands]
    return pl.pallas_call(
        functools.partial(near_kernel, n, parts),
        out_shape=tuple(out_shape[:n]),
        in_specs=[ANY] * len(operands),
        out_specs=(VMEM,) * n,
        scratch_shapes=[pltpu.SemaphoreType.DMA((sum(parts),))],
        compiler_params=PARAMS,
        name="bring_near",
    )(*operands)


def forward_rows(level, sn, g, look_ref, known_refs, c_ref, d_ref):
    if level > 0:
        known = jnp.concatenate([ref[...].reshape(-1, ref.shape[2]) for ref in known_refs], axis=0).astype(BF16)
        found = dot(look_ref[...], known, NN)
    rows = []
    for j in range(sn):
        acc = g[level * sn + j : level * sn + j + 1, :]
        if level > 0:
            n = c_ref.shape[2]
            for i in range(n):
                row = found[j * n + i : j * n + i + 1, :].astype(BF16)
                acc = acc - dot(row, c_ref[0, j, i], NN)
        rows.append(dot(acc.astype(BF16), d_ref[0, j], NN))
    return rows


def backward_rows(level, sn, remaining, c_ref, d_ref, change_ref, stage):
    for j in range(sn):
        change = dot(remaining[j].astype(BF16), d_ref[0, j], NT)
        change_ref[j : j + 1, :] = change
        if level > 0:
            n = c_ref.shape[2]
            low = change.astype(BF16)
            for i in range(n):
                stage[j * n + i : j * n + i + 1, :] = dot(low, c_ref[0, j, i], NT)


def spread(scatter_ref, stage):
    terms = stage[...]
    high = terms.astype(BF16)
    low = (terms - high.astype(F32)).astype(BF16)
    return dot(scatter_ref[...], high, NN) + dot(scatter_ref[...], low, NN)


def store_pend(pend, out_ref, rest_refs):
    n, rows, width = out_ref.shape
    base = pend.shape[0] - n * rows
    out_ref[...] = pend[base:, :].reshape(n, rows, width)
    for ref in rest_refs:
        ref[...] = pend[:base, :]


def spread_rows(rows, own_ref, out_ref):
    out_ref[...] = jnp.zeros_like(out_ref)
    for j, row in enumerate(rows):
        own_ref[j : j + 1, :] = row
        for o in range(out_ref.shape[0]):
            out_ref[o, j : j + 1, :] = row


def first_kernel(sn, parts_ref, d_ref, g_ref, own_ref, out_ref):
    total = parts_ref[0].astype(F32)
    for i in range(1, parts_ref.shape[0]):
        total = total + parts_ref[i].astype(F32)
    g_ref[...] = total
    spread_rows(forward_rows(0, sn, total, None, [], None, d_ref), own_ref, out_ref)


def forward_kernel(level, sn, g_ref, look_ref, *refs):
    known_refs, (c_ref, d_ref, own_ref, out_ref) = refs[:level], refs[level:]
    rows = forward_rows(level, sn, g_ref[...], look_ref, known_refs, c_ref, d_ref)
    spread_rows(rows, own_ref, out_ref)


def turn_kernel(level, sn, g_ref, look_ref, scatter_ref, *refs):
    known_refs, refs = refs[:level], refs[level:]
    c_ref, d_ref, change_ref, out_ref, rest_ref, stage = refs
    rows = forward_rows(level, sn, g_ref[...], look_ref, known_refs, c_ref, d_ref)
    stage[...] = jnp.zeros_like(stage)
    backward_rows(level, sn, rows, c_ref, d_ref, change_ref, stage)
    store_pend(spread(scatter_ref, stage), out_ref, [rest_ref])


def remaining_rows(sn, solved_ref, recv_ref):
    got = recv_ref[0]
    for i in range(1, recv_ref.shape[0]):
        got = got + recv_ref[i]
    return [solved_ref[j : j + 1, :] - got[j : j + 1, :] for j in range(sn)]


def backward_kernel(level, sn, solved_ref, recv_ref, pend_ref, scatter_ref, c_ref, d_ref, *refs):
    change_ref, out_ref, rest_refs, stage = refs[0], refs[1], refs[2:-1], refs[-1]
    stage[...] = jnp.zeros_like(stage)
    backward_rows(level, sn, remaining_rows(sn, solved_ref, recv_ref), c_ref, d_ref, change_ref, stage)
    store_pend(pend_ref[...] + spread(scatter_ref, stage), out_ref, rest_refs)


def last_kernel(sn, solved_ref, recv_ref, c3_ref, c2_ref, c1_ref, d_ref, out_ref, change):
    backward_rows(0, sn, remaining_rows(sn, solved_ref, recv_ref), None, d_ref, change, None)
    mine = jnp.concatenate([change[...], c1_ref[...], c2_ref[...], c3_ref[...]], axis=0).astype(BF16)
    for i in range(out_ref.shape[0]):
        out_ref[i] = mine


def shift(size, step):
    return [(i, (i + step) % size) for i in range(size)]


def local(a_tiles, tile_row, tile_col, right_side, estimate, diag_inverse, coupling, coupling_source):
    tiles, T = a_tiles.shape[0], a_tiles.shape[1]
    row_tiles, K = right_side.shape[0], right_side.shape[1]
    levels, sn = estimate.shape[0], estimate.shape[1]
    snode = ("x", "core")
    width = sn * OWNERS
    mine = levels * sn
    me = lax.axis_index("x") * CORE + lax.axis_index("core")
    here = me.reshape(1)

    e = estimate.astype(BF16).reshape(mine, K, T)
    other = functools.partial(lax.ppermute, axis_name="core", perm=shift(CORE, 1))

    def along(block, way=1):
        perm = []
        for x in range(X):
            perm.append((x * CORE, (x + way) % X * CORE))
            perm.append((x * CORE + 1, (x - way) % X * CORE + 1))
        return lax.ppermute(block, snode, perm)

    half = mine // 2
    first = [along(e[:half]), along(e[half:])]
    second = along(e, -1)
    swapped = other(e)
    plan, note = pl.pallas_call(
        functools.partial(plan_kernel, sn),
        out_shape=(
            jax.ShapeDtypeStruct((5, tiles), jnp.int32),
            pltpu.HBM((OWNERS, 16, T), BF16),
        ),
        in_specs=[SMEM, SMEM, SMEM],
        out_specs=(SMEM, VMEM),
        scratch_shapes=[pltpu.SMEM((OWNERS,), jnp.int32), pltpu.VMEM((OWNERS, 16, T), F32)],
        compiler_params=PARAMS,
        name="plan",
    )(here, in_hbm(tile_col), in_hbm(tile_row))
    first_lo, first_hi, note = lax.optimization_barrier((*first, note))
    first = [first_lo, first_hi]
    far = [along(x) for x in first]
    (a_near,) = bring_near(None, a_tiles)
    second, a_near = lax.optimization_barrier((second, a_near))
    side = in_hbm(right_side)
    blocks = [e, swapped] + far + [other(x) for x in far] + first + [other(second), second] + [other(x) for x in first]

    slot_rows = CAP * K + 16
    residual, send = pl.pallas_call(
        functools.partial(tile_kernel, len(blocks)),
        out_shape=(
            jax.ShapeDtypeStruct((row_tiles, K, T), F32),
            pltpu.HBM((OWNERS * slot_rows // 16, 16, T), BF16),
        ),
        in_specs=[SMEM, SMEM, ANY, ANY, VMEM] + [ANY] * len(blocks),
        out_specs=(VMEM, VMEM),
        scratch_shapes=[
            pltpu.VMEM((OWNERS * mine, K, T), BF16),
            pltpu.VMEM((row_tiles, K, T), BF16),
            pltpu.SemaphoreType.DMA((len(blocks) + 1,)),
            pltpu.SemaphoreType.DMA((OWNERS,)),
        ],
        compiler_params=PARAMS,
        name="tile_products",
    )(lax.axis_index("core").reshape(1), plan, in_hbm(note), side, a_near, *blocks)

    to = jnp.arange(mine * K)
    y = lax.axis_index("y")
    place = jnp.arange(Y * Z * mine)
    column_k = (place // mine) % Z * Y + (place // (mine * Z) + y) % Y
    place = (place % mine) * K + column_k
    send, coupling_source = lax.optimization_barrier((send, coupling_source))
    source = coupling_source.reshape(levels - 1, -1)
    block_rows = 8
    spot_at = source // sn * block_rows + source % sn
    n_terms = source.shape[1]
    pad_terms = -n_terms % 16
    spot_at = jnp.pad(spot_at, ((0, 0), (0, pad_terms)), constant_values=-1)
    look, scatter = [], []
    for level in range(1, levels):
        spots = jnp.arange(level * OWNERS * block_rows)
        look.append((spot_at[level - 1][:, None] == spots[None, :]).astype(BF16))
        scatter.append((spots[:, None] == spot_at[level - 1][None, :]).astype(BF16))
    stage = pltpu.VMEM((n_terms + pad_terms, T), F32)

    recv = lax.all_to_all(send, snode, 0, 0, tiled=True)
    (c_near,) = bring_near(residual, coupling)
    recv, c_near, look, scatter, to, place = lax.optimization_barrier((recv, c_near, look, scatter, to, place))
    recv = recv.reshape(OWNERS, slot_rows, T)

    spot = recv[:, CAP * K : CAP * K + CAP, 0].astype(jnp.int32) - 1
    spot = jnp.pad(jnp.repeat(spot, K, axis=1), ((0, 0), (0, 16)), constant_values=-1).reshape(-1)
    pick_row = jnp.arange(K * mine)
    pick_col = jnp.arange(OWNERS * slot_rows) % slot_rows
    y = lax.axis_index("y")
    row_k = (pick_row // mine) % Z * Y + (pick_row // (mine * Z) + y) % Y
    pick = (row_k[:, None] == pick_col[None, :] % K) & (pick_row[:, None] % mine == spot[None, :])
    part = jnp.dot(pick.astype(BF16), recv.reshape(OWNERS * slot_rows, T), preferred_element_type=F32)
    part = part.astype(BF16).reshape(Y, Z * mine, T)
    total = part[0].astype(F32)
    for s in range(1, Y):
        total = total + lax.ppermute(part[s], "y", shift(Y, s)).astype(F32)
    parts = lax.all_to_all(total.astype(BF16).reshape(Z, mine, T), "z", 0, 0, tiled=True)

    def d_spec(level):
        return pl.BlockSpec((1, sn, T, T), lambda i: (level, 0, 0, 0))

    def c_spec(level):
        return pl.BlockSpec((1, sn, coupling.shape[2], T, T), lambda i: (level - 1, 0, 0, 0, 0))

    row4 = jax.ShapeDtypeStruct((sn, T), F32)
    by_owner = jax.ShapeDtypeStruct((OWNERS, block_rows, T), F32)

    def rest_of(level):
        return (jax.ShapeDtypeStruct(((level - 1) * OWNERS * block_rows, T), F32),) if level > 1 else ()

    g, value, out = pl.pallas_call(
        functools.partial(first_kernel, sn),
        grid=(1,),
        out_shape=(jax.ShapeDtypeStruct((mine, T), F32), row4, by_owner),
        in_specs=[VMEM, d_spec(0)],
        out_specs=(VMEM, VMEM, VMEM),
        compiler_params=PARAMS,
        name="forward_0",
    )(parts, diag_inverse)
    known, solved = [], [value]
    for level in range(1, levels):
        known.append(lax.all_to_all(out, snode, 0, 0, tiled=True))
        if level < levels - 1:
            value, out = pl.pallas_call(
                functools.partial(forward_kernel, level, sn),
                grid=(1,),
                out_shape=(row4, by_owner),
                in_specs=[VMEM] * (2 + level) + [c_spec(level), d_spec(level)],
                out_specs=(VMEM, VMEM),
                compiler_params=PARAMS,
                name=f"forward_{level}",
            )(g, look[level - 1], *known, c_near, diag_inverse)
            solved.append(value)
        else:
            out_shape = (row4, by_owner) + rest_of(level)
            change, out, *rest = pl.pallas_call(
                functools.partial(turn_kernel, level, sn),
                grid=(1,),
                out_shape=out_shape,
                in_specs=[VMEM] * (3 + level) + [c_spec(level), d_spec(level)],
                out_specs=(VMEM,) * len(out_shape),
                scratch_shapes=[stage],
                compiler_params=PARAMS,
                name="turn",
            )(g, look[level - 1], scatter[level - 1], *known, c_near, diag_inverse)
    changes = [change]
    for level in reversed(range(levels - 1)):
        arrived = lax.all_to_all(out, snode, 0, 0, tiled=True)
        if level > 0:
            out_shape = (row4, by_owner) + rest_of(level)
            change, out, *rest = pl.pallas_call(
                functools.partial(backward_kernel, level, sn),
                grid=(1,),
                out_shape=out_shape,
                in_specs=[VMEM] * 4 + [c_spec(level), d_spec(level)],
                out_specs=(VMEM,) * len(out_shape),
                scratch_shapes=[stage],
                compiler_params=PARAMS,
                name=f"backward_{level}",
            )(solved[level], arrived, rest[0], scatter[level - 1], c_near, diag_inverse)
            changes.append(change)
        else:
            change = pl.pallas_call(
                functools.partial(last_kernel, sn),
                grid=(1,),
                out_shape=jax.ShapeDtypeStruct((Z, mine, T), BF16),
                in_specs=[VMEM] * 5 + [d_spec(0)],
                out_specs=VMEM,
                scratch_shapes=[pltpu.VMEM((sn, T), F32)],
                compiler_params=PARAMS,
                name="backward_0",
            )(solved[0], arrived, *changes, diag_inverse)
    column = lax.all_to_all(change, "z", 0, 0, tiled=True)
    pieces = [column] + [lax.ppermute(column, "y", shift(Y, -s % Y)) for s in range(1, Y)]
    pieces = jnp.concatenate(pieces, axis=0).reshape(Y * Z * mine, T)
    sort = (to[:, None] == place[None, :]).astype(BF16)
    change = jnp.dot(sort, pieces, preferred_element_type=F32)
    new_estimate = estimate + change.reshape(estimate.shape)
    return new_estimate, residual


def solution(mesh):
    grid = jax.sharding.Mesh(mesh.devices.reshape(Z, Y, X, CORE), ("z", "y", "x", "core"))
    every, snode = ("z", "y", "x", "core"), ("x", "core")
    in_specs = (
        P(every, None, None),
        P(every),
        P(every),
        P(every, None, None),
        P(None, snode, None, None),
        P(None, snode, None, None),
        P(None, snode, None, None, None),
        P(None, snode, None),
    )
    out_specs = (P(None, snode, None, None), P(every, None, None))
    return jax.shard_map(local, mesh=grid, in_specs=in_specs, out_specs=out_specs, check_vma=False)
```

```python
import functools

import jax
import jax.numpy as jnp
from jax import lax
from jax.experimental import pallas as pl
from jax.experimental.pallas import tpu as pltpu
from jax.sharding import PartitionSpec as P

CAP = 6
X, CORE, Y, Z = 4, 2, 4, 8
OWNERS = X * CORE
F32 = jnp.float32
BF16 = jnp.bfloat16
NT = (((1,), (1,)), ((), ()))
NN = (((1,), (0,)), ((), ()))
SMEM = pl.BlockSpec(memory_space=pltpu.SMEM)
VMEM = pl.BlockSpec(memory_space=pltpu.VMEM)
ANY = pl.BlockSpec(memory_space=pl.ANY)
PARAMS = pltpu.CompilerParams(vmem_limit_bytes=16 * 1024 * 1024)


def dot(x, y, dims):
    return lax.dot_general(x, y, dims, preferred_element_type=F32)


def ring_away(owner, here):
    step = (lax.shift_right_logical(owner, 1) + X - lax.shift_right_logical(here, 1)) & (X - 1)
    return step * CORE + ((owner ^ here) & 1)


def plan_kernel(sn, here_ref, col_ref, row_ref, plan_ref, note_ref, count_ref, note):
    note[...] = jnp.zeros_like(note)
    for o in range(OWNERS):
        count_ref[o] = 0
    for t in range(col_ref.shape[0]):
        c = col_ref[t]
        level, owner, inner = c // (sn * OWNERS), (c // sn) % OWNERS, c % sn
        rank = count_ref[owner]
        count_ref[owner] = rank + 1
        away = ring_away(owner, here_ref[0])
        plan_ref[0, t] = away
        plan_ref[1, t] = level * sn + inner
        plan_ref[2, t] = row_ref[t]
        plan_ref[3, t] = away
        plan_ref[4, t] = rank
        mark = (level * sn + inner + 1).astype(F32)
        note[away, pl.ds(rank, 1), :] = jnp.full((1, note.shape[2]), mark, F32)
    note_ref[...] = note[...].astype(BF16)


def tile_kernel(n_blocks, core_ref, plan_ref, note_ref, side_ref, a_ref, *refs):
    blocks = refs[:n_blocks]
    core = core_ref[0]
    res_ref, out_refs = refs[n_blocks], refs[n_blocks + 1 : n_blocks + 1 + OWNERS]
    send_ref, x_all, low_ref, sems, note_sems = refs[n_blocks + 1 + OWNERS :]
    tiles = a_ref.shape[0]
    mine = x_all.shape[0] // OWNERS
    half = x_all.shape[1] // 2
    per = send_ref.shape[0] // OWNERS
    copies = [pltpu.make_async_copy(side_ref, res_ref, sems.at[len(blocks)])]
    places = [0, 1, 4, 5] + [2 * X - 2 - 4 * core + i for i in range(2)] + [2 + 4 * core + i for i in range(2)]
    for i, block in enumerate(blocks):
        target = x_all.at[pl.ds(places[i] * mine, mine)]
        copies.append(pltpu.make_async_copy(block, target, sems.at[i]))
    for copy in copies:
        copy.start()
    send_ref[...] = jnp.zeros_like(send_ref)
    for o in range(OWNERS):
        copies.append(pltpu.make_async_copy(note_ref.at[o], send_ref.at[(o + 1) * per - 1], note_sems.at[o]))
        copies[-1].start()
    for copy in copies:
        copy.wait()
    for t in range(tiles):
        q = plan_ref[2, t]
        res_ref[q] -= dot(x_all[plan_ref[0, t] * mine + plan_ref[1, t]], a_ref[t], NT)
    low_ref[...] = res_ref[...].astype(BF16)
    for t in range(tiles):
        spot = plan_ref[3, t] * per + 2 * plan_ref[4, t]
        term = dot(low_ref[plan_ref[2, t]], a_ref[t], NN).astype(BF16)
        send_ref[spot] = term[:half]
        send_ref[spot + 1] = term[half:]
    for o, ref in enumerate(out_refs):
        ref[...] = send_ref[o * per : (o + 1) * per]


def in_hbm(x):
    return pltpu.with_memory_space_constraint(x, pltpu.HBM)


def in_vmem(x):
    return pltpu.with_memory_space_constraint(x, pltpu.VMEM)


def near_kernel(n, parts, *refs):
    sems = refs[-1]
    outs = refs[-1 - n : -1]
    copies = []
    for i in range(n):
        size = refs[i].shape[0] // parts[i]
        for k in range(parts[i]):
            piece = pl.ds(k * size, size)
            copies.append(pltpu.make_async_copy(refs[i].at[piece], outs[i].at[piece], sems.at[len(copies)]))
    for copy in copies:
        copy.start()
    for copy in copies:
        copy.wait()


def bring_near(after, *operands):
    n = len(operands)
    parts = tuple(4 if x.shape[0] % 4 == 0 else x.shape[0] for x in operands)
    operands = [in_hbm(x) for x in operands]
    if after is not None:
        operands.append(after)
    out_shape = [jax.ShapeDtypeStruct(x.shape, x.dtype) for x in operands]
    return pl.pallas_call(
        functools.partial(near_kernel, n, parts),
        out_shape=tuple(out_shape[:n]),
        in_specs=[ANY] * len(operands),
        out_specs=(VMEM,) * n,
        scratch_shapes=[pltpu.SemaphoreType.DMA((sum(parts),))],
        compiler_params=PARAMS,
        name="bring_near",
    )(*operands)


def pick_kernel(mine, y_ref, *refs):
    own_hbm, recvs, outs, (own, data, pick, sem) = refs[0], refs[1:OWNERS], refs[OWNERS:-4], refs[-4:]
    copy = pltpu.make_async_copy(own_hbm, own, sem)
    copy.start()
    blocks, size, T = own.shape
    rows = (blocks - 1) * size
    K = rows // CAP
    lane = lax.broadcasted_iota(jnp.int32, (1, 128), 1)
    marks, codes = [], []
    for i, ref in enumerate((*recvs, own)):
        if i == len(recvs):
            copy.wait()
        data[i * rows : (i + 1) * rows, :] = ref[: blocks - 1].reshape(rows, T)
        note = ref[blocks - 1].astype(F32)
        marks += [note[j : j + 1, :128] for j in range(CAP)]
    per = 128 // K
    column = (lane % K).astype(F32)
    for i in range(0, len(marks), per):
        mark = marks[i]
        for j in range(1, per):
            mark = jnp.where(lane // K == j, marks[i + j], mark)
        codes.append((mark - 1.0) * K + column)
    code = jnp.concatenate(codes, axis=1)
    for step, out in enumerate(outs):
        at = lax.broadcasted_iota(jnp.int32, (Z * mine, 1), 0)
        k = at // mine * Y + (y_ref[0] + step) % Y
        wanted = ((at % mine) * K + k).astype(F32)
        pick[...] = jnp.where(wanted == code, 1.0, 0.0).astype(BF16)
        out[...] = dot(pick[...], data[...], NN).astype(BF16)


def forward_rows(level, sn, g, look_ref, known_refs, c_ref, d_ref):
    if level > 0:
        known = jnp.concatenate([ref[...].astype(F32).reshape(-1, ref.shape[2]) for ref in known_refs], axis=0).astype(BF16)
        found = dot(look_ref[...], known, NN)
    rows = []
    for j in range(sn):
        acc = g[level * sn + j : level * sn + j + 1, :]
        if level > 0:
            n = c_ref.shape[2]
            for i in range(n):
                row = found[j * n + i : j * n + i + 1, :].astype(BF16)
                acc = acc - dot(row, c_ref[0, j, i], NN)
        rows.append(dot(acc.astype(BF16), d_ref[0, j], NN))
    return rows


def backward_rows(level, sn, remaining, c_ref, d_ref, change_ref, stage):
    for j in range(sn):
        change = dot(remaining[j].astype(BF16), d_ref[0, j], NT)
        change_ref[j : j + 1, :] = change
        if level > 0:
            n = c_ref.shape[2]
            low = change.astype(BF16)
            for i in range(n):
                stage[j * n + i : j * n + i + 1, :] = dot(low, c_ref[0, j, i], NT)


def spread(scatter_ref, stage):
    terms = stage[...]
    high = terms.astype(BF16)
    low = (terms - high.astype(F32)).astype(BF16)
    return dot(scatter_ref[...], high, NN) + dot(scatter_ref[...], low, NN)


def store_pend(pend, out_ref, rest_refs):
    n, rows, width = out_ref.shape
    base = pend.shape[0] - n * rows
    out_ref[...] = pend[base:, :].reshape(n, rows, width).astype(out_ref.dtype)
    for ref in rest_refs:
        ref[...] = pend[:base, :]


def spread_rows(rows, own_ref, out_ref):
    for j, row in enumerate(rows):
        own_ref[j : j + 1, :] = row
    filler = jnp.zeros((out_ref.shape[1] - len(rows), out_ref.shape[2]), F32)
    block = jnp.concatenate(rows + [filler], axis=0).astype(out_ref.dtype)
    for o in range(out_ref.shape[0]):
        out_ref[o] = block


def first_kernel(sn, parts_ref, d_ref, g_ref, own_ref, out_ref):
    total = parts_ref[0].astype(F32)
    for i in range(1, parts_ref.shape[0]):
        total = total + parts_ref[i].astype(F32)
    g_ref[...] = total
    spread_rows(forward_rows(0, sn, total, None, [], None, d_ref), own_ref, out_ref)


def forward_kernel(level, sn, g_ref, look_ref, *refs):
    known_refs, (c_ref, d_ref, own_ref, out_ref) = refs[:level], refs[level:]
    rows = forward_rows(level, sn, g_ref[...], look_ref, known_refs, c_ref, d_ref)
    spread_rows(rows, own_ref, out_ref)


def turn_kernel(level, sn, g_ref, look_ref, scatter_ref, *refs):
    known_refs, refs = refs[:level], refs[level:]
    c_ref, d_ref, change_ref, out_ref, rest_ref, stage = refs
    rows = forward_rows(level, sn, g_ref[...], look_ref, known_refs, c_ref, d_ref)
    stage[...] = jnp.zeros_like(stage)
    backward_rows(level, sn, rows, c_ref, d_ref, change_ref, stage)
    store_pend(spread(scatter_ref, stage), out_ref, [rest_ref])


def remaining_rows(sn, solved_ref, recv_ref):
    got = recv_ref[0].astype(F32)
    for i in range(1, recv_ref.shape[0]):
        got = got + recv_ref[i].astype(F32)
    return [solved_ref[j : j + 1, :] - got[j : j + 1, :] for j in range(sn)]


def backward_kernel(level, sn, solved_ref, recv_ref, pend_ref, scatter_ref, c_ref, d_ref, *refs):
    change_ref, out_ref, rest_refs, stage = refs[0], refs[1], refs[2:-1], refs[-1]
    stage[...] = jnp.zeros_like(stage)
    backward_rows(level, sn, remaining_rows(sn, solved_ref, recv_ref), c_ref, d_ref, change_ref, stage)
    store_pend(pend_ref[...] + spread(scatter_ref, stage), out_ref, rest_refs)


def last_kernel(sn, solved_ref, recv_ref, c3_ref, c2_ref, c1_ref, d_ref, out_ref, change):
    backward_rows(0, sn, remaining_rows(sn, solved_ref, recv_ref), None, d_ref, change, None)
    mine = jnp.concatenate([change[...], c1_ref[...], c2_ref[...], c3_ref[...]], axis=0).astype(BF16)
    for i in range(out_ref.shape[0]):
        out_ref[i] = mine


def shift(size, step):
    return [(i, (i + step) % size) for i in range(size)]


def local(a_tiles, tile_row, tile_col, right_side, estimate, diag_inverse, coupling, coupling_source):
    tiles, T = a_tiles.shape[0], a_tiles.shape[1]
    row_tiles, K = right_side.shape[0], right_side.shape[1]
    levels, sn = estimate.shape[0], estimate.shape[1]
    snode = ("x", "core")
    width = sn * OWNERS
    mine = levels * sn
    me = lax.axis_index("x") * CORE + lax.axis_index("core")
    here = me.reshape(1)

    e = estimate.astype(BF16).reshape(mine, K, T)
    other = functools.partial(lax.ppermute, axis_name="core", perm=shift(CORE, 1))

    def along(block):
        perm = []
        for x in range(X):
            perm.append((x * CORE, (x + 1) % X * CORE))
            perm.append((x * CORE + 1, (x - 1) % X * CORE + 1))
        return lax.ppermute(block, snode, perm)

    first = along(e)
    swapped = other(e)
    swapped, here = lax.optimization_barrier((swapped, here))
    second = along(swapped)
    plan, note = pl.pallas_call(
        functools.partial(plan_kernel, sn),
        out_shape=(
            jax.ShapeDtypeStruct((5, tiles), jnp.int32),
            pltpu.HBM((OWNERS, 16, T), BF16),
        ),
        in_specs=[SMEM, SMEM, SMEM],
        out_specs=(SMEM, VMEM),
        scratch_shapes=[pltpu.SMEM((OWNERS,), jnp.int32), pltpu.VMEM((OWNERS, 16, T), F32)],
        compiler_params=PARAMS,
        name="plan",
    )(here, in_hbm(tile_col), in_hbm(tile_row))
    third = along(first)
    cross_first = other(first)
    (a_near,) = bring_near(None, a_tiles)
    side = in_hbm(right_side)
    second, note, a_near = lax.optimization_barrier((second, note, a_near))
    cross_second, cross_third = other(second), other(third)
    blocks = [e, swapped, third, cross_third, first, second, cross_second, cross_first]

    slot_rows = CAP * K + 16
    residual, *send = pl.pallas_call(
        functools.partial(tile_kernel, len(blocks)),
        out_shape=(
            jax.ShapeDtypeStruct((row_tiles, K, T), F32),
        )
        + (pltpu.HBM((slot_rows // 16, 16, T), BF16),) * OWNERS,
        in_specs=[SMEM, SMEM, ANY, ANY, VMEM] + [ANY] * len(blocks),
        out_specs=(VMEM,) * (1 + OWNERS),
        scratch_shapes=[
            pltpu.VMEM((OWNERS * slot_rows // 16, 16, T), BF16),
            pltpu.VMEM((OWNERS * mine, K, T), BF16),
            pltpu.VMEM((row_tiles, K, T), BF16),
            pltpu.SemaphoreType.DMA((len(blocks) + 1,)),
            pltpu.SemaphoreType.DMA((OWNERS,)),
        ],
        compiler_params=PARAMS,
        name="tile_products",
    )(lax.axis_index("core").reshape(1), plan, in_hbm(note), side, a_near, *blocks)

    to = jnp.arange(mine * K)
    y = lax.axis_index("y")
    place = jnp.arange(Y * Z * mine)
    column_k = (place // mine) % Z * Y + (place // (mine * Z) + y) % Y
    place = (place % mine) * K + column_k
    first_send, coupling_source = lax.optimization_barrier((send[0], coupling_source))
    source = coupling_source.reshape(levels - 1, -1)
    block_rows = 8
    spot_at = source // sn * block_rows + source % sn
    n_terms = source.shape[1]
    pad_terms = -n_terms % 16
    spot_at = jnp.pad(spot_at, ((0, 0), (0, pad_terms)), constant_values=-1)
    look, scatter = [], []
    for level in range(1, levels):
        spots = jnp.arange(level * OWNERS * block_rows)
        look.append((spot_at[level - 1][:, None] == spots[None, :]).astype(BF16))
        scatter.append((spots[:, None] == spot_at[level - 1][None, :]).astype(BF16))
    stage = pltpu.VMEM((n_terms + pad_terms, T), F32)

    recv = [first_send]
    for away in (3, 2, 1, 4, 5, 6, 7):
        step, swap = away // CORE, away % CORE
        perm = []
        for x in range(X):
            for c in range(CORE):
                perm.append((x * CORE + c, (x + step) % X * CORE + (c + swap) % CORE))
        recv.append(lax.ppermute(send[away], snode, perm))
    recv, look, scatter, to, place = lax.optimization_barrier((recv, look, scatter, to, place))
    part = pl.pallas_call(
        functools.partial(pick_kernel, mine),
        out_shape=(jax.ShapeDtypeStruct((Z * mine, T), BF16),) * Y,
        in_specs=[SMEM, ANY] + [VMEM] * (OWNERS - 1),
        out_specs=(VMEM,) * Y,
        scratch_shapes=[
            pltpu.VMEM((slot_rows // 16, 16, T), BF16),
            pltpu.VMEM((OWNERS * CAP * K, T), BF16),
            pltpu.VMEM((Z * mine, OWNERS * CAP * K), BF16),
            pltpu.SemaphoreType.DMA(()),
        ],
        compiler_params=PARAMS,
        name="pick",
    )(y.reshape(1), in_hbm(recv[0]), *recv[1:])
    total = part[0].astype(F32)
    arrived = [lax.ppermute(part[s], "y", shift(Y, s)) for s in (2, 1, 3)]
    (c_near,) = bring_near(part[0], coupling)
    arrived, c_near = lax.optimization_barrier((arrived, c_near))
    for block in arrived:
        total = total + block.astype(F32)
    parts = lax.all_to_all(total.astype(BF16).reshape(Z, mine, T), "z", 0, 0, tiled=True)

    def d_spec(level):
        return pl.BlockSpec((1, sn, T, T), lambda i: (level, 0, 0, 0))

    def c_spec(level):
        return pl.BlockSpec((1, sn, coupling.shape[2], T, T), lambda i: (level - 1, 0, 0, 0, 0))

    row4 = jax.ShapeDtypeStruct((sn, T), F32)
    by_owner = jax.ShapeDtypeStruct((OWNERS, block_rows, T), BF16)

    def rest_of(level):
        return (jax.ShapeDtypeStruct(((level - 1) * OWNERS * block_rows, T), F32),) if level > 1 else ()

    g, value, out = pl.pallas_call(
        functools.partial(first_kernel, sn),
        grid=(1,),
        out_shape=(jax.ShapeDtypeStruct((mine, T), F32), row4, by_owner),
        in_specs=[VMEM, d_spec(0)],
        out_specs=(VMEM, VMEM, VMEM),
        compiler_params=PARAMS,
        name="forward_0",
    )(parts, diag_inverse)
    known, solved = [], [value]
    for level in range(1, levels):
        known.append(lax.all_to_all(out, snode, 0, 0, tiled=True))
        if level < levels - 1:
            value, out = pl.pallas_call(
                functools.partial(forward_kernel, level, sn),
                grid=(1,),
                out_shape=(row4, by_owner),
                in_specs=[VMEM] * (2 + level) + [c_spec(level), d_spec(level)],
                out_specs=(VMEM, VMEM),
                compiler_params=PARAMS,
                name=f"forward_{level}",
            )(g, look[level - 1], *known, c_near, diag_inverse)
            solved.append(value)
        else:
            out_shape = (row4, by_owner) + rest_of(level)
            change, out, *rest = pl.pallas_call(
                functools.partial(turn_kernel, level, sn),
                grid=(1,),
                out_shape=out_shape,
                in_specs=[VMEM] * (3 + level) + [c_spec(level), d_spec(level)],
                out_specs=(VMEM,) * len(out_shape),
                scratch_shapes=[stage],
                compiler_params=PARAMS,
                name="turn",
            )(g, look[level - 1], scatter[level - 1], *known, c_near, diag_inverse)
    changes = [change]
    for level in reversed(range(levels - 1)):
        arrived = lax.all_to_all(out, snode, 0, 0, tiled=True)
        if level > 0:
            out_shape = (row4, by_owner) + rest_of(level)
            change, out, *rest = pl.pallas_call(
                functools.partial(backward_kernel, level, sn),
                grid=(1,),
                out_shape=out_shape,
                in_specs=[VMEM] * 4 + [c_spec(level), d_spec(level)],
                out_specs=(VMEM,) * len(out_shape),
                scratch_shapes=[stage],
                compiler_params=PARAMS,
                name=f"backward_{level}",
            )(solved[level], arrived, rest[0], scatter[level - 1], c_near, diag_inverse)
            changes.append(change)
        else:
            change = pl.pallas_call(
                functools.partial(last_kernel, sn),
                grid=(1,),
                out_shape=jax.ShapeDtypeStruct((Z, mine, T), BF16),
                in_specs=[VMEM] * 5 + [d_spec(0)],
                out_specs=VMEM,
                scratch_shapes=[pltpu.VMEM((sn, T), F32)],
                compiler_params=PARAMS,
                name="backward_0",
            )(solved[0], arrived, *changes, diag_inverse)
    column = lax.all_to_all(change, "z", 0, 0, tiled=True)
    far, ahead, behind = [lax.ppermute(column, "y", shift(Y, -s % Y)) for s in (2, 1, 3)]
    pieces = [column, ahead, far, behind]
    pieces = jnp.concatenate(pieces, axis=0).reshape(Y * Z * mine, T)
    sort = (to[:, None] == place[None, :]).astype(BF16)
    change = jnp.dot(sort, pieces, preferred_element_type=F32)
    new_estimate = estimate + change.reshape(estimate.shape)
    return new_estimate, residual


def solution(mesh):
    grid = jax.sharding.Mesh(mesh.devices.reshape(Z, Y, X, CORE), ("z", "y", "x", "core"))
    every, snode = ("z", "y", "x", "core"), ("x", "core")
    in_specs = (
        P(every, None, None),
        P(every),
        P(every),
        P(every, None, None),
        P(None, snode, None, None),
        P(None, snode, None, None),
        P(None, snode, None, None, None),
        P(None, snode, None),
    )
    out_specs = (P(None, snode, None, None), P(every, None, None))
    return jax.shard_map(local, mesh=grid, in_specs=in_specs, out_specs=out_specs, check_vma=False)
```

```python
import functools

import jax
import jax.numpy as jnp
from jax import lax
from jax.experimental import pallas as pl
from jax.experimental.pallas import tpu as pltpu
from jax.sharding import PartitionSpec as P

CAP = 6
X, CORE, Y, Z = 4, 2, 4, 8
OWNERS = X * CORE
F32 = jnp.float32
BF16 = jnp.bfloat16
NT = (((1,), (1,)), ((), ()))
NN = (((1,), (0,)), ((), ()))
SMEM = pl.BlockSpec(memory_space=pltpu.SMEM)
VMEM = pl.BlockSpec(memory_space=pltpu.VMEM)
ANY = pl.BlockSpec(memory_space=pl.ANY)
PARAMS = pltpu.CompilerParams(vmem_limit_bytes=16 * 1024 * 1024)


def dot(x, y, dims):
    return lax.dot_general(x, y, dims, preferred_element_type=F32)


def ring_away(owner, here):
    step = (lax.shift_right_logical(owner, 1) + X - lax.shift_right_logical(here, 1)) & (X - 1)
    return step * CORE + ((owner ^ here) & 1)


def plan_kernel(sn, here_ref, col_ref, row_ref, plan_ref, note_ref, count_ref, note):
    note[...] = jnp.zeros_like(note)
    for o in range(OWNERS):
        count_ref[o] = 0
    for t in range(col_ref.shape[0]):
        c = col_ref[t]
        level, owner, inner = c // (sn * OWNERS), (c // sn) % OWNERS, c % sn
        rank = count_ref[owner]
        count_ref[owner] = rank + 1
        away = ring_away(owner, here_ref[0])
        plan_ref[0, t] = away
        plan_ref[1, t] = level * sn + inner
        plan_ref[2, t] = row_ref[t]
        plan_ref[3, t] = away
        plan_ref[4, t] = rank
        mark = (level * sn + inner + 1).astype(F32)
        note[away, pl.ds(rank, 1), :] = jnp.full((1, note.shape[2]), mark, F32)
    note_ref[...] = note[...].astype(BF16)


def tile_kernel(n_blocks, core_ref, plan_ref, note_ref, side_ref, a_ref, *refs):
    blocks = refs[:n_blocks]
    core = core_ref[0]
    res_ref, out_refs = refs[n_blocks], refs[n_blocks + 1 : n_blocks + 2 + X]
    send_ref, x_all, low_ref, sems, note_sems = refs[n_blocks + 2 + X :]
    tiles = a_ref.shape[0]
    mine = x_all.shape[0] // OWNERS
    half = x_all.shape[1] // 2
    per = send_ref.shape[0] // OWNERS
    copies = [pltpu.make_async_copy(side_ref, res_ref, sems.at[len(blocks)])]
    places = [0, 1, 4, 5] + [2 * X - 2 - 4 * core + i for i in range(2)] + [2 + 4 * core + i for i in range(2)]
    for i, block in enumerate(blocks):
        target = x_all.at[pl.ds(places[i] * mine, mine)]
        copies.append(pltpu.make_async_copy(block, target, sems.at[i]))
    for copy in copies:
        copy.start()
    send_ref[...] = jnp.zeros_like(send_ref)
    for o in range(OWNERS):
        copies.append(pltpu.make_async_copy(note_ref.at[o], send_ref.at[(o + 1) * per - 1], note_sems.at[o]))
        copies[-1].start()
    for copy in copies:
        copy.wait()
    for t in range(tiles):
        q = plan_ref[2, t]
        res_ref[q] -= dot(x_all[plan_ref[0, t] * mine + plan_ref[1, t]], a_ref[t], NT)
    low_ref[...] = res_ref[...].astype(BF16)
    for t in range(tiles):
        spot = plan_ref[3, t] * per + 2 * plan_ref[4, t]
        term = dot(low_ref[plan_ref[2, t]], a_ref[t], NN).astype(BF16)
        send_ref[spot] = term[:half]
        send_ref[spot + 1] = term[half:]
    at = 0
    for ref in out_refs:
        ref[...] = send_ref[at : at + ref.shape[0]]
        at += ref.shape[0]


def in_hbm(x):
    return pltpu.with_memory_space_constraint(x, pltpu.HBM)


def in_vmem(x):
    return pltpu.with_memory_space_constraint(x, pltpu.VMEM)


def near_kernel(n, parts, *refs):
    sems = refs[-1]
    outs = refs[-1 - n : -1]
    copies = []
    for i in range(n):
        size = refs[i].shape[0] // parts[i]
        for k in range(parts[i]):
            piece = pl.ds(k * size, size)
            copies.append(pltpu.make_async_copy(refs[i].at[piece], outs[i].at[piece], sems.at[len(copies)]))
    for copy in copies:
        copy.start()
    for copy in copies:
        copy.wait()


def bring_near(after, *operands):
    n = len(operands)
    parts = tuple(4 if x.shape[0] % 4 == 0 else x.shape[0] for x in operands)
    operands = [in_hbm(x) for x in operands]
    if after is not None:
        operands.append(after)
    out_shape = [jax.ShapeDtypeStruct(x.shape, x.dtype) for x in operands]
    return pl.pallas_call(
        functools.partial(near_kernel, n, parts),
        out_shape=tuple(out_shape[:n]),
        in_specs=[ANY] * len(operands),
        out_specs=(VMEM,) * n,
        scratch_shapes=[pltpu.SemaphoreType.DMA((sum(parts),))],
        compiler_params=PARAMS,
        name="bring_near",
    )(*operands)


def pick_kernel(mine, y_ref, *refs):
    recvs, outs, (data, pick) = refs[:OWNERS], refs[OWNERS:-2], refs[-2:]
    blocks, size, T = recvs[0].shape
    rows = (blocks - 1) * size
    K = rows // CAP
    lane = lax.broadcasted_iota(jnp.int32, (1, 128), 1)
    marks, codes = [], []
    for i, ref in enumerate(recvs):
        data[i * rows : (i + 1) * rows, :] = ref[: blocks - 1].reshape(rows, T)
        note = ref[blocks - 1].astype(F32)
        marks += [note[j : j + 1, :128] for j in range(CAP)]
    per = 128 // K
    column = (lane % K).astype(F32)
    for i in range(0, len(marks), per):
        mark = marks[i]
        for j in range(1, per):
            mark = jnp.where(lane // K == j, marks[i + j], mark)
        codes.append((mark - 1.0) * K + column)
    code = jnp.concatenate(codes, axis=1)
    for step, out in enumerate(outs):
        at = lax.broadcasted_iota(jnp.int32, (Z * mine, 1), 0)
        k = at // mine * Y + (y_ref[0] + step) % Y
        wanted = ((at % mine) * K + k).astype(F32)
        pick[...] = jnp.where(wanted == code, 1.0, 0.0).astype(BF16)
        out[...] = dot(pick[...], data[...], NN).astype(BF16)


def forward_rows(level, sn, g, look_ref, known_refs, c_ref, d_ref):
    if level > 0:
        known = jnp.concatenate([ref[...].astype(F32).reshape(-1, ref.shape[2]) for ref in known_refs], axis=0).astype(BF16)
        found = dot(look_ref[...], known, NN)
    rows = []
    for j in range(sn):
        acc = g[level * sn + j : level * sn + j + 1, :]
        if level > 0:
            n = c_ref.shape[2]
            for i in range(n):
                row = found[j * n + i : j * n + i + 1, :].astype(BF16)
                acc = acc - dot(row, c_ref[0, j, i], NN)
        rows.append(dot(acc.astype(BF16), d_ref[0, j], NN))
    return rows


def backward_rows(level, sn, remaining, c_ref, d_ref, change_ref, stage):
    for j in range(sn):
        change = dot(remaining[j].astype(BF16), d_ref[0, j], NT)
        change_ref[j : j + 1, :] = change
        if level > 0:
            n = c_ref.shape[2]
            low = change.astype(BF16)
            for i in range(n):
                stage[j * n + i : j * n + i + 1, :] = dot(low, c_ref[0, j, i], NT)


def spread(scatter_ref, stage):
    terms = stage[...]
    high = terms.astype(BF16)
    low = (terms - high.astype(F32)).astype(BF16)
    return dot(scatter_ref[...], high, NN) + dot(scatter_ref[...], low, NN)


def store_pend(pend, out_ref, rest_refs):
    n, rows, width = out_ref.shape
    base = pend.shape[0] - n * rows
    out_ref[...] = pend[base:, :].reshape(n, rows, width).astype(out_ref.dtype)
    for ref in rest_refs:
        ref[...] = pend[:base, :]


def spread_rows(rows, own_ref, out_ref):
    for j, row in enumerate(rows):
        own_ref[j : j + 1, :] = row
    filler = jnp.zeros((out_ref.shape[1] - len(rows), out_ref.shape[2]), F32)
    block = jnp.concatenate(rows + [filler], axis=0).astype(out_ref.dtype)
    for o in range(out_ref.shape[0]):
        out_ref[o] = block


def first_kernel(sn, parts_ref, d_ref, g_ref, own_ref, out_ref):
    total = parts_ref[0].astype(F32)
    for i in range(1, parts_ref.shape[0]):
        total = total + parts_ref[i].astype(F32)
    g_ref[...] = total
    spread_rows(forward_rows(0, sn, total, None, [], None, d_ref), own_ref, out_ref)


def forward_kernel(level, sn, g_ref, look_ref, *refs):
    known_refs, (c_ref, d_ref, own_ref, out_ref) = refs[:level], refs[level:]
    rows = forward_rows(level, sn, g_ref[...], look_ref, known_refs, c_ref, d_ref)
    spread_rows(rows, own_ref, out_ref)


def turn_kernel(level, sn, g_ref, look_ref, scatter_ref, *refs):
    known_refs, refs = refs[:level], refs[level:]
    c_ref, d_ref, change_ref, out_ref, rest_ref, stage = refs
    rows = forward_rows(level, sn, g_ref[...], look_ref, known_refs, c_ref, d_ref)
    stage[...] = jnp.zeros_like(stage)
    backward_rows(level, sn, rows, c_ref, d_ref, change_ref, stage)
    store_pend(spread(scatter_ref, stage), out_ref, [rest_ref])


def remaining_rows(sn, solved_ref, recv_ref):
    got = recv_ref[0].astype(F32)
    for i in range(1, recv_ref.shape[0]):
        got = got + recv_ref[i].astype(F32)
    return [solved_ref[j : j + 1, :] - got[j : j + 1, :] for j in range(sn)]


def backward_kernel(level, sn, solved_ref, recv_ref, pend_ref, scatter_ref, c_ref, d_ref, *refs):
    change_ref, out_ref, rest_refs, stage = refs[0], refs[1], refs[2:-1], refs[-1]
    stage[...] = jnp.zeros_like(stage)
    backward_rows(level, sn, remaining_rows(sn, solved_ref, recv_ref), c_ref, d_ref, change_ref, stage)
    store_pend(pend_ref[...] + spread(scatter_ref, stage), out_ref, rest_refs)


def last_kernel(sn, solved_ref, recv_ref, c3_ref, c2_ref, c1_ref, d_ref, out_ref, change):
    backward_rows(0, sn, remaining_rows(sn, solved_ref, recv_ref), None, d_ref, change, None)
    mine = jnp.concatenate([change[...], c1_ref[...], c2_ref[...], c3_ref[...]], axis=0).astype(BF16)
    for i in range(out_ref.shape[0]):
        out_ref[i] = mine


def shift(size, step):
    return [(i, (i + step) % size) for i in range(size)]


def local(a_tiles, tile_row, tile_col, right_side, estimate, diag_inverse, coupling, coupling_source):
    tiles, T = a_tiles.shape[0], a_tiles.shape[1]
    row_tiles, K = right_side.shape[0], right_side.shape[1]
    levels, sn = estimate.shape[0], estimate.shape[1]
    snode = ("x", "core")
    width = sn * OWNERS
    mine = levels * sn
    me = lax.axis_index("x") * CORE + lax.axis_index("core")
    here = me.reshape(1)

    e = estimate.astype(BF16).reshape(mine, K, T)
    other = functools.partial(lax.ppermute, axis_name="core", perm=shift(CORE, 1))

    def along(block):
        perm = []
        for x in range(X):
            perm.append((x * CORE, (x + 1) % X * CORE))
            perm.append((x * CORE + 1, (x - 1) % X * CORE + 1))
        return lax.ppermute(block, snode, perm)

    first = along(e)
    swapped = other(e)
    swapped, here = lax.optimization_barrier((swapped, here))
    second = along(swapped)
    plan, note = pl.pallas_call(
        functools.partial(plan_kernel, sn),
        out_shape=(
            jax.ShapeDtypeStruct((5, tiles), jnp.int32),
            pltpu.HBM((OWNERS, 16, T), BF16),
        ),
        in_specs=[SMEM, SMEM, SMEM],
        out_specs=(SMEM, VMEM),
        scratch_shapes=[pltpu.SMEM((OWNERS,), jnp.int32), pltpu.VMEM((OWNERS, 16, T), F32)],
        compiler_params=PARAMS,
        name="plan",
    )(here, in_hbm(tile_col), in_hbm(tile_row))
    third = along(first)
    cross_first = other(first)
    (a_near,) = bring_near(None, a_tiles)
    side = in_hbm(right_side)
    second, note, a_near = lax.optimization_barrier((second, note, a_near))
    cross_second, cross_third = other(second), other(third)
    blocks = [e, swapped, third, cross_third, first, second, cross_second, cross_first]

    slot_rows = CAP * K + 16
    residual, *send = pl.pallas_call(
        functools.partial(tile_kernel, len(blocks)),
        out_shape=(
            jax.ShapeDtypeStruct((row_tiles, K, T), F32),
        )
        + (jax.ShapeDtypeStruct((slot_rows // 16, 16, T), BF16),)
        + (pltpu.HBM((slot_rows // 16, 16, T), BF16),)
        + (pltpu.HBM((CORE * slot_rows // 16, 16, T), BF16),) * (X - 1),
        in_specs=[SMEM, SMEM, ANY, ANY, VMEM] + [ANY] * len(blocks),
        out_specs=(VMEM,) * (2 + X),
        scratch_shapes=[
            pltpu.VMEM((OWNERS * slot_rows // 16, 16, T), BF16),
            pltpu.VMEM((OWNERS * mine, K, T), BF16),
            pltpu.VMEM((row_tiles, K, T), BF16),
            pltpu.SemaphoreType.DMA((len(blocks) + 1,)),
            pltpu.SemaphoreType.DMA((OWNERS,)),
        ],
        compiler_params=PARAMS,
        name="tile_products",
    )(lax.axis_index("core").reshape(1), plan, in_hbm(note), side, a_near, *blocks)

    to = jnp.arange(mine * K)
    y = lax.axis_index("y")
    place = jnp.arange(Y * Z * mine)
    column_k = (place // mine) % Z * Y + (place // (mine * Z) + y) % Y
    place = (place % mine) * K + column_k
    first_send, coupling_source = lax.optimization_barrier((send[0], coupling_source))
    source = coupling_source.reshape(levels - 1, -1)
    block_rows = 8
    spot_at = source // sn * block_rows + source % sn
    n_terms = source.shape[1]
    pad_terms = -n_terms % 16
    spot_at = jnp.pad(spot_at, ((0, 0), (0, pad_terms)), constant_values=-1)
    look, scatter = [], []
    for level in range(1, levels):
        spots = jnp.arange(level * OWNERS * block_rows)
        look.append((spot_at[level - 1][:, None] == spots[None, :]).astype(BF16))
        scatter.append((spots[:, None] == spot_at[level - 1][None, :]).astype(BF16))
    stage = pltpu.VMEM((n_terms + pad_terms, T), F32)

    arrived = {step: lax.ppermute(send[1 + step], "x", shift(X, step)) for step in (2, 1, 3)}
    n = slot_rows // 16
    recv = [first_send, other(send[1])] + [other(arrived[step][n:]) for step in (2, 1, 3)] + [arrived[step] for step in (2, 1, 3)]
    recv, look, scatter, to, place = lax.optimization_barrier((recv, look, scatter, to, place))
    part = pl.pallas_call(
        functools.partial(pick_kernel, mine),
        out_shape=(jax.ShapeDtypeStruct((Z * mine, T), BF16),) * Y,
        in_specs=[SMEM] + [VMEM] * OWNERS,
        out_specs=(VMEM,) * Y,
        scratch_shapes=[
            pltpu.VMEM((OWNERS * CAP * K, T), BF16),
            pltpu.VMEM((Z * mine, OWNERS * CAP * K), BF16),
        ],
        compiler_params=PARAMS,
        name="pick",
    )(y.reshape(1), *recv)
    total = part[0].astype(F32)
    arrived = [lax.ppermute(part[s], "y", shift(Y, s)) for s in (2, 1, 3)]
    (c_near,) = bring_near(part[0], coupling)
    arrived, c_near = lax.optimization_barrier((arrived, c_near))
    for block in arrived:
        total = total + block.astype(F32)
    parts = lax.all_to_all(total.astype(BF16).reshape(Z, mine, T), "z", 0, 0, tiled=True)

    def d_spec(level):
        return pl.BlockSpec((1, sn, T, T), lambda i: (level, 0, 0, 0))

    def c_spec(level):
        return pl.BlockSpec((1, sn, coupling.shape[2], T, T), lambda i: (level - 1, 0, 0, 0, 0))

    row4 = jax.ShapeDtypeStruct((sn, T), F32)
    by_owner = jax.ShapeDtypeStruct((OWNERS, block_rows, T), BF16)

    def rest_of(level):
        return (jax.ShapeDtypeStruct(((level - 1) * OWNERS * block_rows, T), F32),) if level > 1 else ()

    g, value, out = pl.pallas_call(
        functools.partial(first_kernel, sn),
        grid=(1,),
        out_shape=(jax.ShapeDtypeStruct((mine, T), F32), row4, by_owner),
        in_specs=[VMEM, d_spec(0)],
        out_specs=(VMEM, VMEM, VMEM),
        compiler_params=PARAMS,
        name="forward_0",
    )(parts, diag_inverse)
    known, solved = [], [value]
    for level in range(1, levels):
        known.append(lax.all_to_all(out, snode, 0, 0, tiled=True))
        if level < levels - 1:
            value, out = pl.pallas_call(
                functools.partial(forward_kernel, level, sn),
                grid=(1,),
                out_shape=(row4, by_owner),
                in_specs=[VMEM] * (2 + level) + [c_spec(level), d_spec(level)],
                out_specs=(VMEM, VMEM),
                compiler_params=PARAMS,
                name=f"forward_{level}",
            )(g, look[level - 1], *known, c_near, diag_inverse)
            solved.append(value)
        else:
            out_shape = (row4, by_owner) + rest_of(level)
            change, out, *rest = pl.pallas_call(
                functools.partial(turn_kernel, level, sn),
                grid=(1,),
                out_shape=out_shape,
                in_specs=[VMEM] * (3 + level) + [c_spec(level), d_spec(level)],
                out_specs=(VMEM,) * len(out_shape),
                scratch_shapes=[stage],
                compiler_params=PARAMS,
                name="turn",
            )(g, look[level - 1], scatter[level - 1], *known, c_near, diag_inverse)
    changes = [change]
    for level in reversed(range(levels - 1)):
        arrived = lax.all_to_all(out, snode, 0, 0, tiled=True)
        if level > 0:
            out_shape = (row4, by_owner) + rest_of(level)
            change, out, *rest = pl.pallas_call(
                functools.partial(backward_kernel, level, sn),
                grid=(1,),
                out_shape=out_shape,
                in_specs=[VMEM] * 4 + [c_spec(level), d_spec(level)],
                out_specs=(VMEM,) * len(out_shape),
                scratch_shapes=[stage],
                compiler_params=PARAMS,
                name=f"backward_{level}",
            )(solved[level], arrived, rest[0], scatter[level - 1], c_near, diag_inverse)
            changes.append(change)
        else:
            change = pl.pallas_call(
                functools.partial(last_kernel, sn),
                grid=(1,),
                out_shape=jax.ShapeDtypeStruct((Z, mine, T), BF16),
                in_specs=[VMEM] * 5 + [d_spec(0)],
                out_specs=VMEM,
                scratch_shapes=[pltpu.VMEM((sn, T), F32)],
                compiler_params=PARAMS,
                name="backward_0",
            )(solved[0], arrived, *changes, diag_inverse)
    column = lax.all_to_all(change, "z", 0, 0, tiled=True)
    far, ahead, behind = [lax.ppermute(column, "y", shift(Y, -s % Y)) for s in (2, 1, 3)]
    pieces = [column, ahead, far, behind]
    pieces = jnp.concatenate(pieces, axis=0).reshape(Y * Z * mine, T)
    sort = (to[:, None] == place[None, :]).astype(BF16)
    change = jnp.dot(sort, pieces, preferred_element_type=F32)
    new_estimate = estimate + change.reshape(estimate.shape)
    return new_estimate, residual


def solution(mesh):
    grid = jax.sharding.Mesh(mesh.devices.reshape(Z, Y, X, CORE), ("z", "y", "x", "core"))
    every, snode = ("z", "y", "x", "core"), ("x", "core")
    in_specs = (
        P(every, None, None),
        P(every),
        P(every),
        P(every, None, None),
        P(None, snode, None, None),
        P(None, snode, None, None),
        P(None, snode, None, None, None),
        P(None, snode, None),
    )
    out_specs = (P(None, snode, None, None), P(every, None, None))
    return jax.shard_map(local, mesh=grid, in_specs=in_specs, out_specs=out_specs, check_vma=False)
```

```python
import functools

import jax
import jax.numpy as jnp
from jax import lax
from jax.experimental import pallas as pl
from jax.experimental.pallas import tpu as pltpu
from jax.sharding import PartitionSpec as P

CAP = 6
X, CORE, Y, Z = 4, 2, 4, 8
OWNERS = X * CORE
F32 = jnp.float32
BF16 = jnp.bfloat16
NT = (((1,), (1,)), ((), ()))
NN = (((1,), (0,)), ((), ()))
SMEM = pl.BlockSpec(memory_space=pltpu.SMEM)
VMEM = pl.BlockSpec(memory_space=pltpu.VMEM)
ANY = pl.BlockSpec(memory_space=pl.ANY)
PARAMS = pltpu.CompilerParams(vmem_limit_bytes=16 * 1024 * 1024)


def dot(x, y, dims):
    return lax.dot_general(x, y, dims, preferred_element_type=F32)


def ring_away(owner, here):
    step = (lax.shift_right_logical(owner, 1) + X - lax.shift_right_logical(here, 1)) & (X - 1)
    return step * CORE + ((owner ^ here) & 1)


def plan_kernel(sn, here_ref, col_ref, row_ref, plan_ref, note_ref, count_ref, note):
    note[...] = jnp.zeros_like(note)
    for o in range(OWNERS):
        count_ref[o] = 0
    for t in range(col_ref.shape[0]):
        c = col_ref[t]
        level, owner, inner = c // (sn * OWNERS), (c // sn) % OWNERS, c % sn
        rank = count_ref[owner]
        count_ref[owner] = rank + 1
        away = ring_away(owner, here_ref[0])
        plan_ref[0, t] = away
        plan_ref[1, t] = level * sn + inner
        plan_ref[2, t] = row_ref[t]
        plan_ref[3, t] = away
        plan_ref[4, t] = rank
        mark = (level * sn + inner + 1).astype(F32)
        note[away, pl.ds(rank, 1), :] = jnp.full((1, note.shape[2]), mark, F32)
    note_ref[...] = note[...].astype(BF16)


def tile_kernel(n_blocks, core_ref, plan_ref, note_ref, side_ref, a_ref, *refs):
    blocks = refs[:n_blocks]
    core = core_ref[0]
    res_ref, out_refs = refs[n_blocks], refs[n_blocks + 1 : n_blocks + 1 + OWNERS]
    send_ref, x_all, low_ref, sems, note_sems = refs[n_blocks + 1 + OWNERS :]
    tiles = a_ref.shape[0]
    mine = x_all.shape[0] // OWNERS
    half = x_all.shape[1] // 2
    per = send_ref.shape[0] // OWNERS
    copies = [pltpu.make_async_copy(side_ref, res_ref, sems.at[len(blocks)])]
    places = [0, 1, 4, 5] + [2 * X - 2 - 4 * core + i for i in range(2)] + [2 + 4 * core + i for i in range(2)]
    for i, block in enumerate(blocks):
        target = x_all.at[pl.ds(places[i] * mine, mine)]
        copies.append(pltpu.make_async_copy(block, target, sems.at[i]))
    for copy in copies:
        copy.start()
    send_ref[...] = jnp.zeros_like(send_ref)
    for o in range(OWNERS):
        copies.append(pltpu.make_async_copy(note_ref.at[o], send_ref.at[(o + 1) * per - 1], note_sems.at[o]))
        copies[-1].start()
    for copy in copies:
        copy.wait()
    for t in range(tiles):
        q = plan_ref[2, t]
        res_ref[q] -= dot(x_all[plan_ref[0, t] * mine + plan_ref[1, t]], a_ref[t], NT)
    low_ref[...] = res_ref[...].astype(BF16)
    for t in range(tiles):
        spot = plan_ref[3, t] * per + 2 * plan_ref[4, t]
        term = dot(low_ref[plan_ref[2, t]], a_ref[t], NN).astype(BF16)
        send_ref[spot] = term[:half]
        send_ref[spot + 1] = term[half:]
    for o, ref in enumerate(out_refs):
        ref[...] = send_ref[o * per : (o + 1) * per]


def in_hbm(x):
    return pltpu.with_memory_space_constraint(x, pltpu.HBM)


def in_vmem(x):
    return pltpu.with_memory_space_constraint(x, pltpu.VMEM)


def near_kernel(n, parts, *refs):
    sems = refs[-1]
    outs = refs[-1 - n : -1]
    copies = []
    for i in range(n):
        size = refs[i].shape[0] // parts[i]
        for k in range(parts[i]):
            piece = pl.ds(k * size, size)
            copies.append(pltpu.make_async_copy(refs[i].at[piece], outs[i].at[piece], sems.at[len(copies)]))
    for copy in copies:
        copy.start()
    for copy in copies:
        copy.wait()


def bring_near(after, *operands):
    n = len(operands)
    parts = tuple(4 if x.shape[0] % 4 == 0 else x.shape[0] for x in operands)
    operands = [in_hbm(x) for x in operands]
    if after is not None:
        operands.append(after)
    out_shape = [jax.ShapeDtypeStruct(x.shape, x.dtype) for x in operands]
    return pl.pallas_call(
        functools.partial(near_kernel, n, parts),
        out_shape=tuple(out_shape[:n]),
        in_specs=[ANY] * len(operands),
        out_specs=(VMEM,) * n,
        scratch_shapes=[pltpu.SemaphoreType.DMA((sum(parts),))],
        compiler_params=PARAMS,
        name="bring_near",
    )(*operands)


def pick_kernel(mine, y_ref, *refs):
    recvs, outs, (data, pick) = refs[:OWNERS], refs[OWNERS:-2], refs[-2:]
    blocks, size, T = recvs[0].shape
    rows = (blocks - 1) * size
    K = rows // CAP
    lane = lax.broadcasted_iota(jnp.int32, (1, 128), 1)
    marks, codes = [], []
    for i, ref in enumerate(recvs):
        data[i * rows : (i + 1) * rows, :] = ref[: blocks - 1].reshape(rows, T)
        note = ref[blocks - 1].astype(F32)
        marks += [note[j : j + 1, :128] for j in range(CAP)]
    per = 128 // K
    column = (lane % K).astype(F32)
    for i in range(0, len(marks), per):
        mark = marks[i]
        for j in range(1, per):
            mark = jnp.where(lane // K == j, marks[i + j], mark)
        codes.append((mark - 1.0) * K + column)
    code = jnp.concatenate(codes, axis=1)
    for step, out in enumerate(outs):
        at = lax.broadcasted_iota(jnp.int32, (Z * mine, 1), 0)
        k = at // mine * Y + (y_ref[0] + step) % Y
        wanted = ((at % mine) * K + k).astype(F32)
        pick[...] = jnp.where(wanted == code, 1.0, 0.0).astype(BF16)
        out[...] = dot(pick[...], data[...], NN).astype(BF16)


def forward_rows(level, sn, g, look_ref, known_refs, c_ref, d_ref):
    if level > 0:
        known = jnp.concatenate([ref[...].astype(F32).reshape(-1, ref.shape[2]) for ref in known_refs], axis=0).astype(BF16)
        found = dot(look_ref[...], known, NN)
    rows = []
    for j in range(sn):
        acc = g[level * sn + j : level * sn + j + 1, :]
        if level > 0:
            n = c_ref.shape[2]
            for i in range(n):
                row = found[j * n + i : j * n + i + 1, :].astype(BF16)
                acc = acc - dot(row, c_ref[0, j, i], NN)
        rows.append(dot(acc.astype(BF16), d_ref[0, j], NN))
    return rows


def backward_rows(level, sn, remaining, c_ref, d_ref, change_ref, stage):
    for j in range(sn):
        change = dot(remaining[j].astype(BF16), d_ref[0, j], NT)
        change_ref[j : j + 1, :] = change
        if level > 0:
            n = c_ref.shape[2]
            low = change.astype(BF16)
            for i in range(n):
                stage[j * n + i : j * n + i + 1, :] = dot(low, c_ref[0, j, i], NT)


def spread(scatter_ref, stage):
    terms = stage[...]
    high = terms.astype(BF16)
    low = (terms - high.astype(F32)).astype(BF16)
    return dot(scatter_ref[...], high, NN) + dot(scatter_ref[...], low, NN)


def store_pend(pend, out_ref, rest_refs):
    n, rows, width = out_ref.shape
    base = pend.shape[0] - n * rows
    out_ref[...] = pend[base:, :].reshape(n, rows, width).astype(out_ref.dtype)
    for ref in rest_refs:
        ref[...] = pend[:base, :]


def spread_rows(rows, own_ref, out_ref):
    for j, row in enumerate(rows):
        own_ref[j : j + 1, :] = row
    filler = jnp.zeros((out_ref.shape[1] - len(rows), out_ref.shape[2]), F32)
    block = jnp.concatenate(rows + [filler], axis=0).astype(out_ref.dtype)
    for o in range(out_ref.shape[0]):
        out_ref[o] = block


def first_kernel(sn, parts_ref, d_ref, g_ref, own_ref, out_ref):
    total = parts_ref[0].astype(F32)
    for i in range(1, parts_ref.shape[0]):
        total = total + parts_ref[i].astype(F32)
    g_ref[...] = total
    spread_rows(forward_rows(0, sn, total, None, [], None, d_ref), own_ref, out_ref)


def forward_kernel(level, sn, g_ref, look_ref, *refs):
    known_refs, (c_ref, d_ref, own_ref, out_ref) = refs[:level], refs[level:]
    rows = forward_rows(level, sn, g_ref[...], look_ref, known_refs, c_ref, d_ref)
    spread_rows(rows, own_ref, out_ref)


def turn_kernel(level, sn, g_ref, look_ref, scatter_ref, *refs):
    known_refs, refs = refs[:level], refs[level:]
    c_ref, d_ref, change_ref, out_ref, rest_ref, stage = refs
    rows = forward_rows(level, sn, g_ref[...], look_ref, known_refs, c_ref, d_ref)
    stage[...] = jnp.zeros_like(stage)
    backward_rows(level, sn, rows, c_ref, d_ref, change_ref, stage)
    store_pend(spread(scatter_ref, stage), out_ref, [rest_ref])


def remaining_rows(sn, solved_ref, recv_ref):
    got = recv_ref[0].astype(F32)
    for i in range(1, recv_ref.shape[0]):
        got = got + recv_ref[i].astype(F32)
    return [solved_ref[j : j + 1, :] - got[j : j + 1, :] for j in range(sn)]


def backward_kernel(level, sn, solved_ref, recv_ref, pend_ref, scatter_ref, c_ref, d_ref, *refs):
    change_ref, out_ref, rest_refs, stage = refs[0], refs[1], refs[2:-1], refs[-1]
    stage[...] = jnp.zeros_like(stage)
    backward_rows(level, sn, remaining_rows(sn, solved_ref, recv_ref), c_ref, d_ref, change_ref, stage)
    store_pend(pend_ref[...] + spread(scatter_ref, stage), out_ref, rest_refs)


def last_kernel(sn, solved_ref, recv_ref, c3_ref, c2_ref, c1_ref, d_ref, out_ref, change):
    backward_rows(0, sn, remaining_rows(sn, solved_ref, recv_ref), None, d_ref, change, None)
    mine = jnp.concatenate([change[...], c1_ref[...], c2_ref[...], c3_ref[...]], axis=0).astype(BF16)
    for i in range(out_ref.shape[0]):
        out_ref[i] = mine


def shift(size, step):
    return [(i, (i + step) % size) for i in range(size)]


def local(a_tiles, tile_row, tile_col, right_side, estimate, diag_inverse, coupling, coupling_source):
    tiles, T = a_tiles.shape[0], a_tiles.shape[1]
    row_tiles, K = right_side.shape[0], right_side.shape[1]
    levels, sn = estimate.shape[0], estimate.shape[1]
    snode = ("x", "core")
    width = sn * OWNERS
    mine = levels * sn
    me = lax.axis_index("x") * CORE + lax.axis_index("core")
    here = me.reshape(1)

    e = estimate.astype(BF16).reshape(mine, K, T)
    other = functools.partial(lax.ppermute, axis_name="core", perm=shift(CORE, 1))

    def along(block):
        perm = []
        for x in range(X):
            perm.append((x * CORE, (x + 1) % X * CORE))
            perm.append((x * CORE + 1, (x - 1) % X * CORE + 1))
        return lax.ppermute(block, snode, perm)

    first = along(e)
    swapped = other(e)
    swapped, here = lax.optimization_barrier((swapped, here))
    second = along(swapped)
    plan, note = pl.pallas_call(
        functools.partial(plan_kernel, sn),
        out_shape=(
            jax.ShapeDtypeStruct((5, tiles), jnp.int32),
            pltpu.HBM((OWNERS, 16, T), BF16),
        ),
        in_specs=[SMEM, SMEM, SMEM],
        out_specs=(SMEM, VMEM),
        scratch_shapes=[pltpu.SMEM((OWNERS,), jnp.int32), pltpu.VMEM((OWNERS, 16, T), F32)],
        compiler_params=PARAMS,
        name="plan",
    )(here, in_hbm(tile_col), in_hbm(tile_row))
    third = along(first)
    cross_first = other(first)
    (a_near,) = bring_near(None, a_tiles)
    side = in_hbm(right_side)
    second, note, a_near = lax.optimization_barrier((second, note, a_near))
    cross_second, cross_third = other(second), other(third)
    blocks = [e, swapped, third, cross_third, first, second, cross_second, cross_first]

    slot_rows = CAP * K + 16
    residual, *send = pl.pallas_call(
        functools.partial(tile_kernel, len(blocks)),
        out_shape=(
            jax.ShapeDtypeStruct((row_tiles, K, T), F32),
        )
        + (jax.ShapeDtypeStruct((slot_rows // 16, 16, T), BF16),)
        + (pltpu.HBM((slot_rows // 16, 16, T), BF16),) * (OWNERS - 1),
        in_specs=[SMEM, SMEM, ANY, ANY, VMEM] + [ANY] * len(blocks),
        out_specs=(VMEM,) * (1 + OWNERS),
        scratch_shapes=[
            pltpu.VMEM((OWNERS * slot_rows // 16, 16, T), BF16),
            pltpu.VMEM((OWNERS * mine, K, T), BF16),
            pltpu.VMEM((row_tiles, K, T), BF16),
            pltpu.SemaphoreType.DMA((len(blocks) + 1,)),
            pltpu.SemaphoreType.DMA((OWNERS,)),
        ],
        compiler_params=PARAMS,
        name="tile_products",
    )(lax.axis_index("core").reshape(1), plan, in_hbm(note), side, a_near, *blocks)

    to = jnp.arange(mine * K)
    y = lax.axis_index("y")
    place = jnp.arange(Y * Z * mine)
    column_k = (place // mine) % Z * Y + (place // (mine * Z) + y) % Y
    place = (place % mine) * K + column_k
    first_send, coupling_source = lax.optimization_barrier((send[0], coupling_source))
    source = coupling_source.reshape(levels - 1, -1)
    block_rows = 8
    owner = source // sn % OWNERS
    block = source // width * OWNERS + owner % CORE * X + owner // CORE
    spot_at = block * block_rows + source % sn
    n_terms = source.shape[1]
    pad_terms = -n_terms % 16
    spot_at = jnp.pad(spot_at, ((0, 0), (0, pad_terms)), constant_values=-1)
    look, scatter = [], []
    for level in range(1, levels):
        spots = jnp.arange(level * OWNERS * block_rows)
        look.append((spot_at[level - 1][:, None] == spots[None, :]).astype(BF16))
        scatter.append((spots[:, None] == spot_at[level - 1][None, :]).astype(BF16))
    stage = pltpu.VMEM((n_terms + pad_terms, T), F32)

    recv = [first_send]
    for away in (3, 2, 1, 4, 5, 6, 7):
        step, swap = away // CORE, away % CORE
        perm = []
        for x in range(X):
            for c in range(CORE):
                perm.append((x * CORE + c, (x + step) % X * CORE + (c + swap) % CORE))
        recv.append(lax.ppermute(send[away], snode, perm))
    recv, look, scatter, to, place = lax.optimization_barrier((recv, look, scatter, to, place))
    part = pl.pallas_call(
        functools.partial(pick_kernel, mine),
        out_shape=(jax.ShapeDtypeStruct((Z * mine, T), BF16),) * Y,
        in_specs=[SMEM] + [VMEM] * OWNERS,
        out_specs=(VMEM,) * Y,
        scratch_shapes=[
            pltpu.VMEM((OWNERS * CAP * K, T), BF16),
            pltpu.VMEM((Z * mine, OWNERS * CAP * K), BF16),
        ],
        compiler_params=PARAMS,
        name="pick",
    )(y.reshape(1), *recv)
    total = part[0].astype(F32)
    arrived = [lax.ppermute(part[s], "y", shift(Y, s)) for s in (2, 1, 3)]
    (c_near,) = bring_near(part[0], coupling)
    arrived, c_near = lax.optimization_barrier((arrived, c_near))
    for block in arrived:
        total = total + block.astype(F32)
    parts = lax.all_to_all(total.astype(BF16).reshape(Z, mine, T), "z", 0, 0, tiled=True)

    def d_spec(level):
        return pl.BlockSpec((1, sn, T, T), lambda i: (level, 0, 0, 0))

    def c_spec(level):
        return pl.BlockSpec((1, sn, coupling.shape[2], T, T), lambda i: (level - 1, 0, 0, 0, 0))

    row4 = jax.ShapeDtypeStruct((sn, T), F32)
    by_owner = jax.ShapeDtypeStruct((OWNERS, block_rows, T), BF16)

    def rest_of(level):
        return (jax.ShapeDtypeStruct(((level - 1) * OWNERS * block_rows, T), F32),) if level > 1 else ()

    g, value, out = pl.pallas_call(
        functools.partial(first_kernel, sn),
        grid=(1,),
        out_shape=(jax.ShapeDtypeStruct((mine, T), F32), row4, by_owner),
        in_specs=[VMEM, d_spec(0)],
        out_specs=(VMEM, VMEM, VMEM),
        compiler_params=PARAMS,
        name="forward_0",
    )(parts, diag_inverse)
    known, solved = [], [value]
    for level in range(1, levels):
        known.append(lax.all_to_all(out, ("core", "x"), 0, 0, tiled=True))
        if level < levels - 1:
            value, out = pl.pallas_call(
                functools.partial(forward_kernel, level, sn),
                grid=(1,),
                out_shape=(row4, by_owner),
                in_specs=[VMEM] * (2 + level) + [c_spec(level), d_spec(level)],
                out_specs=(VMEM, VMEM),
                compiler_params=PARAMS,
                name=f"forward_{level}",
            )(g, look[level - 1], *known, c_near, diag_inverse)
            solved.append(value)
        else:
            out_shape = (row4, by_owner) + rest_of(level)
            change, out, *rest = pl.pallas_call(
                functools.partial(turn_kernel, level, sn),
                grid=(1,),
                out_shape=out_shape,
                in_specs=[VMEM] * (3 + level) + [c_spec(level), d_spec(level)],
                out_specs=(VMEM,) * len(out_shape),
                scratch_shapes=[stage],
                compiler_params=PARAMS,
                name="turn",
            )(g, look[level - 1], scatter[level - 1], *known, c_near, diag_inverse)
    changes = [change]
    for level in reversed(range(levels - 1)):
        arrived = lax.all_to_all(out, ("core", "x"), 0, 0, tiled=True)
        if level > 0:
            out_shape = (row4, by_owner) + rest_of(level)
            change, out, *rest = pl.pallas_call(
                functools.partial(backward_kernel, level, sn),
                grid=(1,),
                out_shape=out_shape,
                in_specs=[VMEM] * 4 + [c_spec(level), d_spec(level)],
                out_specs=(VMEM,) * len(out_shape),
                scratch_shapes=[stage],
                compiler_params=PARAMS,
                name=f"backward_{level}",
            )(solved[level], arrived, rest[0], scatter[level - 1], c_near, diag_inverse)
            changes.append(change)
        else:
            change = pl.pallas_call(
                functools.partial(last_kernel, sn),
                grid=(1,),
                out_shape=jax.ShapeDtypeStruct((Z, mine, T), BF16),
                in_specs=[VMEM] * 5 + [d_spec(0)],
                out_specs=VMEM,
                scratch_shapes=[pltpu.VMEM((sn, T), F32)],
                compiler_params=PARAMS,
                name="backward_0",
            )(solved[0], arrived, *changes, diag_inverse)
    column = lax.all_to_all(change, "z", 0, 0, tiled=True)
    far, ahead, behind = [lax.ppermute(column, "y", shift(Y, -s % Y)) for s in (2, 1, 3)]
    pieces = [column, ahead, far, behind]
    pieces = jnp.concatenate(pieces, axis=0).reshape(Y * Z * mine, T)
    sort = (to[:, None] == place[None, :]).astype(BF16)
    change = jnp.dot(sort, pieces, preferred_element_type=F32)
    new_estimate = estimate + change.reshape(estimate.shape)
    return new_estimate, residual


def solution(mesh):
    grid = jax.sharding.Mesh(mesh.devices.reshape(Z, Y, X, CORE), ("z", "y", "x", "core"))
    every, snode = ("z", "y", "x", "core"), ("x", "core")
    in_specs = (
        P(every, None, None),
        P(every),
        P(every),
        P(every, None, None),
        P(None, snode, None, None),
        P(None, snode, None, None),
        P(None, snode, None, None, None),
        P(None, snode, None),
    )
    out_specs = (P(None, snode, None, None), P(every, None, None))
    return jax.shard_map(local, mesh=grid, in_specs=in_specs, out_specs=out_specs, check_vma=False)
```

```python
import functools

import jax
import jax.numpy as jnp
from jax import lax
from jax.experimental import pallas as pl
from jax.experimental.pallas import tpu as pltpu
from jax.sharding import PartitionSpec as P

CAP = 6
X, CORE, Y, Z = 4, 2, 4, 8
OWNERS = X * CORE
LAST = 2 * CORE + 1
F32 = jnp.float32
BF16 = jnp.bfloat16
NT = (((1,), (1,)), ((), ()))
NN = (((1,), (0,)), ((), ()))
SMEM = pl.BlockSpec(memory_space=pltpu.SMEM)
VMEM = pl.BlockSpec(memory_space=pltpu.VMEM)
ANY = pl.BlockSpec(memory_space=pl.ANY)
PARAMS = pltpu.CompilerParams(vmem_limit_bytes=16 * 1024 * 1024)


def dot(x, y, dims):
    return lax.dot_general(x, y, dims, preferred_element_type=F32)


def ring_away(owner, here):
    step = (lax.shift_right_logical(owner, 1) + X - lax.shift_right_logical(here, 1)) & (X - 1)
    return step * CORE + ((owner ^ here) & 1)


def plan_kernel(sn, here_ref, col_ref, row_ref, plan_ref, note_ref, count_ref, note):
    note[...] = jnp.zeros_like(note)
    for o in range(OWNERS):
        count_ref[o] = 0
    for i in range(CAP):
        plan_ref[5, i] = -1
    for t in range(col_ref.shape[0]):
        c = col_ref[t]
        level, owner, inner = c // (sn * OWNERS), (c // sn) % OWNERS, c % sn
        rank = count_ref[owner]
        count_ref[owner] = rank + 1
        away = ring_away(owner, here_ref[0])
        plan_ref[0, t] = away
        plan_ref[1, t] = level * sn + inner
        plan_ref[2, t] = row_ref[t]
        plan_ref[3, t] = away
        plan_ref[4, t] = rank

        @pl.when(away == LAST)
        def _():
            plan_ref[5, rank] = t

        mark = (level * sn + inner + 1).astype(F32)
        note[away, pl.ds(rank, 1), :] = jnp.full((1, note.shape[2]), mark, F32)
    note_ref[...] = note[...].astype(BF16)


def first_tiles_kernel(n_blocks, core_ref, plan_ref, side_ref, a_ref, *refs):
    blocks = refs[:n_blocks]
    core = core_ref[0]
    res_ref, x_all, sems = refs[n_blocks:]
    mine = x_all.shape[0] // OWNERS
    own, rest = 2 * X - 2 - 4 * core, 2 + 4 * core
    places = [0, 1, 4, own, own + 1, rest, rest + 1]
    copies = [pltpu.make_async_copy(side_ref, res_ref, sems.at[n_blocks])]
    for i, block in enumerate(blocks):
        copies.append(pltpu.make_async_copy(block, x_all.at[pl.ds(places[i] * mine, mine)], sems.at[i]))
    for copy in copies:
        copy.start()
    x_all[LAST * mine : (LAST + 1) * mine] = jnp.zeros((mine,) + x_all.shape[1:], BF16)
    for copy in copies:
        copy.wait()
    for t in range(a_ref.shape[0]):
        q = plan_ref[2, t]
        res_ref[q] -= dot(x_all[plan_ref[0, t] * mine + plan_ref[1, t]], a_ref[t], NT)


def last_tiles_kernel(plan_ref, note_ref, sum_ref, a_ref, block_ref, res_hbm, own_ref, *refs):
    out_refs, (send_ref, x_last, res_ref, low_ref, sems, note_sems) = refs[: OWNERS - 1], refs[OWNERS - 1 :]
    half = x_last.shape[1] // 2
    per = own_ref.shape[0]
    copies = [pltpu.make_async_copy(block_ref, x_last, sems.at[0])]
    copies[0].start()
    send_ref[...] = jnp.zeros_like(send_ref)
    for o in range(OWNERS):
        copies.append(pltpu.make_async_copy(note_ref.at[o], send_ref.at[(o + 1) * per - 1], note_sems.at[o]))
        copies[-1].start()
    res_ref[...] = sum_ref[...]
    for copy in copies:
        copy.wait()
    for i in range(CAP):
        t = jnp.maximum(plan_ref[5, i], 0)
        there = (plan_ref[5, i] >= 0).astype(F32)
        q = plan_ref[2, t]
        res_ref[q] -= there * dot(x_last[plan_ref[1, t]], a_ref[t], NT)
    copies = [pltpu.make_async_copy(res_ref, res_hbm, sems.at[0])]
    copies[0].start()
    low_ref[...] = res_ref[...].astype(BF16)
    for t in range(a_ref.shape[0]):
        spot = plan_ref[3, t] * per + 2 * plan_ref[4, t]
        term = dot(low_ref[plan_ref[2, t]], a_ref[t], NN).astype(BF16)
        send_ref[spot] = term[:half]
        send_ref[spot + 1] = term[half:]
    for i, ref in enumerate(out_refs):
        piece = send_ref.at[pl.ds((i + 1) * per, per)]
        copies.append(pltpu.make_async_copy(piece, ref, sems.at[i + 1]))
        copies[-1].start()
    own_ref[...] = send_ref[:per]
    for copy in copies:
        copy.wait()


def in_hbm(x):
    return pltpu.with_memory_space_constraint(x, pltpu.HBM)


def in_vmem(x):
    return pltpu.with_memory_space_constraint(x, pltpu.VMEM)


def near_kernel(n, parts, *refs):
    sems = refs[-1]
    outs = refs[-1 - n : -1]
    copies = []
    for i in range(n):
        size = refs[i].shape[0] // parts[i]
        for k in range(parts[i]):
            piece = pl.ds(k * size, size)
            copies.append(pltpu.make_async_copy(refs[i].at[piece], outs[i].at[piece], sems.at[len(copies)]))
    for copy in copies:
        copy.start()
    for copy in copies:
        copy.wait()


def bring_near(after, *operands):
    n = len(operands)
    parts = tuple(4 if x.shape[0] % 4 == 0 else x.shape[0] for x in operands)
    operands = [in_hbm(x) for x in operands]
    if after is not None:
        operands.append(after)
    out_shape = [jax.ShapeDtypeStruct(x.shape, x.dtype) for x in operands]
    return pl.pallas_call(
        functools.partial(near_kernel, n, parts),
        out_shape=tuple(out_shape[:n]),
        in_specs=[ANY] * len(operands),
        out_specs=(VMEM,) * n,
        scratch_shapes=[pltpu.SemaphoreType.DMA((sum(parts),))],
        compiler_params=PARAMS,
        name="bring_near",
    )(*operands)


def pick_kernel(mine, y_ref, *refs):
    recvs, outs, (data, pick) = refs[:OWNERS], refs[OWNERS:-2], refs[-2:]
    blocks, size, T = recvs[0].shape
    rows = (blocks - 1) * size
    K = rows // CAP
    lane = lax.broadcasted_iota(jnp.int32, (1, 128), 1)
    marks, codes = [], []
    for i, ref in enumerate(recvs):
        data[i * rows : (i + 1) * rows, :] = ref[: blocks - 1].reshape(rows, T)
        note = ref[blocks - 1].astype(F32)
        marks += [note[j : j + 1, :128] for j in range(CAP)]
    per = 128 // K
    column = (lane % K).astype(F32)
    for i in range(0, len(marks), per):
        mark = marks[i]
        for j in range(1, per):
            mark = jnp.where(lane // K == j, marks[i + j], mark)
        codes.append((mark - 1.0) * K + column)
    code = jnp.concatenate(codes, axis=1)
    for step, out in enumerate(outs):
        at = lax.broadcasted_iota(jnp.int32, (Z * mine, 1), 0)
        k = at // mine * Y + (y_ref[0] + step) % Y
        wanted = ((at % mine) * K + k).astype(F32)
        pick[...] = jnp.where(wanted == code, 1.0, 0.0).astype(BF16)
        out[...] = dot(pick[...], data[...], NN).astype(BF16)


def forward_rows(level, sn, g, look_ref, known_refs, c_ref, d_ref):
    if level > 0:
        known = jnp.concatenate([ref[...].astype(F32).reshape(-1, ref.shape[2]) for ref in known_refs], axis=0).astype(BF16)
        found = dot(look_ref[...], known, NN)
    rows = []
    for j in range(sn):
        acc = g[level * sn + j : level * sn + j + 1, :]
        if level > 0:
            n = c_ref.shape[2]
            for i in range(n):
                row = found[j * n + i : j * n + i + 1, :].astype(BF16)
                acc = acc - dot(row, c_ref[0, j, i], NN)
        rows.append(dot(acc.astype(BF16), d_ref[0, j], NN))
    return rows


def backward_rows(level, sn, remaining, c_ref, d_ref, change_ref, stage):
    for j in range(sn):
        change = dot(remaining[j].astype(BF16), d_ref[0, j], NT)
        change_ref[j : j + 1, :] = change
        if level > 0:
            n = c_ref.shape[2]
            low = change.astype(BF16)
            for i in range(n):
                stage[j * n + i : j * n + i + 1, :] = dot(low, c_ref[0, j, i], NT)


def spread(scatter_ref, stage):
    terms = stage[...]
    high = terms.astype(BF16)
    low = (terms - high.astype(F32)).astype(BF16)
    return dot(scatter_ref[...], high, NN) + dot(scatter_ref[...], low, NN)


def store_pend(pend, out_ref, rest_refs):
    n, rows, width = out_ref.shape
    base = pend.shape[0] - n * rows
    out_ref[...] = pend[base:, :].reshape(n, rows, width).astype(out_ref.dtype)
    for ref in rest_refs:
        ref[...] = pend[:base, :]


def spread_rows(rows, own_ref, out_ref):
    for j, row in enumerate(rows):
        own_ref[j : j + 1, :] = row
    filler = jnp.zeros((out_ref.shape[1] - len(rows), out_ref.shape[2]), F32)
    block = jnp.concatenate(rows + [filler], axis=0).astype(out_ref.dtype)
    for o in range(out_ref.shape[0]):
        out_ref[o] = block


def first_kernel(sn, parts_ref, d_ref, g_ref, own_ref, out_ref):
    total = parts_ref[0].astype(F32)
    for i in range(1, parts_ref.shape[0]):
        total = total + parts_ref[i].astype(F32)
    g_ref[...] = total
    spread_rows(forward_rows(0, sn, total, None, [], None, d_ref), own_ref, out_ref)


def forward_kernel(level, sn, g_ref, look_ref, *refs):
    known_refs, (c_ref, d_ref, own_ref, out_ref) = refs[:level], refs[level:]
    rows = forward_rows(level, sn, g_ref[...], look_ref, known_refs, c_ref, d_ref)
    spread_rows(rows, own_ref, out_ref)


def turn_kernel(level, sn, g_ref, look_ref, scatter_ref, *refs):
    known_refs, refs = refs[:level], refs[level:]
    c_ref, d_ref, change_ref, out_ref, rest_ref, stage = refs
    rows = forward_rows(level, sn, g_ref[...], look_ref, known_refs, c_ref, d_ref)
    stage[...] = jnp.zeros_like(stage)
    backward_rows(level, sn, rows, c_ref, d_ref, change_ref, stage)
    store_pend(spread(scatter_ref, stage), out_ref, [rest_ref])


def remaining_rows(sn, solved_ref, recv_ref):
    got = recv_ref[0].astype(F32)
    for i in range(1, recv_ref.shape[0]):
        got = got + recv_ref[i].astype(F32)
    return [solved_ref[j : j + 1, :] - got[j : j + 1, :] for j in range(sn)]


def backward_kernel(level, sn, solved_ref, recv_ref, pend_ref, scatter_ref, c_ref, d_ref, *refs):
    change_ref, out_ref, rest_refs, stage = refs[0], refs[1], refs[2:-1], refs[-1]
    stage[...] = jnp.zeros_like(stage)
    backward_rows(level, sn, remaining_rows(sn, solved_ref, recv_ref), c_ref, d_ref, change_ref, stage)
    store_pend(pend_ref[...] + spread(scatter_ref, stage), out_ref, rest_refs)


def last_kernel(sn, solved_ref, recv_ref, c3_ref, c2_ref, c1_ref, d_ref, out_ref, change):
    backward_rows(0, sn, remaining_rows(sn, solved_ref, recv_ref), None, d_ref, change, None)
    mine = jnp.concatenate([change[...], c1_ref[...], c2_ref[...], c3_ref[...]], axis=0).astype(BF16)
    for i in range(out_ref.shape[0]):
        out_ref[i] = mine


def shift(size, step):
    return [(i, (i + step) % size) for i in range(size)]


def local(a_tiles, tile_row, tile_col, right_side, estimate, diag_inverse, coupling, coupling_source):
    tiles, T = a_tiles.shape[0], a_tiles.shape[1]
    row_tiles, K = right_side.shape[0], right_side.shape[1]
    levels, sn = estimate.shape[0], estimate.shape[1]
    snode = ("x", "core")
    width = sn * OWNERS
    mine = levels * sn
    me = lax.axis_index("x") * CORE + lax.axis_index("core")
    here = me.reshape(1)

    e = estimate.astype(BF16).reshape(mine, K, T)
    other = functools.partial(lax.ppermute, axis_name="core", perm=shift(CORE, 1))

    def along(block):
        perm = []
        for x in range(X):
            perm.append((x * CORE, (x + 1) % X * CORE))
            perm.append((x * CORE + 1, (x - 1) % X * CORE + 1))
        return lax.ppermute(block, snode, perm)

    first = along(e)
    swapped = other(e)
    swapped, here = lax.optimization_barrier((swapped, here))
    second = along(swapped)
    plan, note = pl.pallas_call(
        functools.partial(plan_kernel, sn),
        out_shape=(
            jax.ShapeDtypeStruct((6, tiles), jnp.int32),
            pltpu.HBM((OWNERS, 16, T), BF16),
        ),
        in_specs=[SMEM, SMEM, SMEM],
        out_specs=(SMEM, VMEM),
        scratch_shapes=[pltpu.SMEM((OWNERS,), jnp.int32), pltpu.VMEM((OWNERS, 16, T), F32)],
        compiler_params=PARAMS,
        name="plan",
    )(here, in_hbm(tile_col), in_hbm(tile_row))
    third = along(first)
    cross_first = other(first)
    (a_near,) = bring_near(None, a_tiles)
    side = in_hbm(right_side)
    second, note, a_near = lax.optimization_barrier((second, note, a_near))
    cross_second, cross_third = other(second), other(third)
    blocks = [e, swapped, third, first, second, cross_second, cross_first]

    slot_rows = CAP * K + 16
    part_sum = pl.pallas_call(
        functools.partial(first_tiles_kernel, len(blocks)),
        out_shape=jax.ShapeDtypeStruct((row_tiles, K, T), F32),
        in_specs=[SMEM, SMEM, ANY, VMEM] + [ANY] * len(blocks),
        out_specs=VMEM,
        scratch_shapes=[pltpu.VMEM((OWNERS * mine, K, T), BF16), pltpu.SemaphoreType.DMA((len(blocks) + 1,))],
        compiler_params=PARAMS,
        name="first_tiles",
    )(lax.axis_index("core").reshape(1), plan, side, a_near, *blocks)
    slots = slot_rows // 16
    residual, *send = pl.pallas_call(
        last_tiles_kernel,
        out_shape=(
            jax.ShapeDtypeStruct((row_tiles, K, T), F32),
            jax.ShapeDtypeStruct((slots, 16, T), BF16),
        )
        + (pltpu.HBM((slots, 16, T), BF16),) * (OWNERS - 1),
        in_specs=[SMEM, ANY, VMEM, VMEM, ANY],
        out_specs=(ANY, VMEM) + (ANY,) * (OWNERS - 1),
        scratch_shapes=[
            pltpu.VMEM((OWNERS * slots, 16, T), BF16),
            pltpu.VMEM((mine, K, T), BF16),
            pltpu.VMEM((row_tiles, K, T), F32),
            pltpu.VMEM((row_tiles, K, T), BF16),
            pltpu.SemaphoreType.DMA((OWNERS,)),
            pltpu.SemaphoreType.DMA((OWNERS,)),
        ],
        compiler_params=PARAMS,
        name="last_tiles",
    )(plan, in_hbm(note), part_sum, a_near, cross_third)

    to = jnp.arange(mine * K)
    y = lax.axis_index("y")
    place = jnp.arange(Y * Z * mine)
    column_k = (place // mine) % Z * Y + (place // (mine * Z) + y) % Y
    place = (place % mine) * K + column_k
    first_send, coupling_source = lax.optimization_barrier((send[0], coupling_source))
    source = coupling_source.reshape(levels - 1, -1)
    block_rows = 8
    owner = source // sn % OWNERS
    block = source // width * OWNERS + owner % CORE * X + owner // CORE
    spot_at = block * block_rows + source % sn
    n_terms = source.shape[1]
    pad_terms = -n_terms % 16
    spot_at = jnp.pad(spot_at, ((0, 0), (0, pad_terms)), constant_values=-1)
    look, scatter = [], []
    for level in range(1, levels):
        spots = jnp.arange(level * OWNERS * block_rows)
        look.append((spot_at[level - 1][:, None] == spots[None, :]).astype(BF16))
        scatter.append((spots[:, None] == spot_at[level - 1][None, :]).astype(BF16))
    stage = pltpu.VMEM((n_terms + pad_terms, T), F32)

    recv = [first_send]
    for away in (4, 5, 6, 7, 3, 2, 1):
        step, swap = away // CORE, away % CORE
        perm = []
        for x in range(X):
            for c in range(CORE):
                perm.append((x * CORE + c, (x + step) % X * CORE + (c + swap) % CORE))
        recv.append(lax.ppermute(send[away], snode, perm))
    recv, look, scatter, to, place = lax.optimization_barrier((recv, look, scatter, to, place))
    part = pl.pallas_call(
        functools.partial(pick_kernel, mine),
        out_shape=(jax.ShapeDtypeStruct((Z * mine, T), BF16),) * Y,
        in_specs=[SMEM] + [VMEM] * OWNERS,
        out_specs=(VMEM,) * Y,
        scratch_shapes=[
            pltpu.VMEM((OWNERS * CAP * K, T), BF16),
            pltpu.VMEM((Z * mine, OWNERS * CAP * K), BF16),
        ],
        compiler_params=PARAMS,
        name="pick",
    )(y.reshape(1), *recv)
    total = part[0].astype(F32)
    arrived = [lax.ppermute(part[s], "y", shift(Y, s)) for s in (2, 1, 3)]
    (c_near,) = bring_near(part[0], coupling)
    arrived, c_near = lax.optimization_barrier((arrived, c_near))
    for block in arrived:
        total = total + block.astype(F32)
    parts = lax.all_to_all(total.astype(BF16).reshape(Z, mine, T), "z", 0, 0, tiled=True)

    def d_spec(level):
        return pl.BlockSpec((1, sn, T, T), lambda i: (level, 0, 0, 0))

    def c_spec(level):
        return pl.BlockSpec((1, sn, coupling.shape[2], T, T), lambda i: (level - 1, 0, 0, 0, 0))

    row4 = jax.ShapeDtypeStruct((sn, T), F32)
    by_owner = jax.ShapeDtypeStruct((OWNERS, block_rows, T), BF16)

    def rest_of(level):
        return (jax.ShapeDtypeStruct(((level - 1) * OWNERS * block_rows, T), F32),) if level > 1 else ()

    g, value, out = pl.pallas_call(
        functools.partial(first_kernel, sn),
        grid=(1,),
        out_shape=(jax.ShapeDtypeStruct((mine, T), F32), row4, by_owner),
        in_specs=[VMEM, d_spec(0)],
        out_specs=(VMEM, VMEM, VMEM),
        compiler_params=PARAMS,
        name="forward_0",
    )(parts, diag_inverse)
    known, solved = [], [value]
    for level in range(1, levels):
        known.append(lax.all_to_all(out, ("core", "x"), 0, 0, tiled=True))
        if level < levels - 1:
            value, out = pl.pallas_call(
                functools.partial(forward_kernel, level, sn),
                grid=(1,),
                out_shape=(row4, by_owner),
                in_specs=[VMEM] * (2 + level) + [c_spec(level), d_spec(level)],
                out_specs=(VMEM, VMEM),
                compiler_params=PARAMS,
                name=f"forward_{level}",
            )(g, look[level - 1], *known, c_near, diag_inverse)
            solved.append(value)
        else:
            out_shape = (row4, by_owner) + rest_of(level)
            change, out, *rest = pl.pallas_call(
                functools.partial(turn_kernel, level, sn),
                grid=(1,),
                out_shape=out_shape,
                in_specs=[VMEM] * (3 + level) + [c_spec(level), d_spec(level)],
                out_specs=(VMEM,) * len(out_shape),
                scratch_shapes=[stage],
                compiler_params=PARAMS,
                name="turn",
            )(g, look[level - 1], scatter[level - 1], *known, c_near, diag_inverse)
    changes = [change]
    for level in reversed(range(levels - 1)):
        arrived = lax.all_to_all(out, ("core", "x"), 0, 0, tiled=True)
        if level > 0:
            out_shape = (row4, by_owner) + rest_of(level)
            change, out, *rest = pl.pallas_call(
                functools.partial(backward_kernel, level, sn),
                grid=(1,),
                out_shape=out_shape,
                in_specs=[VMEM] * 4 + [c_spec(level), d_spec(level)],
                out_specs=(VMEM,) * len(out_shape),
                scratch_shapes=[stage],
                compiler_params=PARAMS,
                name=f"backward_{level}",
            )(solved[level], arrived, rest[0], scatter[level - 1], c_near, diag_inverse)
            changes.append(change)
        else:
            change = pl.pallas_call(
                functools.partial(last_kernel, sn),
                grid=(1,),
                out_shape=jax.ShapeDtypeStruct((Z, mine, T), BF16),
                in_specs=[VMEM] * 5 + [d_spec(0)],
                out_specs=VMEM,
                scratch_shapes=[pltpu.VMEM((sn, T), F32)],
                compiler_params=PARAMS,
                name="backward_0",
            )(solved[0], arrived, *changes, diag_inverse)
    column = lax.all_to_all(change, "z", 0, 0, tiled=True)
    behind, ahead, far = [lax.ppermute(column, "y", shift(Y, -s % Y)) for s in (3, 1, 2)]
    pieces = [column, ahead, far, behind]
    pieces = jnp.concatenate(pieces, axis=0).reshape(Y * Z * mine, T)
    sort = (to[:, None] == place[None, :]).astype(BF16)
    change = jnp.dot(sort, pieces, preferred_element_type=F32)
    new_estimate = estimate + change.reshape(estimate.shape)
    return new_estimate, residual


def solution(mesh):
    grid = jax.sharding.Mesh(mesh.devices.reshape(Z, Y, X, CORE), ("z", "y", "x", "core"))
    every, snode = ("z", "y", "x", "core"), ("x", "core")
    in_specs = (
        P(every, None, None),
        P(every),
        P(every),
        P(every, None, None),
        P(None, snode, None, None),
        P(None, snode, None, None),
        P(None, snode, None, None, None),
        P(None, snode, None),
    )
    out_specs = (P(None, snode, None, None), P(every, None, None))
    return jax.shard_map(local, mesh=grid, in_specs=in_specs, out_specs=out_specs, check_vma=False)
```

```python
import functools

import jax
import jax.numpy as jnp
from jax import lax
from jax.experimental import pallas as pl
from jax.experimental.pallas import tpu as pltpu
from jax.sharding import PartitionSpec as P

CAP = 6
X, CORE, Y, Z = 4, 2, 4, 8
OWNERS = X * CORE
LAST = 2 * CORE + 1
F32 = jnp.float32
BF16 = jnp.bfloat16
NT = (((1,), (1,)), ((), ()))
NN = (((1,), (0,)), ((), ()))
SMEM = pl.BlockSpec(memory_space=pltpu.SMEM)
VMEM = pl.BlockSpec(memory_space=pltpu.VMEM)
ANY = pl.BlockSpec(memory_space=pl.ANY)
PARAMS = pltpu.CompilerParams(vmem_limit_bytes=16 * 1024 * 1024)


def dot(x, y, dims):
    return lax.dot_general(x, y, dims, preferred_element_type=F32)


def ring_away(owner, here):
    step = (lax.shift_right_logical(owner, 1) + X - lax.shift_right_logical(here, 1)) & (X - 1)
    return step * CORE + ((owner ^ here) & 1)


def plan_kernel(sn, here_ref, col_ref, row_ref, plan_ref, note_ref, count_ref, note):
    note[...] = jnp.zeros_like(note)
    for o in range(OWNERS):
        count_ref[o] = 0
    for o in range(OWNERS):
        for i in range(CAP):
            plan_ref[5 + o, i] = -1
    for t in range(col_ref.shape[0]):
        c = col_ref[t]
        level, owner, inner = c // (sn * OWNERS), (c // sn) % OWNERS, c % sn
        rank = count_ref[owner]
        count_ref[owner] = rank + 1
        away = ring_away(owner, here_ref[0])
        plan_ref[0, t] = away
        plan_ref[1, t] = level * sn + inner
        plan_ref[2, t] = row_ref[t]
        plan_ref[3, t] = away
        plan_ref[4, t] = rank
        plan_ref[5 + away, rank] = t
        mark = (level * sn + inner + 1).astype(F32)
        note[away, pl.ds(rank, 1), :] = jnp.full((1, note.shape[2]), mark, F32)
    note_ref[...] = note[...].astype(BF16)


def add_slots(away, first, x_ref, plan_ref, a_ref, res_ref):
    for i in range(CAP):
        t = jnp.maximum(plan_ref[5 + away, i], 0)
        there = (plan_ref[5 + away, i] >= 0).astype(F32)
        res_ref[plan_ref[2, t]] -= there * dot(x_ref[first + plan_ref[1, t]], a_ref[t], NT)


def first_tiles_kernel(core_ref, plan_ref, side_ref, a_ref, own, other, near, near_2, res_ref, x_all, sems):
    mine = x_all.shape[0] // OWNERS
    side = 2 * X - 2 - 4 * core_ref[0]
    copies = [pltpu.make_async_copy(side_ref, res_ref, sems.at[4])]
    copies[0].start()
    x_all[...] = jnp.zeros_like(x_all)
    for i, (block, place) in enumerate(((own, 0), (other, 1), (near, side), (near_2, side + 1))):
        copies.append(pltpu.make_async_copy(block, x_all.at[pl.ds(place * mine, mine)], sems.at[i]))
        copies[-1].start()
    for copy in copies:
        copy.wait()
    for t in range(a_ref.shape[0]):
        q = plan_ref[2, t]
        res_ref[q] -= dot(x_all[plan_ref[0, t] * mine + plan_ref[1, t]], a_ref[t], NT)


def next_tiles_kernel(core_ref, plan_ref, sum_ref, a_ref, far, cross, cross_2, res_ref, x_ref, sems):
    mine = x_ref.shape[0] // 3
    sums = pltpu.make_async_copy(sum_ref, res_ref, sems.at[3])
    sums.start()
    copies = []
    for i, block in enumerate((far, cross, cross_2)):
        copies.append(pltpu.make_async_copy(block, x_ref.at[pl.ds(i * mine, mine)], sems.at[i]))
        copies[-1].start()
    side = 2 + 4 * core_ref[0]
    sums.wait()
    for i, away in enumerate((2 * CORE, side, side + 1)):
        copies[i].wait()
        add_slots(away, i * mine, x_ref, plan_ref, a_ref, res_ref)


def last_tiles_kernel(plan_ref, note_ref, sum_ref, a_ref, block_ref, res_hbm, own_ref, *refs):
    out_refs, (send_ref, x_last, res_ref, low_ref, sems, note_sems) = refs[: OWNERS - 1], refs[OWNERS - 1 :]
    half = x_last.shape[1] // 2
    per = own_ref.shape[0]
    copies = [pltpu.make_async_copy(block_ref, x_last, sems.at[0])]
    copies[0].start()
    send_ref[...] = jnp.zeros_like(send_ref)
    for o in range(OWNERS):
        copies.append(pltpu.make_async_copy(note_ref.at[o], send_ref.at[(o + 1) * per - 1], note_sems.at[o]))
        copies[-1].start()
    res_ref[...] = sum_ref[...]
    for copy in copies:
        copy.wait()
    add_slots(LAST, 0, x_last, plan_ref, a_ref, res_ref)
    copies = [pltpu.make_async_copy(res_ref, res_hbm, sems.at[0])]
    copies[0].start()
    low_ref[...] = res_ref[...].astype(BF16)
    for t in range(a_ref.shape[0]):
        spot = plan_ref[3, t] * per + 2 * plan_ref[4, t]
        term = dot(low_ref[plan_ref[2, t]], a_ref[t], NN).astype(BF16)
        send_ref[spot] = term[:half]
        send_ref[spot + 1] = term[half:]
    for i, ref in enumerate(out_refs):
        piece = send_ref.at[pl.ds((i + 1) * per, per)]
        copies.append(pltpu.make_async_copy(piece, ref, sems.at[i + 1]))
        copies[-1].start()
    own_ref[...] = send_ref[:per]
    for copy in copies:
        copy.wait()


def in_hbm(x):
    return pltpu.with_memory_space_constraint(x, pltpu.HBM)


def in_vmem(x):
    return pltpu.with_memory_space_constraint(x, pltpu.VMEM)


def near_kernel(n, parts, *refs):
    sems = refs[-1]
    outs = refs[-1 - n : -1]
    copies = []
    for i in range(n):
        size = refs[i].shape[0] // parts[i]
        for k in range(parts[i]):
            piece = pl.ds(k * size, size)
            copies.append(pltpu.make_async_copy(refs[i].at[piece], outs[i].at[piece], sems.at[len(copies)]))
    for copy in copies:
        copy.start()
    for copy in copies:
        copy.wait()


def bring_near(after, *operands):
    n = len(operands)
    parts = tuple(4 if x.shape[0] % 4 == 0 else x.shape[0] for x in operands)
    operands = [in_hbm(x) for x in operands]
    if after is not None:
        operands.append(after)
    out_shape = [jax.ShapeDtypeStruct(x.shape, x.dtype) for x in operands]
    return pl.pallas_call(
        functools.partial(near_kernel, n, parts),
        out_shape=tuple(out_shape[:n]),
        in_specs=[ANY] * len(operands),
        out_specs=(VMEM,) * n,
        scratch_shapes=[pltpu.SemaphoreType.DMA((sum(parts),))],
        compiler_params=PARAMS,
        name="bring_near",
    )(*operands)


def pick_kernel(mine, y_ref, *refs):
    recvs, outs, (data, pick) = refs[:OWNERS], refs[OWNERS:-2], refs[-2:]
    blocks, size, T = recvs[0].shape
    rows = (blocks - 1) * size
    K = rows // CAP
    lane = lax.broadcasted_iota(jnp.int32, (1, 128), 1)
    marks, codes = [], []
    for i, ref in enumerate(recvs):
        data[i * rows : (i + 1) * rows, :] = ref[: blocks - 1].reshape(rows, T)
        note = ref[blocks - 1].astype(F32)
        marks += [note[j : j + 1, :128] for j in range(CAP)]
    per = 128 // K
    column = (lane % K).astype(F32)
    for i in range(0, len(marks), per):
        mark = marks[i]
        for j in range(1, per):
            mark = jnp.where(lane // K == j, marks[i + j], mark)
        codes.append((mark - 1.0) * K + column)
    code = jnp.concatenate(codes, axis=1)
    for step, out in enumerate(outs):
        at = lax.broadcasted_iota(jnp.int32, (Z * mine, 1), 0)
        k = at // mine * Y + (y_ref[0] + step) % Y
        wanted = ((at % mine) * K + k).astype(F32)
        pick[...] = jnp.where(wanted == code, 1.0, 0.0).astype(BF16)
        out[...] = dot(pick[...], data[...], NN).astype(BF16)


def forward_rows(level, sn, g, look_ref, known_refs, c_ref, d_ref):
    if level > 0:
        known = jnp.concatenate([ref[...].astype(F32).reshape(-1, ref.shape[2]) for ref in known_refs], axis=0).astype(BF16)
        found = dot(look_ref[...], known, NN)
    rows = []
    for j in range(sn):
        acc = g[level * sn + j : level * sn + j + 1, :]
        if level > 0:
            n = c_ref.shape[2]
            for i in range(n):
                row = found[j * n + i : j * n + i + 1, :].astype(BF16)
                acc = acc - dot(row, c_ref[0, j, i], NN)
        rows.append(dot(acc.astype(BF16), d_ref[0, j], NN))
    return rows


def backward_rows(level, sn, remaining, c_ref, d_ref, change_ref, stage):
    for j in range(sn):
        change = dot(remaining[j].astype(BF16), d_ref[0, j], NT)
        change_ref[j : j + 1, :] = change
        if level > 0:
            n = c_ref.shape[2]
            low = change.astype(BF16)
            for i in range(n):
                stage[j * n + i : j * n + i + 1, :] = dot(low, c_ref[0, j, i], NT)


def spread(scatter_ref, stage):
    terms = stage[...]
    high = terms.astype(BF16)
    low = (terms - high.astype(F32)).astype(BF16)
    return dot(scatter_ref[...], high, NN) + dot(scatter_ref[...], low, NN)


def store_pend(pend, out_ref, rest_refs):
    n, rows, width = out_ref.shape
    base = pend.shape[0] - n * rows
    out_ref[...] = pend[base:, :].reshape(n, rows, width).astype(out_ref.dtype)
    for ref in rest_refs:
        ref[...] = pend[:base, :]


def spread_rows(rows, own_ref, out_ref):
    for j, row in enumerate(rows):
        own_ref[j : j + 1, :] = row
    filler = jnp.zeros((out_ref.shape[1] - len(rows), out_ref.shape[2]), F32)
    block = jnp.concatenate(rows + [filler], axis=0).astype(out_ref.dtype)
    for o in range(out_ref.shape[0]):
        out_ref[o] = block


def first_kernel(sn, parts_ref, d_ref, g_ref, own_ref, out_ref):
    total = parts_ref[0].astype(F32)
    for i in range(1, parts_ref.shape[0]):
        total = total + parts_ref[i].astype(F32)
    g_ref[...] = total
    spread_rows(forward_rows(0, sn, total, None, [], None, d_ref), own_ref, out_ref)


def forward_kernel(level, sn, g_ref, look_ref, *refs):
    known_refs, (c_ref, d_ref, own_ref, out_ref) = refs[:level], refs[level:]
    rows = forward_rows(level, sn, g_ref[...], look_ref, known_refs, c_ref, d_ref)
    spread_rows(rows, own_ref, out_ref)


def turn_kernel(level, sn, g_ref, look_ref, scatter_ref, *refs):
    known_refs, refs = refs[:level], refs[level:]
    c_ref, d_ref, change_ref, out_ref, rest_ref, stage = refs
    rows = forward_rows(level, sn, g_ref[...], look_ref, known_refs, c_ref, d_ref)
    stage[...] = jnp.zeros_like(stage)
    backward_rows(level, sn, rows, c_ref, d_ref, change_ref, stage)
    store_pend(spread(scatter_ref, stage), out_ref, [rest_ref])


def remaining_rows(sn, solved_ref, recv_ref):
    got = recv_ref[0].astype(F32)
    for i in range(1, recv_ref.shape[0]):
        got = got + recv_ref[i].astype(F32)
    return [solved_ref[j : j + 1, :] - got[j : j + 1, :] for j in range(sn)]


def backward_kernel(level, sn, solved_ref, recv_ref, pend_ref, scatter_ref, c_ref, d_ref, *refs):
    change_ref, out_ref, rest_refs, stage = refs[0], refs[1], refs[2:-1], refs[-1]
    stage[...] = jnp.zeros_like(stage)
    backward_rows(level, sn, remaining_rows(sn, solved_ref, recv_ref), c_ref, d_ref, change_ref, stage)
    store_pend(pend_ref[...] + spread(scatter_ref, stage), out_ref, rest_refs)


def last_kernel(sn, solved_ref, recv_ref, c3_ref, c2_ref, c1_ref, d_ref, out_ref, change):
    backward_rows(0, sn, remaining_rows(sn, solved_ref, recv_ref), None, d_ref, change, None)
    mine = jnp.concatenate([change[...], c1_ref[...], c2_ref[...], c3_ref[...]], axis=0).astype(BF16)
    for i in range(out_ref.shape[0]):
        out_ref[i] = mine


def shift(size, step):
    return [(i, (i + step) % size) for i in range(size)]


def local(a_tiles, tile_row, tile_col, right_side, estimate, diag_inverse, coupling, coupling_source):
    tiles, T = a_tiles.shape[0], a_tiles.shape[1]
    row_tiles, K = right_side.shape[0], right_side.shape[1]
    levels, sn = estimate.shape[0], estimate.shape[1]
    snode = ("x", "core")
    width = sn * OWNERS
    mine = levels * sn
    me = lax.axis_index("x") * CORE + lax.axis_index("core")
    here = me.reshape(1)

    e = estimate.astype(BF16).reshape(mine, K, T)
    other = functools.partial(lax.ppermute, axis_name="core", perm=shift(CORE, 1))

    def along(block):
        perm = []
        for x in range(X):
            perm.append((x * CORE, (x + 1) % X * CORE))
            perm.append((x * CORE + 1, (x - 1) % X * CORE + 1))
        return lax.ppermute(block, snode, perm)

    first = along(e)
    swapped = other(e)
    swapped, here = lax.optimization_barrier((swapped, here))
    second = along(swapped)
    plan, note = pl.pallas_call(
        functools.partial(plan_kernel, sn),
        out_shape=(
            jax.ShapeDtypeStruct((5 + OWNERS, tiles), jnp.int32),
            pltpu.HBM((OWNERS, 16, T), BF16),
        ),
        in_specs=[SMEM, SMEM, SMEM],
        out_specs=(SMEM, VMEM),
        scratch_shapes=[pltpu.SMEM((OWNERS,), jnp.int32), pltpu.VMEM((OWNERS, 16, T), F32)],
        compiler_params=PARAMS,
        name="plan",
    )(here, in_hbm(tile_col), in_hbm(tile_row))
    (a_near,) = bring_near(swapped, a_tiles)
    first, note, a_near = lax.optimization_barrier((first, note, a_near))
    third = along(first)
    cross_first, cross_second = other(first), other(second)
    side = in_hbm(right_side)

    slot_rows = CAP * K + 16
    core = lax.axis_index("core").reshape(1)
    part_sum = pl.pallas_call(
        first_tiles_kernel,
        out_shape=pltpu.HBM((row_tiles, K, T), F32),
        in_specs=[SMEM, SMEM, ANY, VMEM] + [ANY] * 4,
        out_specs=VMEM,
        scratch_shapes=[pltpu.VMEM((OWNERS * mine, K, T), BF16), pltpu.SemaphoreType.DMA((5,))],
        compiler_params=PARAMS,
        name="first_tiles",
    )(core, plan, side, a_near, e, swapped, first, second)
    third, part_sum = lax.optimization_barrier((third, part_sum))
    cross_third = other(third)
    part_sum = pl.pallas_call(
        next_tiles_kernel,
        out_shape=jax.ShapeDtypeStruct((row_tiles, K, T), F32),
        in_specs=[SMEM, SMEM, ANY, VMEM] + [ANY] * 3,
        out_specs=VMEM,
        scratch_shapes=[pltpu.VMEM((3 * mine, K, T), BF16), pltpu.SemaphoreType.DMA((4,))],
        compiler_params=PARAMS,
        name="next_tiles",
    )(core, plan, in_hbm(part_sum), a_near, third, cross_second, cross_first)
    slots = slot_rows // 16
    residual, *send = pl.pallas_call(
        last_tiles_kernel,
        out_shape=(
            jax.ShapeDtypeStruct((row_tiles, K, T), F32),
            jax.ShapeDtypeStruct((slots, 16, T), BF16),
        )
        + (pltpu.HBM((slots, 16, T), BF16),) * (OWNERS - 1),
        in_specs=[SMEM, ANY, VMEM, VMEM, ANY],
        out_specs=(ANY, VMEM) + (ANY,) * (OWNERS - 1),
        scratch_shapes=[
            pltpu.VMEM((OWNERS * slots, 16, T), BF16),
            pltpu.VMEM((mine, K, T), BF16),
            pltpu.VMEM((row_tiles, K, T), F32),
            pltpu.VMEM((row_tiles, K, T), BF16),
            pltpu.SemaphoreType.DMA((OWNERS,)),
            pltpu.SemaphoreType.DMA((OWNERS,)),
        ],
        compiler_params=PARAMS,
        name="last_tiles",
    )(plan, in_hbm(note), part_sum, a_near, cross_third)

    to = jnp.arange(mine * K)
    y = lax.axis_index("y")
    place = jnp.arange(Y * Z * mine)
    column_k = (place // mine) % Z * Y + (place // (mine * Z) + y) % Y
    place = (place % mine) * K + column_k
    first_send, coupling_source = lax.optimization_barrier((send[0], coupling_source))
    source = coupling_source.reshape(levels - 1, -1)
    block_rows = 8
    owner = source // sn % OWNERS
    block = source // width * OWNERS + owner % CORE * X + owner // CORE
    spot_at = block * block_rows + source % sn
    n_terms = source.shape[1]
    pad_terms = -n_terms % 16
    spot_at = jnp.pad(spot_at, ((0, 0), (0, pad_terms)), constant_values=-1)
    look, scatter = [], []
    for level in range(1, levels):
        spots = jnp.arange(level * OWNERS * block_rows)
        look.append((spot_at[level - 1][:, None] == spots[None, :]).astype(BF16))
        scatter.append((spots[:, None] == spot_at[level - 1][None, :]).astype(BF16))
    stage = pltpu.VMEM((n_terms + pad_terms, T), F32)

    recv = [first_send]
    for away in (4, 5, 6, 7, 3, 2, 1):
        step, swap = away // CORE, away % CORE
        perm = []
        for x in range(X):
            for c in range(CORE):
                perm.append((x * CORE + c, (x + step) % X * CORE + (c + swap) % CORE))
        recv.append(lax.ppermute(send[away], snode, perm))
    recv, look, scatter, to, place = lax.optimization_barrier((recv, look, scatter, to, place))
    part = pl.pallas_call(
        functools.partial(pick_kernel, mine),
        out_shape=(jax.ShapeDtypeStruct((Z * mine, T), BF16),) * Y,
        in_specs=[SMEM] + [VMEM] * OWNERS,
        out_specs=(VMEM,) * Y,
        scratch_shapes=[
            pltpu.VMEM((OWNERS * CAP * K, T), BF16),
            pltpu.VMEM((Z * mine, OWNERS * CAP * K), BF16),
        ],
        compiler_params=PARAMS,
        name="pick",
    )(y.reshape(1), *recv)
    total = part[0].astype(F32)
    arrived = [lax.ppermute(part[s], "y", shift(Y, s)) for s in (2, 1, 3)]
    (c_near,) = bring_near(part[0], coupling)
    arrived, c_near = lax.optimization_barrier((arrived, c_near))
    for block in arrived:
        total = total + block.astype(F32)
    parts = lax.all_to_all(total.astype(BF16).reshape(Z, mine, T), "z", 0, 0, tiled=True)

    def d_spec(level):
        return pl.BlockSpec((1, sn, T, T), lambda i: (level, 0, 0, 0))

    def c_spec(level):
        return pl.BlockSpec((1, sn, coupling.shape[2], T, T), lambda i: (level - 1, 0, 0, 0, 0))

    row4 = jax.ShapeDtypeStruct((sn, T), F32)
    by_owner = jax.ShapeDtypeStruct((OWNERS, block_rows, T), BF16)

    def rest_of(level):
        return (jax.ShapeDtypeStruct(((level - 1) * OWNERS * block_rows, T), F32),) if level > 1 else ()

    g, value, out = pl.pallas_call(
        functools.partial(first_kernel, sn),
        grid=(1,),
        out_shape=(jax.ShapeDtypeStruct((mine, T), F32), row4, by_owner),
        in_specs=[VMEM, d_spec(0)],
        out_specs=(VMEM, VMEM, VMEM),
        compiler_params=PARAMS,
        name="forward_0",
    )(parts, diag_inverse)
    known, solved = [], [value]
    for level in range(1, levels):
        known.append(lax.all_to_all(out, ("core", "x"), 0, 0, tiled=True))
        if level < levels - 1:
            value, out = pl.pallas_call(
                functools.partial(forward_kernel, level, sn),
                grid=(1,),
                out_shape=(row4, by_owner),
                in_specs=[VMEM] * (2 + level) + [c_spec(level), d_spec(level)],
                out_specs=(VMEM, VMEM),
                compiler_params=PARAMS,
                name=f"forward_{level}",
            )(g, look[level - 1], *known, c_near, diag_inverse)
            solved.append(value)
        else:
            out_shape = (row4, by_owner) + rest_of(level)
            change, out, *rest = pl.pallas_call(
                functools.partial(turn_kernel, level, sn),
                grid=(1,),
                out_shape=out_shape,
                in_specs=[VMEM] * (3 + level) + [c_spec(level), d_spec(level)],
                out_specs=(VMEM,) * len(out_shape),
                scratch_shapes=[stage],
                compiler_params=PARAMS,
                name="turn",
            )(g, look[level - 1], scatter[level - 1], *known, c_near, diag_inverse)
    changes = [change]
    for level in reversed(range(levels - 1)):
        arrived = lax.all_to_all(out, ("core", "x"), 0, 0, tiled=True)
        if level > 0:
            out_shape = (row4, by_owner) + rest_of(level)
            change, out, *rest = pl.pallas_call(
                functools.partial(backward_kernel, level, sn),
                grid=(1,),
                out_shape=out_shape,
                in_specs=[VMEM] * 4 + [c_spec(level), d_spec(level)],
                out_specs=(VMEM,) * len(out_shape),
                scratch_shapes=[stage],
                compiler_params=PARAMS,
                name=f"backward_{level}",
            )(solved[level], arrived, rest[0], scatter[level - 1], c_near, diag_inverse)
            changes.append(change)
        else:
            change = pl.pallas_call(
                functools.partial(last_kernel, sn),
                grid=(1,),
                out_shape=jax.ShapeDtypeStruct((Z, mine, T), BF16),
                in_specs=[VMEM] * 5 + [d_spec(0)],
                out_specs=VMEM,
                scratch_shapes=[pltpu.VMEM((sn, T), F32)],
                compiler_params=PARAMS,
                name="backward_0",
            )(solved[0], arrived, *changes, diag_inverse)
    column = lax.all_to_all(change, "z", 0, 0, tiled=True)
    behind, ahead, far = [lax.ppermute(column, "y", shift(Y, -s % Y)) for s in (3, 1, 2)]
    pieces = [column, ahead, far, behind]
    pieces = jnp.concatenate(pieces, axis=0).reshape(Y * Z * mine, T)
    sort = (to[:, None] == place[None, :]).astype(BF16)
    change = jnp.dot(sort, pieces, preferred_element_type=F32)
    new_estimate = estimate + change.reshape(estimate.shape)
    return new_estimate, residual


def solution(mesh):
    grid = jax.sharding.Mesh(mesh.devices.reshape(Z, Y, X, CORE), ("z", "y", "x", "core"))
    every, snode = ("z", "y", "x", "core"), ("x", "core")
    in_specs = (
        P(every, None, None),
        P(every),
        P(every),
        P(every, None, None),
        P(None, snode, None, None),
        P(None, snode, None, None),
        P(None, snode, None, None, None),
        P(None, snode, None),
    )
    out_specs = (P(None, snode, None, None), P(every, None, None))
    return jax.shard_map(local, mesh=grid, in_specs=in_specs, out_specs=out_specs, check_vma=False)
```

```python
import functools

import jax
import jax.numpy as jnp
from jax import lax
from jax.experimental import pallas as pl
from jax.experimental.pallas import tpu as pltpu
from jax.sharding import PartitionSpec as P

CAP = 6
X, CORE, Y, Z = 4, 2, 4, 8
OWNERS = X * CORE
LAST = 2 * CORE + 1
F32 = jnp.float32
BF16 = jnp.bfloat16
NT = (((1,), (1,)), ((), ()))
NN = (((1,), (0,)), ((), ()))
SMEM = pl.BlockSpec(memory_space=pltpu.SMEM)
VMEM = pl.BlockSpec(memory_space=pltpu.VMEM)
ANY = pl.BlockSpec(memory_space=pl.ANY)
PARAMS = pltpu.CompilerParams(vmem_limit_bytes=16 * 1024 * 1024)


def dot(x, y, dims):
    return lax.dot_general(x, y, dims, preferred_element_type=F32)


def ring_away(owner, here):
    step = (lax.shift_right_logical(owner, 1) + X - lax.shift_right_logical(here, 1)) & (X - 1)
    return step * CORE + ((owner ^ here) & 1)


def plan_kernel(sn, here_ref, col_ref, row_ref, plan_ref, note_ref, count_ref, note):
    note[...] = jnp.zeros_like(note)
    for o in range(OWNERS):
        count_ref[o] = 0
    for o in range(OWNERS):
        for i in range(CAP):
            plan_ref[5 + o, i] = -1
    for t in range(col_ref.shape[0]):
        c = col_ref[t]
        level, owner, inner = c // (sn * OWNERS), (c // sn) % OWNERS, c % sn
        rank = count_ref[owner]
        count_ref[owner] = rank + 1
        away = ring_away(owner, here_ref[0])
        plan_ref[0, t] = away
        plan_ref[1, t] = level * sn + inner
        plan_ref[2, t] = row_ref[t]
        plan_ref[3, t] = away
        plan_ref[4, t] = rank
        plan_ref[5 + away, rank] = t
        mark = (level * sn + inner + 1).astype(F32)
        note[away, pl.ds(rank, 1), :] = jnp.full((1, note.shape[2]), mark, F32)
    note_ref[...] = note[...].astype(BF16)


def add_slots(away, first, x_ref, plan_ref, a_ref, res_ref):
    for i in range(CAP):
        t = jnp.maximum(plan_ref[5 + away, i], 0)
        there = (plan_ref[5 + away, i] >= 0).astype(F32)
        res_ref[plan_ref[2, t]] -= there * dot(x_ref[first + plan_ref[1, t]], a_ref[t], NT)


def tiles_kernel(aways, core_ref, plan_ref, sum_ref, a_ref, *refs):
    blocks, (res_ref, x_ref, sems) = refs[: len(aways)], refs[len(aways) :]
    mine = x_ref.shape[0] // len(aways)
    sums = pltpu.make_async_copy(sum_ref, res_ref, sems.at[len(aways)])
    sums.start()
    copies = []
    for i, block in enumerate(blocks):
        copies.append(pltpu.make_async_copy(block, x_ref.at[pl.ds(i * mine, mine)], sems.at[i]))
        copies[-1].start()
    sums.wait()
    for i, (at, per_core) in enumerate(aways):
        copies[i].wait()
        add_slots(at + per_core * core_ref[0], i * mine, x_ref, plan_ref, a_ref, res_ref)


def last_tiles_kernel(plan_ref, note_ref, sum_ref, a_ref, block_ref, res_hbm, own_ref, *refs):
    out_refs, (send_ref, x_last, res_ref, low_ref, sems, note_sems) = refs[: OWNERS - 1], refs[OWNERS - 1 :]
    half = x_last.shape[1] // 2
    per = own_ref.shape[0]
    copies = [pltpu.make_async_copy(block_ref, x_last, sems.at[0])]
    copies[0].start()
    send_ref[...] = jnp.zeros_like(send_ref)
    for o in range(OWNERS):
        copies.append(pltpu.make_async_copy(note_ref.at[o], send_ref.at[(o + 1) * per - 1], note_sems.at[o]))
        copies[-1].start()
    res_ref[...] = sum_ref[...]
    for copy in copies:
        copy.wait()
    add_slots(LAST, 0, x_last, plan_ref, a_ref, res_ref)
    copies = [pltpu.make_async_copy(res_ref, res_hbm, sems.at[0])]
    copies[0].start()
    low_ref[...] = res_ref[...].astype(BF16)
    for t in range(a_ref.shape[0]):
        spot = plan_ref[3, t] * per + 2 * plan_ref[4, t]
        term = dot(low_ref[plan_ref[2, t]], a_ref[t], NN).astype(BF16)
        send_ref[spot] = term[:half]
        send_ref[spot + 1] = term[half:]
    for i, ref in enumerate(out_refs):
        piece = send_ref.at[pl.ds((i + 1) * per, per)]
        copies.append(pltpu.make_async_copy(piece, ref, sems.at[i + 1]))
        copies[-1].start()
    own_ref[...] = send_ref[:per]
    for copy in copies:
        copy.wait()


def in_hbm(x):
    return pltpu.with_memory_space_constraint(x, pltpu.HBM)


def in_vmem(x):
    return pltpu.with_memory_space_constraint(x, pltpu.VMEM)


def near_kernel(n, parts, *refs):
    sems = refs[-1]
    outs = refs[-1 - n : -1]
    copies = []
    for i in range(n):
        size = refs[i].shape[0] // parts[i]
        for k in range(parts[i]):
            piece = pl.ds(k * size, size)
            copies.append(pltpu.make_async_copy(refs[i].at[piece], outs[i].at[piece], sems.at[len(copies)]))
    for copy in copies:
        copy.start()
    for copy in copies:
        copy.wait()


def bring_near(after, *operands):
    n = len(operands)
    parts = tuple(4 if x.shape[0] % 4 == 0 else x.shape[0] for x in operands)
    operands = [in_hbm(x) for x in operands]
    if after is not None:
        operands.append(after)
    out_shape = [jax.ShapeDtypeStruct(x.shape, x.dtype) for x in operands]
    return pl.pallas_call(
        functools.partial(near_kernel, n, parts),
        out_shape=tuple(out_shape[:n]),
        in_specs=[ANY] * len(operands),
        out_specs=(VMEM,) * n,
        scratch_shapes=[pltpu.SemaphoreType.DMA((sum(parts),))],
        compiler_params=PARAMS,
        name="bring_near",
    )(*operands)


def pick_kernel(mine, y_ref, *refs):
    recvs, outs, (data, pick) = refs[:OWNERS], refs[OWNERS:-2], refs[-2:]
    blocks, size, T = recvs[0].shape
    rows = (blocks - 1) * size
    K = rows // CAP
    lane = lax.broadcasted_iota(jnp.int32, (1, 128), 1)
    marks, codes = [], []
    for i, ref in enumerate(recvs):
        data[i * rows : (i + 1) * rows, :] = ref[: blocks - 1].reshape(rows, T)
        note = ref[blocks - 1].astype(F32)
        marks += [note[j : j + 1, :128] for j in range(CAP)]
    per = 128 // K
    column = (lane % K).astype(F32)
    for i in range(0, len(marks), per):
        mark = marks[i]
        for j in range(1, per):
            mark = jnp.where(lane // K == j, marks[i + j], mark)
        codes.append((mark - 1.0) * K + column)
    code = jnp.concatenate(codes, axis=1)
    for step, out in enumerate(outs):
        at = lax.broadcasted_iota(jnp.int32, (Z * mine, 1), 0)
        k = at // mine * Y + (y_ref[0] + step) % Y
        wanted = ((at % mine) * K + k).astype(F32)
        pick[...] = jnp.where(wanted == code, 1.0, 0.0).astype(BF16)
        out[...] = dot(pick[...], data[...], NN).astype(BF16)


def forward_rows(level, sn, g, look_ref, known_refs, c_ref, d_ref):
    if level > 0:
        known = jnp.concatenate([ref[...].astype(F32).reshape(-1, ref.shape[2]) for ref in known_refs], axis=0).astype(BF16)
        found = dot(look_ref[...], known, NN)
    rows = []
    for j in range(sn):
        acc = g[level * sn + j : level * sn + j + 1, :]
        if level > 0:
            n = c_ref.shape[2]
            for i in range(n):
                row = found[j * n + i : j * n + i + 1, :].astype(BF16)
                acc = acc - dot(row, c_ref[0, j, i], NN)
        rows.append(dot(acc.astype(BF16), d_ref[0, j], NN))
    return rows


def backward_rows(level, sn, remaining, c_ref, d_ref, change_ref, stage):
    for j in range(sn):
        change = dot(remaining[j].astype(BF16), d_ref[0, j], NT)
        change_ref[j : j + 1, :] = change
        if level > 0:
            n = c_ref.shape[2]
            low = change.astype(BF16)
            for i in range(n):
                stage[j * n + i : j * n + i + 1, :] = dot(low, c_ref[0, j, i], NT)


def spread(scatter_ref, stage):
    terms = stage[...]
    high = terms.astype(BF16)
    low = (terms - high.astype(F32)).astype(BF16)
    return dot(scatter_ref[...], high, NN) + dot(scatter_ref[...], low, NN)


def store_pend(pend, out_ref, rest_refs):
    n, rows, width = out_ref.shape
    base = pend.shape[0] - n * rows
    out_ref[...] = pend[base:, :].reshape(n, rows, width).astype(out_ref.dtype)
    for ref in rest_refs:
        ref[...] = pend[:base, :]


def spread_rows(rows, own_ref, out_ref):
    for j, row in enumerate(rows):
        own_ref[j : j + 1, :] = row
    filler = jnp.zeros((out_ref.shape[1] - len(rows), out_ref.shape[2]), F32)
    block = jnp.concatenate(rows + [filler], axis=0).astype(out_ref.dtype)
    for o in range(out_ref.shape[0]):
        out_ref[o] = block


def first_kernel(sn, parts_ref, d_ref, g_ref, own_ref, out_ref):
    total = parts_ref[0].astype(F32)
    for i in range(1, parts_ref.shape[0]):
        total = total + parts_ref[i].astype(F32)
    g_ref[...] = total
    spread_rows(forward_rows(0, sn, total, None, [], None, d_ref), own_ref, out_ref)


def forward_kernel(level, sn, g_ref, look_ref, *refs):
    known_refs, (c_ref, d_ref, own_ref, out_ref) = refs[:level], refs[level:]
    rows = forward_rows(level, sn, g_ref[...], look_ref, known_refs, c_ref, d_ref)
    spread_rows(rows, own_ref, out_ref)


def turn_kernel(level, sn, g_ref, look_ref, scatter_ref, *refs):
    known_refs, refs = refs[:level], refs[level:]
    c_ref, d_ref, change_ref, out_ref, rest_ref, stage = refs
    rows = forward_rows(level, sn, g_ref[...], look_ref, known_refs, c_ref, d_ref)
    stage[...] = jnp.zeros_like(stage)
    backward_rows(level, sn, rows, c_ref, d_ref, change_ref, stage)
    store_pend(spread(scatter_ref, stage), out_ref, [rest_ref])


def remaining_rows(sn, solved_ref, recv_ref):
    got = recv_ref[0].astype(F32)
    for i in range(1, recv_ref.shape[0]):
        got = got + recv_ref[i].astype(F32)
    return [solved_ref[j : j + 1, :] - got[j : j + 1, :] for j in range(sn)]


def backward_kernel(level, sn, solved_ref, recv_ref, pend_ref, scatter_ref, c_ref, d_ref, *refs):
    change_ref, out_ref, rest_refs, stage = refs[0], refs[1], refs[2:-1], refs[-1]
    stage[...] = jnp.zeros_like(stage)
    backward_rows(level, sn, remaining_rows(sn, solved_ref, recv_ref), c_ref, d_ref, change_ref, stage)
    store_pend(pend_ref[...] + spread(scatter_ref, stage), out_ref, rest_refs)


def last_kernel(sn, solved_ref, recv_ref, c3_ref, c2_ref, c1_ref, d_ref, out_ref, change):
    backward_rows(0, sn, remaining_rows(sn, solved_ref, recv_ref), None, d_ref, change, None)
    mine = jnp.concatenate([change[...], c1_ref[...], c2_ref[...], c3_ref[...]], axis=0).astype(BF16)
    for i in range(out_ref.shape[0]):
        out_ref[i] = mine


def shift(size, step):
    return [(i, (i + step) % size) for i in range(size)]


def local(a_tiles, tile_row, tile_col, right_side, estimate, diag_inverse, coupling, coupling_source):
    tiles, T = a_tiles.shape[0], a_tiles.shape[1]
    row_tiles, K = right_side.shape[0], right_side.shape[1]
    levels, sn = estimate.shape[0], estimate.shape[1]
    snode = ("x", "core")
    width = sn * OWNERS
    mine = levels * sn
    me = lax.axis_index("x") * CORE + lax.axis_index("core")
    here = me.reshape(1)

    e = estimate.astype(BF16).reshape(mine, K, T)
    other = functools.partial(lax.ppermute, axis_name="core", perm=shift(CORE, 1))

    def along(block):
        perm = []
        for x in range(X):
            perm.append((x * CORE, (x + 1) % X * CORE))
            perm.append((x * CORE + 1, (x - 1) % X * CORE + 1))
        return lax.ppermute(block, snode, perm)

    first = along(e)
    swapped = other(e)
    swapped, here = lax.optimization_barrier((swapped, here))
    second = along(swapped)
    plan, note = pl.pallas_call(
        functools.partial(plan_kernel, sn),
        out_shape=(
            jax.ShapeDtypeStruct((5 + OWNERS, tiles), jnp.int32),
            pltpu.HBM((OWNERS, 16, T), BF16),
        ),
        in_specs=[SMEM, SMEM, SMEM],
        out_specs=(SMEM, VMEM),
        scratch_shapes=[pltpu.SMEM((OWNERS,), jnp.int32), pltpu.VMEM((OWNERS, 16, T), F32)],
        compiler_params=PARAMS,
        name="plan",
    )(here, in_hbm(tile_col), in_hbm(tile_row))
    (a_near,) = bring_near(swapped, a_tiles)
    first, note, a_near = lax.optimization_barrier((first, note, a_near))
    third = along(first)
    cross_first, cross_second = other(first), other(second)

    slot_rows = CAP * K + 16
    core = lax.axis_index("core").reshape(1)
    def take_off(name, out_kind, aways, so_far, blocks):
        n = len(blocks)
        return pl.pallas_call(
            functools.partial(tiles_kernel, aways),
            out_shape=out_kind((row_tiles, K, T), F32),
            in_specs=[SMEM, SMEM, ANY, VMEM] + [ANY] * n,
            out_specs=VMEM,
            scratch_shapes=[pltpu.VMEM((n * mine, K, T), BF16), pltpu.SemaphoreType.DMA((n + 1,))],
            compiler_params=PARAMS,
            name=name,
        )(core, plan, in_hbm(so_far), a_near, *blocks)

    own, rest = 2 * X - 2, 2
    first_aways = ((0, 0), (1, 0), (own, -4), (own + 1, -4))
    part_sum = take_off("first_tiles", pltpu.HBM, first_aways, right_side, (e, swapped, first, second))
    third, part_sum = lax.optimization_barrier((third, part_sum))
    cross_third = other(third)
    next_aways = ((2 * CORE, 0), (rest, 4), (rest + 1, 4))
    next_blocks = (third, cross_second, cross_first)
    part_sum = take_off("next_tiles", jax.ShapeDtypeStruct, next_aways, part_sum, next_blocks)
    slots = slot_rows // 16
    residual, *send = pl.pallas_call(
        last_tiles_kernel,
        out_shape=(
            jax.ShapeDtypeStruct((row_tiles, K, T), F32),
            jax.ShapeDtypeStruct((slots, 16, T), BF16),
        )
        + (pltpu.HBM((slots, 16, T), BF16),) * (OWNERS - 1),
        in_specs=[SMEM, ANY, VMEM, VMEM, ANY],
        out_specs=(ANY, VMEM) + (ANY,) * (OWNERS - 1),
        scratch_shapes=[
            pltpu.VMEM((OWNERS * slots, 16, T), BF16),
            pltpu.VMEM((mine, K, T), BF16),
            pltpu.VMEM((row_tiles, K, T), F32),
            pltpu.VMEM((row_tiles, K, T), BF16),
            pltpu.SemaphoreType.DMA((OWNERS,)),
            pltpu.SemaphoreType.DMA((OWNERS,)),
        ],
        compiler_params=PARAMS,
        name="last_tiles",
    )(plan, in_hbm(note), part_sum, a_near, cross_third)

    to = jnp.arange(mine * K)
    y = lax.axis_index("y")
    place = jnp.arange(Y * Z * mine)
    column_k = (place // mine) % Z * Y + (place // (mine * Z) + y) % Y
    place = (place % mine) * K + column_k
    first_send, coupling_source = lax.optimization_barrier((send[0], coupling_source))
    source = coupling_source.reshape(levels - 1, -1)
    block_rows = 8
    owner = source // sn % OWNERS
    block = source // width * OWNERS + owner % CORE * X + owner // CORE
    spot_at = block * block_rows + source % sn
    n_terms = source.shape[1]
    pad_terms = -n_terms % 16
    spot_at = jnp.pad(spot_at, ((0, 0), (0, pad_terms)), constant_values=-1)
    look, scatter = [], []
    for level in range(1, levels):
        spots = jnp.arange(level * OWNERS * block_rows)
        look.append((spot_at[level - 1][:, None] == spots[None, :]).astype(BF16))
        scatter.append((spots[:, None] == spot_at[level - 1][None, :]).astype(BF16))
    stage = pltpu.VMEM((n_terms + pad_terms, T), F32)

    recv = [first_send]
    for away in (4, 5, 6, 7, 3, 2, 1):
        step, swap = away // CORE, away % CORE
        perm = []
        for x in range(X):
            for c in range(CORE):
                perm.append((x * CORE + c, (x + step) % X * CORE + (c + swap) % CORE))
        recv.append(lax.ppermute(send[away], snode, perm))
    recv, look, scatter, to, place = lax.optimization_barrier((recv, look, scatter, to, place))
    part = pl.pallas_call(
        functools.partial(pick_kernel, mine),
        out_shape=(jax.ShapeDtypeStruct((Z * mine, T), BF16),) * Y,
        in_specs=[SMEM] + [VMEM] * OWNERS,
        out_specs=(VMEM,) * Y,
        scratch_shapes=[
            pltpu.VMEM((OWNERS * CAP * K, T), BF16),
            pltpu.VMEM((Z * mine, OWNERS * CAP * K), BF16),
        ],
        compiler_params=PARAMS,
        name="pick",
    )(y.reshape(1), *recv)
    total = part[0].astype(F32)
    arrived = [lax.ppermute(part[s], "y", shift(Y, s)) for s in (2, 1, 3)]
    (c_near,) = bring_near(part[0], coupling)
    arrived, c_near = lax.optimization_barrier((arrived, c_near))
    for block in arrived:
        total = total + block.astype(F32)
    parts = lax.all_to_all(total.astype(BF16).reshape(Z, mine, T), "z", 0, 0, tiled=True)

    def d_spec(level):
        return pl.BlockSpec((1, sn, T, T), lambda i: (level, 0, 0, 0))

    def c_spec(level):
        return pl.BlockSpec((1, sn, coupling.shape[2], T, T), lambda i: (level - 1, 0, 0, 0, 0))

    row4 = jax.ShapeDtypeStruct((sn, T), F32)
    by_owner = jax.ShapeDtypeStruct((OWNERS, block_rows, T), BF16)

    def rest_of(level):
        return (jax.ShapeDtypeStruct(((level - 1) * OWNERS * block_rows, T), F32),) if level > 1 else ()

    g, value, out = pl.pallas_call(
        functools.partial(first_kernel, sn),
        grid=(1,),
        out_shape=(jax.ShapeDtypeStruct((mine, T), F32), row4, by_owner),
        in_specs=[VMEM, d_spec(0)],
        out_specs=(VMEM, VMEM, VMEM),
        compiler_params=PARAMS,
        name="forward_0",
    )(parts, diag_inverse)
    known, solved = [], [value]
    for level in range(1, levels):
        known.append(lax.all_to_all(out, ("core", "x"), 0, 0, tiled=True))
        if level < levels - 1:
            value, out = pl.pallas_call(
                functools.partial(forward_kernel, level, sn),
                grid=(1,),
                out_shape=(row4, by_owner),
                in_specs=[VMEM] * (2 + level) + [c_spec(level), d_spec(level)],
                out_specs=(VMEM, VMEM),
                compiler_params=PARAMS,
                name=f"forward_{level}",
            )(g, look[level - 1], *known, c_near, diag_inverse)
            solved.append(value)
        else:
            out_shape = (row4, by_owner) + rest_of(level)
            change, out, *rest = pl.pallas_call(
                functools.partial(turn_kernel, level, sn),
                grid=(1,),
                out_shape=out_shape,
                in_specs=[VMEM] * (3 + level) + [c_spec(level), d_spec(level)],
                out_specs=(VMEM,) * len(out_shape),
                scratch_shapes=[stage],
                compiler_params=PARAMS,
                name="turn",
            )(g, look[level - 1], scatter[level - 1], *known, c_near, diag_inverse)
    changes = [change]
    for level in reversed(range(levels - 1)):
        arrived = lax.all_to_all(out, ("core", "x"), 0, 0, tiled=True)
        if level > 0:
            out_shape = (row4, by_owner) + rest_of(level)
            change, out, *rest = pl.pallas_call(
                functools.partial(backward_kernel, level, sn),
                grid=(1,),
                out_shape=out_shape,
                in_specs=[VMEM] * 4 + [c_spec(level), d_spec(level)],
                out_specs=(VMEM,) * len(out_shape),
                scratch_shapes=[stage],
                compiler_params=PARAMS,
                name=f"backward_{level}",
            )(solved[level], arrived, rest[0], scatter[level - 1], c_near, diag_inverse)
            changes.append(change)
        else:
            change = pl.pallas_call(
                functools.partial(last_kernel, sn),
                grid=(1,),
                out_shape=jax.ShapeDtypeStruct((Z, mine, T), BF16),
                in_specs=[VMEM] * 5 + [d_spec(0)],
                out_specs=VMEM,
                scratch_shapes=[pltpu.VMEM((sn, T), F32)],
                compiler_params=PARAMS,
                name="backward_0",
            )(solved[0], arrived, *changes, diag_inverse)
    column = lax.all_to_all(change, "z", 0, 0, tiled=True)
    behind, ahead, far = [lax.ppermute(column, "y", shift(Y, -s % Y)) for s in (3, 1, 2)]
    pieces = [column, ahead, far, behind]
    pieces = jnp.concatenate(pieces, axis=0).reshape(Y * Z * mine, T)
    sort = (to[:, None] == place[None, :]).astype(BF16)
    change = jnp.dot(sort, pieces, preferred_element_type=F32)
    new_estimate = estimate + change.reshape(estimate.shape)
    return new_estimate, residual


def solution(mesh):
    grid = jax.sharding.Mesh(mesh.devices.reshape(Z, Y, X, CORE), ("z", "y", "x", "core"))
    every, snode = ("z", "y", "x", "core"), ("x", "core")
    in_specs = (
        P(every, None, None),
        P(every),
        P(every),
        P(every, None, None),
        P(None, snode, None, None),
        P(None, snode, None, None),
        P(None, snode, None, None, None),
        P(None, snode, None),
    )
    out_specs = (P(None, snode, None, None), P(every, None, None))
    return jax.shard_map(local, mesh=grid, in_specs=in_specs, out_specs=out_specs, check_vma=False)
```

```python
import functools

import jax
import jax.numpy as jnp
from jax import lax
from jax.experimental import pallas as pl
from jax.experimental.pallas import tpu as pltpu
from jax.sharding import PartitionSpec as P

CAP = 6
X, CORE, Y, Z = 4, 2, 4, 8
OWNERS = X * CORE
LAST = 2 * CORE + 1
F32 = jnp.float32
BF16 = jnp.bfloat16
NT = (((1,), (1,)), ((), ()))
NN = (((1,), (0,)), ((), ()))
SMEM = pl.BlockSpec(memory_space=pltpu.SMEM)
VMEM = pl.BlockSpec(memory_space=pltpu.VMEM)
ANY = pl.BlockSpec(memory_space=pl.ANY)
PARAMS = pltpu.CompilerParams(vmem_limit_bytes=16 * 1024 * 1024)


def dot(x, y, dims):
    return lax.dot_general(x, y, dims, preferred_element_type=F32)


def ring_away(owner, here):
    step = (lax.shift_right_logical(owner, 1) + X - lax.shift_right_logical(here, 1)) & (X - 1)
    return step * CORE + ((owner ^ here) & 1)


def plan_kernel(sn, here_ref, col_ref, row_ref, plan_ref, note_ref, count_ref, note):
    note[...] = jnp.zeros_like(note)
    for o in range(OWNERS):
        count_ref[o] = 0
    for o in range(OWNERS):
        for i in range(CAP):
            plan_ref[5 + o, i] = 0
            plan_ref[5 + OWNERS + o, i] = -1
    for t in range(col_ref.shape[0]):
        c = col_ref[t]
        level, owner, inner = c // (sn * OWNERS), (c // sn) % OWNERS, c % sn
        rank = count_ref[owner]
        count_ref[owner] = rank + 1
        away = ring_away(owner, here_ref[0])
        plan_ref[0, t] = away
        plan_ref[1, t] = level * sn + inner
        plan_ref[2, t] = row_ref[t]
        plan_ref[3, t] = away
        plan_ref[4, t] = rank
        plan_ref[5 + away, rank] = t
        plan_ref[5 + OWNERS + away, rank] = level * sn + inner
        mark = (level * sn + inner + 1).astype(F32)
        note[away, pl.ds(rank, 1), :] = jnp.full((1, note.shape[2]), mark, F32)
    note_ref[...] = note[...].astype(BF16)


def add_slots(away, first, x_ref, plan_ref, a_ref, res_ref):
    for i in range(CAP):
        t, spot = plan_ref[5 + away, i], plan_ref[5 + OWNERS + away, i]
        at = jnp.where(spot >= 0, first + spot, x_ref.shape[0] - 1)
        res_ref[plan_ref[2, t]] -= dot(x_ref[at], a_ref[t], NT)


def tiles_kernel(aways, core_ref, plan_ref, sum_ref, a_ref, *refs):
    blocks, (res_ref, x_ref, sems) = refs[: len(aways)], refs[len(aways) :]
    mine = x_ref.shape[0] // len(aways)
    x_ref[x_ref.shape[0] - 1] = jnp.zeros(x_ref.shape[1:], BF16)
    sums = pltpu.make_async_copy(sum_ref, res_ref, sems.at[len(aways)])
    sums.start()
    copies = []
    for i, block in enumerate(blocks):
        copies.append(pltpu.make_async_copy(block, x_ref.at[pl.ds(i * mine, mine)], sems.at[i]))
        copies[-1].start()
    sums.wait()
    for i, (at, per_core) in enumerate(aways):
        copies[i].wait()
        add_slots(at + per_core * core_ref[0], i * mine, x_ref, plan_ref, a_ref, res_ref)


def last_tiles_kernel(plan_ref, note_ref, sum_ref, a_ref, block_ref, res_hbm, own_ref, *refs):
    out_refs, (send_ref, x_last, res_ref, low_ref, sems, note_sems) = refs[: OWNERS - 1], refs[OWNERS - 1 :]
    half = x_last.shape[1] // 2
    per = own_ref.shape[0]
    mine = block_ref.shape[0]
    copies = [pltpu.make_async_copy(block_ref, x_last.at[pl.ds(0, mine)], sems.at[0])]
    copies[0].start()
    x_last[mine] = jnp.zeros(x_last.shape[1:], BF16)
    send_ref[...] = jnp.zeros_like(send_ref)
    for o in range(OWNERS):
        copies.append(pltpu.make_async_copy(note_ref.at[o], send_ref.at[(o + 1) * per - 1], note_sems.at[o]))
        copies[-1].start()
    res_ref[...] = sum_ref[...]
    for copy in copies:
        copy.wait()
    add_slots(LAST, 0, x_last, plan_ref, a_ref, res_ref)
    copies = [pltpu.make_async_copy(res_ref, res_hbm, sems.at[0])]
    copies[0].start()
    low_ref[...] = res_ref[...].astype(BF16)
    for t in range(a_ref.shape[0]):
        spot = plan_ref[3, t] * per + 2 * plan_ref[4, t]
        term = dot(low_ref[plan_ref[2, t]], a_ref[t], NN).astype(BF16)
        send_ref[spot] = term[:half]
        send_ref[spot + 1] = term[half:]
    for i, ref in enumerate(out_refs):
        piece = send_ref.at[pl.ds((i + 1) * per, per)]
        copies.append(pltpu.make_async_copy(piece, ref, sems.at[i + 1]))
        copies[-1].start()
    own_ref[...] = send_ref[:per]
    for copy in copies:
        copy.wait()


def in_hbm(x):
    return pltpu.with_memory_space_constraint(x, pltpu.HBM)


def in_vmem(x):
    return pltpu.with_memory_space_constraint(x, pltpu.VMEM)


def near_kernel(n, parts, *refs):
    sems = refs[-1]
    outs = refs[-1 - n : -1]
    copies = []
    for i in range(n):
        size = refs[i].shape[0] // parts[i]
        for k in range(parts[i]):
            piece = pl.ds(k * size, size)
            copies.append(pltpu.make_async_copy(refs[i].at[piece], outs[i].at[piece], sems.at[len(copies)]))
    for copy in copies:
        copy.start()
    for copy in copies:
        copy.wait()


def bring_near(after, *operands):
    n = len(operands)
    parts = tuple(4 if x.shape[0] % 4 == 0 else x.shape[0] for x in operands)
    operands = [in_hbm(x) for x in operands]
    if after is not None:
        operands.append(after)
    out_shape = [jax.ShapeDtypeStruct(x.shape, x.dtype) for x in operands]
    return pl.pallas_call(
        functools.partial(near_kernel, n, parts),
        out_shape=tuple(out_shape[:n]),
        in_specs=[ANY] * len(operands),
        out_specs=(VMEM,) * n,
        scratch_shapes=[pltpu.SemaphoreType.DMA((sum(parts),))],
        compiler_params=PARAMS,
        name="bring_near",
    )(*operands)


def pick_kernel(mine, y_ref, *refs):
    recvs, outs, (data, pick) = refs[:OWNERS], refs[OWNERS:-2], refs[-2:]
    blocks, size, T = recvs[0].shape
    rows = (blocks - 1) * size
    K = rows // CAP
    lane = lax.broadcasted_iota(jnp.int32, (1, 128), 1)
    marks, codes = [], []
    for i, ref in enumerate(recvs):
        data[i * rows : (i + 1) * rows, :] = ref[: blocks - 1].reshape(rows, T)
        note = ref[blocks - 1].astype(F32)
        marks += [note[j : j + 1, :128] for j in range(CAP)]
    per = 128 // K
    column = (lane % K).astype(F32)
    for i in range(0, len(marks), per):
        mark = marks[i]
        for j in range(1, per):
            mark = jnp.where(lane // K == j, marks[i + j], mark)
        codes.append((mark - 1.0) * K + column)
    code = jnp.concatenate(codes, axis=1)
    for step, out in enumerate(outs):
        at = lax.broadcasted_iota(jnp.int32, (Z * mine, 1), 0)
        k = at // mine * Y + (y_ref[0] + step) % Y
        wanted = ((at % mine) * K + k).astype(F32)
        pick[...] = jnp.where(wanted == code, 1.0, 0.0).astype(BF16)
        out[...] = dot(pick[...], data[...], NN).astype(BF16)


def forward_rows(level, sn, g, look_ref, known_refs, c_ref, d_ref):
    if level > 0:
        known = jnp.concatenate([ref[...].astype(F32).reshape(-1, ref.shape[2]) for ref in known_refs], axis=0).astype(BF16)
        found = dot(look_ref[...], known, NN)
    rows = []
    for j in range(sn):
        acc = g[level * sn + j : level * sn + j + 1, :]
        if level > 0:
            n = c_ref.shape[2]
            for i in range(n):
                row = found[j * n + i : j * n + i + 1, :].astype(BF16)
                acc = acc - dot(row, c_ref[0, j, i], NN)
        rows.append(dot(acc.astype(BF16), d_ref[0, j], NN))
    return rows


def backward_rows(level, sn, remaining, c_ref, d_ref, change_ref, stage):
    for j in range(sn):
        change = dot(remaining[j].astype(BF16), d_ref[0, j], NT)
        change_ref[j : j + 1, :] = change
        if level > 0:
            n = c_ref.shape[2]
            low = change.astype(BF16)
            for i in range(n):
                stage[j * n + i : j * n + i + 1, :] = dot(low, c_ref[0, j, i], NT)


def spread(scatter_ref, stage):
    terms = stage[...]
    high = terms.astype(BF16)
    low = (terms - high.astype(F32)).astype(BF16)
    return dot(scatter_ref[...], high, NN) + dot(scatter_ref[...], low, NN)


def store_pend(pend, out_ref, rest_refs):
    n, rows, width = out_ref.shape
    base = pend.shape[0] - n * rows
    out_ref[...] = pend[base:, :].reshape(n, rows, width).astype(out_ref.dtype)
    for ref in rest_refs:
        ref[...] = pend[:base, :]


def spread_rows(rows, own_ref, out_ref):
    for j, row in enumerate(rows):
        own_ref[j : j + 1, :] = row
    filler = jnp.zeros((out_ref.shape[1] - len(rows), out_ref.shape[2]), F32)
    block = jnp.concatenate(rows + [filler], axis=0).astype(out_ref.dtype)
    for o in range(out_ref.shape[0]):
        out_ref[o] = block


def first_kernel(sn, parts_ref, d_ref, g_ref, own_ref, out_ref):
    total = parts_ref[0].astype(F32)
    for i in range(1, parts_ref.shape[0]):
        total = total + parts_ref[i].astype(F32)
    g_ref[...] = total
    spread_rows(forward_rows(0, sn, total, None, [], None, d_ref), own_ref, out_ref)


def forward_kernel(level, sn, g_ref, look_ref, *refs):
    known_refs, (c_ref, d_ref, own_ref, out_ref) = refs[:level], refs[level:]
    rows = forward_rows(level, sn, g_ref[...], look_ref, known_refs, c_ref, d_ref)
    spread_rows(rows, own_ref, out_ref)


def turn_kernel(level, sn, g_ref, look_ref, scatter_ref, *refs):
    known_refs, refs = refs[:level], refs[level:]
    c_ref, d_ref, change_ref, out_ref, rest_ref, stage = refs
    rows = forward_rows(level, sn, g_ref[...], look_ref, known_refs, c_ref, d_ref)
    stage[...] = jnp.zeros_like(stage)
    backward_rows(level, sn, rows, c_ref, d_ref, change_ref, stage)
    store_pend(spread(scatter_ref, stage), out_ref, [rest_ref])


def remaining_rows(sn, solved_ref, recv_ref):
    got = recv_ref[0].astype(F32)
    for i in range(1, recv_ref.shape[0]):
        got = got + recv_ref[i].astype(F32)
    return [solved_ref[j : j + 1, :] - got[j : j + 1, :] for j in range(sn)]


def backward_kernel(level, sn, solved_ref, recv_ref, pend_ref, scatter_ref, c_ref, d_ref, *refs):
    change_ref, out_ref, rest_refs, stage = refs[0], refs[1], refs[2:-1], refs[-1]
    stage[...] = jnp.zeros_like(stage)
    backward_rows(level, sn, remaining_rows(sn, solved_ref, recv_ref), c_ref, d_ref, change_ref, stage)
    store_pend(pend_ref[...] + spread(scatter_ref, stage), out_ref, rest_refs)


def last_kernel(sn, solved_ref, recv_ref, c3_ref, c2_ref, c1_ref, d_ref, out_ref, change):
    backward_rows(0, sn, remaining_rows(sn, solved_ref, recv_ref), None, d_ref, change, None)
    mine = jnp.concatenate([change[...], c1_ref[...], c2_ref[...], c3_ref[...]], axis=0).astype(BF16)
    for i in range(out_ref.shape[0]):
        out_ref[i] = mine


def shift(size, step):
    return [(i, (i + step) % size) for i in range(size)]


def local(a_tiles, tile_row, tile_col, right_side, estimate, diag_inverse, coupling, coupling_source):
    tiles, T = a_tiles.shape[0], a_tiles.shape[1]
    row_tiles, K = right_side.shape[0], right_side.shape[1]
    levels, sn = estimate.shape[0], estimate.shape[1]
    snode = ("x", "core")
    width = sn * OWNERS
    mine = levels * sn
    me = lax.axis_index("x") * CORE + lax.axis_index("core")
    here = me.reshape(1)

    e = estimate.astype(BF16).reshape(mine, K, T)
    other = functools.partial(lax.ppermute, axis_name="core", perm=shift(CORE, 1))

    def along(block):
        perm = []
        for x in range(X):
            perm.append((x * CORE, (x + 1) % X * CORE))
            perm.append((x * CORE + 1, (x - 1) % X * CORE + 1))
        return lax.ppermute(block, snode, perm)

    first = along(e)
    swapped = other(e)
    swapped, here = lax.optimization_barrier((swapped, here))
    second = along(swapped)
    plan, note = pl.pallas_call(
        functools.partial(plan_kernel, sn),
        out_shape=(
            jax.ShapeDtypeStruct((5 + 2 * OWNERS, tiles), jnp.int32),
            pltpu.HBM((OWNERS, 16, T), BF16),
        ),
        in_specs=[SMEM, SMEM, SMEM],
        out_specs=(SMEM, VMEM),
        scratch_shapes=[pltpu.SMEM((OWNERS,), jnp.int32), pltpu.VMEM((OWNERS, 16, T), F32)],
        compiler_params=PARAMS,
        name="plan",
    )(here, in_hbm(tile_col), in_hbm(tile_row))
    (a_near,) = bring_near(swapped, a_tiles)
    first, note, a_near = lax.optimization_barrier((first, note, a_near))
    third = along(first)
    cross_first, cross_second = other(first), other(second)

    slot_rows = CAP * K + 16
    core = lax.axis_index("core").reshape(1)
    def take_off(name, out_kind, aways, so_far, blocks):
        n = len(blocks)
        return pl.pallas_call(
            functools.partial(tiles_kernel, aways),
            out_shape=out_kind((row_tiles, K, T), F32),
            in_specs=[SMEM, SMEM, ANY, VMEM] + [ANY] * n,
            out_specs=VMEM,
            scratch_shapes=[pltpu.VMEM((n * mine + 1, K, T), BF16), pltpu.SemaphoreType.DMA((n + 1,))],
            compiler_params=PARAMS,
            name=name,
        )(core, plan, in_hbm(so_far), a_near, *blocks)

    own, rest = 2 * X - 2, 2
    first_aways = ((0, 0), (1, 0), (own, -4), (own + 1, -4))
    part_sum = take_off("first_tiles", pltpu.HBM, first_aways, right_side, (e, swapped, first, second))
    third, part_sum = lax.optimization_barrier((third, part_sum))
    cross_third = other(third)
    next_aways = ((2 * CORE, 0), (rest, 4), (rest + 1, 4))
    next_blocks = (third, cross_second, cross_first)
    part_sum = take_off("next_tiles", jax.ShapeDtypeStruct, next_aways, part_sum, next_blocks)
    slots = slot_rows // 16
    residual, *send = pl.pallas_call(
        last_tiles_kernel,
        out_shape=(
            jax.ShapeDtypeStruct((row_tiles, K, T), F32),
            jax.ShapeDtypeStruct((slots, 16, T), BF16),
        )
        + (pltpu.HBM((slots, 16, T), BF16),) * (OWNERS - 1),
        in_specs=[SMEM, ANY, VMEM, VMEM, ANY],
        out_specs=(ANY, VMEM) + (ANY,) * (OWNERS - 1),
        scratch_shapes=[
            pltpu.VMEM((OWNERS * slots, 16, T), BF16),
            pltpu.VMEM((mine + 1, K, T), BF16),
            pltpu.VMEM((row_tiles, K, T), F32),
            pltpu.VMEM((row_tiles, K, T), BF16),
            pltpu.SemaphoreType.DMA((OWNERS,)),
            pltpu.SemaphoreType.DMA((OWNERS,)),
        ],
        compiler_params=PARAMS,
        name="last_tiles",
    )(plan, in_hbm(note), part_sum, a_near, cross_third)

    to = jnp.arange(mine * K)
    y = lax.axis_index("y")
    place = jnp.arange(Y * Z * mine)
    column_k = (place // mine) % Z * Y + (place // (mine * Z) + y) % Y
    place = (place % mine) * K + column_k
    first_send, coupling_source = lax.optimization_barrier((send[0], coupling_source))
    source = coupling_source.reshape(levels - 1, -1)
    block_rows = 8
    owner = source // sn % OWNERS
    block = source // width * OWNERS + owner % CORE * X + owner // CORE
    spot_at = block * block_rows + source % sn
    n_terms = source.shape[1]
    pad_terms = -n_terms % 16
    spot_at = jnp.pad(spot_at, ((0, 0), (0, pad_terms)), constant_values=-1)
    look, scatter = [], []
    for level in range(1, levels):
        spots = jnp.arange(level * OWNERS * block_rows)
        look.append((spot_at[level - 1][:, None] == spots[None, :]).astype(BF16))
        scatter.append((spots[:, None] == spot_at[level - 1][None, :]).astype(BF16))
    stage = pltpu.VMEM((n_terms + pad_terms, T), F32)

    recv = [first_send]
    for away in (4, 5, 6, 7, 3, 2, 1):
        step, swap = away // CORE, away % CORE
        perm = []
        for x in range(X):
            for c in range(CORE):
                perm.append((x * CORE + c, (x + step) % X * CORE + (c + swap) % CORE))
        recv.append(lax.ppermute(send[away], snode, perm))
    recv, look, scatter, to, place = lax.optimization_barrier((recv, look, scatter, to, place))
    part = pl.pallas_call(
        functools.partial(pick_kernel, mine),
        out_shape=(jax.ShapeDtypeStruct((Z * mine, T), BF16),) * Y,
        in_specs=[SMEM] + [VMEM] * OWNERS,
        out_specs=(VMEM,) * Y,
        scratch_shapes=[
            pltpu.VMEM((OWNERS * CAP * K, T), BF16),
            pltpu.VMEM((Z * mine, OWNERS * CAP * K), BF16),
        ],
        compiler_params=PARAMS,
        name="pick",
    )(y.reshape(1), *recv)
    total = part[0].astype(F32)
    arrived = [lax.ppermute(part[s], "y", shift(Y, s)) for s in (2, 1, 3)]
    (c_near,) = bring_near(part[0], coupling)
    arrived, c_near = lax.optimization_barrier((arrived, c_near))
    for block in arrived:
        total = total + block.astype(F32)
    parts = lax.all_to_all(total.astype(BF16).reshape(Z, mine, T), "z", 0, 0, tiled=True)

    def d_spec(level):
        return pl.BlockSpec((1, sn, T, T), lambda i: (level, 0, 0, 0))

    def c_spec(level):
        return pl.BlockSpec((1, sn, coupling.shape[2], T, T), lambda i: (level - 1, 0, 0, 0, 0))

    row4 = jax.ShapeDtypeStruct((sn, T), F32)
    by_owner = jax.ShapeDtypeStruct((OWNERS, block_rows, T), BF16)

    def rest_of(level):
        return (jax.ShapeDtypeStruct(((level - 1) * OWNERS * block_rows, T), F32),) if level > 1 else ()

    g, value, out = pl.pallas_call(
        functools.partial(first_kernel, sn),
        grid=(1,),
        out_shape=(jax.ShapeDtypeStruct((mine, T), F32), row4, by_owner),
        in_specs=[VMEM, d_spec(0)],
        out_specs=(VMEM, VMEM, VMEM),
        compiler_params=PARAMS,
        name="forward_0",
    )(parts, diag_inverse)
    known, solved = [], [value]
    for level in range(1, levels):
        known.append(lax.all_to_all(out, ("core", "x"), 0, 0, tiled=True))
        if level < levels - 1:
            value, out = pl.pallas_call(
                functools.partial(forward_kernel, level, sn),
                grid=(1,),
                out_shape=(row4, by_owner),
                in_specs=[VMEM] * (2 + level) + [c_spec(level), d_spec(level)],
                out_specs=(VMEM, VMEM),
                compiler_params=PARAMS,
                name=f"forward_{level}",
            )(g, look[level - 1], *known, c_near, diag_inverse)
            solved.append(value)
        else:
            out_shape = (row4, by_owner) + rest_of(level)
            change, out, *rest = pl.pallas_call(
                functools.partial(turn_kernel, level, sn),
                grid=(1,),
                out_shape=out_shape,
                in_specs=[VMEM] * (3 + level) + [c_spec(level), d_spec(level)],
                out_specs=(VMEM,) * len(out_shape),
                scratch_shapes=[stage],
                compiler_params=PARAMS,
                name="turn",
            )(g, look[level - 1], scatter[level - 1], *known, c_near, diag_inverse)
    changes = [change]
    for level in reversed(range(levels - 1)):
        arrived = lax.all_to_all(out, ("core", "x"), 0, 0, tiled=True)
        if level > 0:
            out_shape = (row4, by_owner) + rest_of(level)
            change, out, *rest = pl.pallas_call(
                functools.partial(backward_kernel, level, sn),
                grid=(1,),
                out_shape=out_shape,
                in_specs=[VMEM] * 4 + [c_spec(level), d_spec(level)],
                out_specs=(VMEM,) * len(out_shape),
                scratch_shapes=[stage],
                compiler_params=PARAMS,
                name=f"backward_{level}",
            )(solved[level], arrived, rest[0], scatter[level - 1], c_near, diag_inverse)
            changes.append(change)
        else:
            change = pl.pallas_call(
                functools.partial(last_kernel, sn),
                grid=(1,),
                out_shape=jax.ShapeDtypeStruct((Z, mine, T), BF16),
                in_specs=[VMEM] * 5 + [d_spec(0)],
                out_specs=VMEM,
                scratch_shapes=[pltpu.VMEM((sn, T), F32)],
                compiler_params=PARAMS,
                name="backward_0",
            )(solved[0], arrived, *changes, diag_inverse)
    column = lax.all_to_all(change, "z", 0, 0, tiled=True)
    behind, ahead, far = [lax.ppermute(column, "y", shift(Y, -s % Y)) for s in (3, 1, 2)]
    pieces = [column, ahead, far, behind]
    pieces = jnp.concatenate(pieces, axis=0).reshape(Y * Z * mine, T)
    sort = (to[:, None] == place[None, :]).astype(BF16)
    change = jnp.dot(sort, pieces, preferred_element_type=F32)
    new_estimate = estimate + change.reshape(estimate.shape)
    return new_estimate, residual


def solution(mesh):
    grid = jax.sharding.Mesh(mesh.devices.reshape(Z, Y, X, CORE), ("z", "y", "x", "core"))
    every, snode = ("z", "y", "x", "core"), ("x", "core")
    in_specs = (
        P(every, None, None),
        P(every),
        P(every),
        P(every, None, None),
        P(None, snode, None, None),
        P(None, snode, None, None),
        P(None, snode, None, None, None),
        P(None, snode, None),
    )
    out_specs = (P(None, snode, None, None), P(every, None, None))
    return jax.shard_map(local, mesh=grid, in_specs=in_specs, out_specs=out_specs, check_vma=False)
```
